128 devices in a mesh: rep: 8 (over y, core), seq: 16 (over z, x).
Axes of the slice: x: 4, y: 4, z: 4, core: 2. Of those that a mesh axis runs over, the one named last changes fastest.
Arguments:
- tokens: bfloat16 [16384, 1536], P(('rep', 'seq')), may hold values from -24 to 24
- norm_gain: float32 [1536], replicated, may hold values from 0.5 to 1.5
- w_main: bfloat16 [1536, 6400], P('seq'), may hold values from -0.15625 to 0.15625
- w_dt: bfloat16 [1536, 48], P('seq'), may hold values from -0.078125 to 0.078125
- conv_weight: float32 [4, 3328], replicated, may hold values from -3 to 3
- conv_bias: float32 [3328], replicated, may hold values from -3 to 3
- dt_bias: float32 [48], replicated, as said below
- a_log: float32 [48], replicated, as said below
- skip_gain: float32 [48], replicated, may hold values from 0.5 to 1.5
- out_gain: float32 [3072], replicated, may hold values from 0.5 to 1.5
- w_out: bfloat16 [3072, 1536], P('seq'), may hold values from -0.109375 to 0.109375
- cotangent: bfloat16 [16384, 1536], P(('rep', 'seq')), may hold values from -6 to 6
Outputs:
- block_out: bfloat16 [16384, 1536], P(('rep', 'seq'))
- grad_tokens: bfloat16 [16384, 1536], P(('rep', 'seq'))
- grad_norm_gain: float32 [1536], replicated
- grad_w_main: float32 [1536, 6400], P('seq')
- grad_w_dt: float32 [1536, 48], P('seq')
- grad_conv_weight: float32 [4, 3328], replicated
- grad_conv_bias: float32 [3328], replicated
- grad_dt_bias: float32 [48], replicated
- grad_a_log: float32 [48], replicated
- grad_skip_gain: float32 [48], replicated
- grad_out_gain: float32 [3072], replicated
- grad_w_out: float32 [3072, 1536], P('seq')
The draws below stay inside these ranges and needn't reach their ends.
Inputs may be any that keep to these rules, and one draw needn't show every extreme that they name: softplus(dt_bias) lies between 0.02 and 0.1 for every head. For every head, exp(a_log) * softplus(dt_bias) lies between 0.3 / 2048 and 0.04.
All inputs are finite; a program needn't handle non-finite values.
Results may differ from the reference program's by a relative error of at most 0.019.
Values may be sent and summed in bfloat16 or wider, within the bound.
No kernel may reach another device: no remote copies, remote signals or barrier semaphores. Data moves between devices by JAX's collectives and lax.ppermute only.
A program may use at most 192 MiB of HBM per device.

```python
import math
import jax
import jax.numpy as jnp
from jax import lax

D = 1536
HEADS = 48
CONV = 4
TOK_DEV = 128
DI = 3072
CONV_CH = 3328
IN_MAIN = 6400
LENGTH = 2048
TOKENS = 16384
N_REP = 8
N_SEQ = 16


def head_rates(key, slow_share):
    key_step = jax.random.fold_in(key, 11)
    key_mask = jax.random.fold_in(key, 12)
    key_slow = jax.random.fold_in(key, 13)
    key_fast = jax.random.fold_in(key, 14)
    step_size = jnp.exp(jax.random.uniform(key_step, (HEADS,), jnp.float32, math.log(0.02), math.log(0.1)))
    slow_mask = jax.random.uniform(key_mask, (HEADS,), jnp.float32) < slow_share
    slow_rate = jnp.exp(jax.random.uniform(key_slow, (HEADS,), jnp.float32, math.log(0.3), math.log(1.5))) / LENGTH
    fast_rate = jnp.exp(jax.random.uniform(key_fast, (HEADS,), jnp.float32, math.log(0.02), math.log(0.04)))
    return (step_size, jnp.where(slow_mask, slow_rate, fast_rate))


def draw_dt_bias(key, part):
    step_size, decay_rate = head_rates(key, 0.5)
    return jnp.log(jnp.expm1(step_size))


def draw_a_log(key, part):
    slow_share = 0.5
    step_size, decay_rate = head_rates(key, slow_share)
    return jnp.log(decay_rate / step_size)


def raised(values, own_key, source, target, shards_of, factor):
    owner, partner = [(jnp.arange(values.shape[position]) // (values.shape[position] // shards_of)).reshape([-1 if axis == position else 1 for axis in range(values.ndim)]) for position in (source, target)]
    chosen = jax.random.permutation(own_key, shards_of)[partner]
    strong = (owner == chosen) | (owner == (partner + shards_of // 2) % shards_of)
    return jnp.where(strong, factor * values, values)


def level_of(own_key, shape, pieces, low, largest):
    loudness, own = 1.0, jax.random.fold_in(own_key, 6)
    for position, parts in pieces:
        draws = jnp.exp(jax.random.uniform(jax.random.fold_in(own, position), (parts,), jnp.float32, low / len(pieces), largest / len(pieces)))
        loudness = loudness * jnp.repeat(draws, shape[position] // parts).reshape([-1 if axis == position else 1 for axis in range(len(shape))])
    return loudness


def noise(key, extent, scale, limit, split=(), kind=jnp.bfloat16):
    drawn = jax.random.normal(key, extent, jnp.float32) * scale
    if len(split) > 0:
        drawn = level_of(key, extent, split, -0.22, 0.18) * drawn
    return jnp.clip(drawn, min=-limit, max=limit).astype(kind)


def gaussian_with(rng, extent, width, most, cuts, heavy, held_as=jnp.bfloat16):
    drawn = width * jax.random.normal(rng, extent, jnp.float32)
    if cuts:
        drawn = drawn * level_of(rng, extent, cuts, -0.22, 0.18)
    return jnp.clip(raised(drawn, jax.random.fold_in(rng, 3), *heavy), -most, most).astype(held_as)


def setup_inputs(seed: int = 0) -> dict:
    seeds = jax.random.split(jax.random.key(seed), 13)
    tokens = gaussian_with(seeds[0], (TOKENS, D), 1.0, 24.0, ((0, 128),), (0, 1, 128, 5.5))
    norm_gain = jnp.clip(1.0 + 0.1 * jax.random.normal(seeds[1], (D,), jnp.float32), 0.5, 1.5)
    w_main = noise(seeds[2], (D, IN_MAIN), D ** -0.5, 0.15625, ((0, 16),))
    w_dt = noise(seeds[3], (D, HEADS), (4 * D) ** -0.5, 0.078125, ((0, 16),))
    conv_weight = noise(seeds[4], (CONV, CONV_CH), CONV ** -0.5, 3.0, (), jnp.float32)
    conv_bias = noise(seeds[5], (CONV_CH,), 0.5, 3.0, (), jnp.float32)
    dt_bias = draw_dt_bias(jax.random.fold_in(seeds[12], 71), 0)
    a_log = draw_a_log(jax.random.fold_in(seeds[12], 71), 0)
    skip_gain = jnp.clip(jax.random.uniform(seeds[8], (HEADS,), jnp.float32, 0.5, 1.5), 0.5, 1.5)
    out_gain = jnp.clip(1.0 + 0.1 * jax.random.normal(seeds[9], (DI,), jnp.float32), 0.5, 1.5)
    w_out = noise(seeds[10], (DI, D), DI ** -0.5, 0.109375, ((0, 16),))
    cotangent = noise(seeds[11], (TOKENS, D), 1.0, 6.0, ((0, 128),))
    return dict(tokens=tokens, norm_gain=norm_gain, w_main=w_main, w_dt=w_dt, conv_weight=conv_weight, conv_bias=conv_bias, dt_bias=dt_bias, a_log=a_log, skip_gain=skip_gain, out_gain=out_gain, w_out=w_out, cotangent=cotangent)


EPS = 1e-05
PRECISE = lax.Precision.HIGHEST

@jax.custom_vjp
def low(v):
    return lax.optimization_barrier(v.astype(jnp.bfloat16)).astype(jnp.float32)

@jax.custom_vjp
def low_back(v):
    return v

def low_keep(v):
    return (low(v), None)

def low_pass(kept, grad):
    return (grad,)

def back_keep(v):
    return (v, None)

def back_low(kept, grad):
    return (low(grad),)
low.defvjp(low_keep, low_pass)
low_back.defvjp(back_keep, back_low)

def pre_norm(seq_tokens, norm_gain):
    inv_root = lax.rsqrt(lax.optimization_barrier(jnp.mean(seq_tokens * seq_tokens, axis=-1, keepdims=True)) + EPS)
    return seq_tokens * inv_root * norm_gain

def gated_norm(mixed_y, gate_branch, out_gain):
    gated = mixed_y * jax.nn.silu(gate_branch)
    inv_root = lax.rsqrt(lax.optimization_barrier(jnp.mean(gated * gated, axis=-1, keepdims=True)) + EPS)
    return gated * inv_root * out_gain

def causal_conv(extended, conv_weight, conv_bias):
    conv_width = conv_weight.shape[0]
    row_count = extended.shape[0] - conv_width + 1
    summed = conv_bias + extended[0:row_count] * conv_weight[0]
    for offset in range(1, conv_width):
        summed = summed + extended[offset:offset + row_count] * conv_weight[offset]
    return jax.nn.silu(summed)

def span_step(carry_state, inputs):
    block_values, block_write, block_read, block_dt, block_decay = inputs
    block_len = block_values.shape[0]
    log_growth = jnp.cumsum(block_decay, axis=0)
    causal = (lax.broadcasted_iota(jnp.int32, (block_len, block_len), 0) >= lax.broadcasted_iota(jnp.int32, (block_len, block_len), 1))[:, :, None]
    spread = log_growth[:, None, :] - log_growth[None, :, :]
    decay_matrix = jnp.where(causal, jnp.exp(jnp.where(causal, spread, 0.0)), 0.0)
    scores = jnp.dot(block_read, block_write.T, precision=PRECISE)
    scaled_values = block_values * block_dt[:, :, None]
    outputs = jnp.einsum('tsh,shp->thp', scores[:, :, None] * decay_matrix, scaled_values, precision=PRECISE)
    outputs = outputs + jnp.exp(log_growth)[:, :, None] * jnp.einsum('tn,hpn->thp', block_read, carry_state, precision=PRECISE)
    last_log = log_growth[-1]
    tail_decay = jnp.exp(last_log[None, :] - log_growth)
    carry_state = jnp.exp(last_log)[:, None, None] * carry_state + jnp.einsum('th,thp,tn->hpn', tail_decay, scaled_values, block_write, precision=PRECISE)
    return (carry_state, outputs)

def state_scan(values, write_rows, read_rows, step_sizes, log_decay):
    row_count, head_count, head_size = values.shape
    block_len = min(256, row_count)
    block_count = row_count // block_len

    def split_blocks(member):
        return member.reshape((block_count, block_len) + member.shape[1:])
    start = jnp.zeros((head_count, head_size, write_rows.shape[1]), values.dtype)
    final_state, outputs = lax.scan(jax.checkpoint(span_step), start, (split_blocks(values), split_blocks(write_rows), split_blocks(read_rows), split_blocks(step_sizes), split_blocks(log_decay)))
    return (outputs.reshape(values.shape), final_state)

def mixer_block(seq_tokens, norm_gain, w_main, w_dt, conv_weight, conv_bias, dt_bias, a_log, skip_gain, out_gain, w_out):
    head_count = a_log.shape[0]
    inner_width = out_gain.shape[0]
    state_size = (conv_weight.shape[1] - inner_width) // 2
    row_count = seq_tokens.shape[0]
    normed = low(pre_norm(seq_tokens, norm_gain))
    projected = low_back(jnp.dot(normed, w_main, precision=PRECISE))
    dt_raw = low_back(jnp.dot(normed, w_dt, precision=PRECISE))
    gate_branch = projected[:, :inner_width]
    conv_input = low(projected[:, inner_width:])
    zeros_rim = jnp.zeros((conv_weight.shape[0] - 1, conv_input.shape[1]), conv_input.dtype)
    activated = causal_conv(jnp.concatenate([zeros_rim, conv_input], axis=0), conv_weight, conv_bias)
    values = low(activated[:, :inner_width]).reshape(row_count, head_count, inner_width // head_count)
    write_rows = low(activated[:, inner_width:inner_width + state_size])
    read_rows = low(activated[:, inner_width + state_size:])
    step_sizes = jax.nn.softplus(dt_raw + dt_bias)
    log_decay = -step_sizes * jnp.exp(a_log)
    scanned, final_state = state_scan(values, write_rows, read_rows, step_sizes, log_decay)
    mixed_y = scanned + skip_gain[None, :, None] * values
    normed_y = low(gated_norm(mixed_y.reshape(row_count, inner_width), gate_branch, out_gain))
    return seq_tokens + jnp.dot(normed_y, w_out, precision=PRECISE)

def reference(tokens, norm_gain, w_main, w_dt, conv_weight, conv_bias, dt_bias, a_log, skip_gain, out_gain, w_out, cotangent):
    params = tuple((member.astype(jnp.float32) for member in (norm_gain, w_main, w_dt, conv_weight, conv_bias, dt_bias, a_log, skip_gain, out_gain, w_out)))
    seq_length = TOK_DEV * N_SEQ
    sequences = tokens.astype(jnp.float32).reshape(N_REP, seq_length, D)
    seq_cots = cotangent.astype(jnp.float32).reshape(N_REP, seq_length, D)

    def one_sequence(grad_totals, seq_pair):
        seq_tokens, seq_cot = seq_pair
        result, pullback = jax.vjp(mixer_block, seq_tokens, *params)
        grads = pullback(seq_cot)
        return (tuple((total + grad for total, grad in zip(grad_totals, grads[1:]))), (result, grads[0]))
    start = tuple((jnp.zeros_like(member) for member in params))
    grad_totals, (results, grad_inputs) = lax.scan(one_sequence, start, (sequences, seq_cots))
    block_out = results.reshape(TOKENS, D).astype(jnp.bfloat16)
    grad_tokens = grad_inputs.reshape(TOKENS, D).astype(jnp.bfloat16)
    return (block_out, grad_tokens, grad_totals[0], grad_totals[1], grad_totals[2], grad_totals[3], grad_totals[4], grad_totals[5], grad_totals[6], grad_totals[7], grad_totals[8], grad_totals[9])
```

```python
import functools

import jax
import jax.numpy as jnp
from jax import lax
from jax.experimental import pallas as pl
from jax.experimental.pallas import tpu as pltpu
from jax.sharding import Mesh, PartitionSpec as P

EPS = 1e-05
BF = jnp.bfloat16
F32 = jnp.float32
HIGH = lax.Precision.HIGHEST
NX = 4
NZ = 4
D = 1536
HL = 12
PW = 64
HW = 768
NS = 128
L = 128
NC = 4
T = 512
RIM = 16
TR = T + RIM
CC = 1024
CA = 1152
DI = 3072
VMEM = 58 * 1024 * 1024


def call(body, outs, ins, scratch=(), flops=0, smem=1):
    specs = [pl.BlockSpec(memory_space=pltpu.SMEM)] * smem
    specs += [pl.BlockSpec(memory_space=pltpu.VMEM)] * (len(ins) - smem)
    return pl.pallas_call(
        body,
        out_shape=[jax.ShapeDtypeStruct(shape, kind) for shape, kind in outs],
        in_specs=specs,
        out_specs=[pl.BlockSpec(memory_space=pltpu.VMEM)] * len(outs),
        scratch_shapes=[pltpu.VMEM(shape, kind) for shape, kind in scratch],
        compiler_params=pltpu.CompilerParams(vmem_limit_bytes=VMEM),
        cost_estimate=pl.CostEstimate(flops=flops, bytes_accessed=4 << 20, transcendentals=0),
        name=body.__name__,
    )(*ins)


def mm(a, b):
    return lax.dot_general(a, b, (((1,), (0,)), ((), ())), preferred_element_type=F32)


def mm_nt(a, b):
    return lax.dot_general(a, b, (((1,), (1,)), ((), ())), preferred_element_type=F32)


def mm_tn(a, b):
    return lax.dot_general(a, b, (((0,), (0,)), ((), ())), preferred_element_type=F32)


def mm_high(a, b):
    return lax.dot_general(
        a, b, (((1,), (0,)), ((), ())), precision=HIGH, preferred_element_type=F32
    )


def iota2(shape, dim):
    return lax.broadcasted_iota(jnp.int32, shape, dim)


def spread_matrix(kind):
    return (
        lax.shift_right_logical(iota2((128, HW), 1), 6) == iota2((128, HW), 0)
    ).astype(kind)


def spread(v, e):
    hi = v.astype(BF)
    rest = v - hi.astype(F32)
    mid = rest.astype(BF)
    lo = (rest - mid.astype(F32)).astype(BF)
    return mm(hi, e) + mm(mid, e) + mm(lo, e)


def head_sums(v, e):
    hi = v.astype(BF)
    lo = (v - hi.astype(F32)).astype(BF)
    return mm_nt(hi, e) + mm_nt(lo, e)


def sigmoid(v):
    return 1.0 / (1.0 + jnp.exp(-v))


def chunk(ref, c, lanes=slice(None), base=0):
    return ref[pl.ds(pl.multiple_of(base + c * L, 16), L), lanes]


def pack_weights(idx, wm, wd, *rest):
    outs_a, outs_g, sa, sg = rest[:4], rest[4:8], rest[8], rest[9]
    x, core = idx[0], idx[2]
    rows = pl.ds(pl.multiple_of(core * 48, 16), 48)
    for xp in range(NX):
        for zp in range(NZ):
            at = 768 * zp + 192 * xp
            sg[xp, :, 192 * zp : 192 * zp + 192] = wm[rows, at : at + 192]
            sa[xp, :, 192 * zp : 192 * zp + 192] = wm[rows, DI + at : DI + at + 192]
        sa[xp, :, HW:CC] = wm[rows, 2 * DI : 2 * DI + 256]
        sa[xp, :, CC:CA] = wd[xp, rows]
    for k in range(NX):
        to = lax.rem(x + k, NX)
        outs_a[k][...] = sa[to]
        outs_g[k][...] = sg[to]


def norm_rows(idx, t0, t1, t2, t3, gain, normed, tail):
    x = idx[0]
    for k, piece in enumerate((t0, t1, t2, t3)):
        v = piece[...].astype(F32)
        root = lax.rsqrt(jnp.mean(v * v, axis=1, keepdims=True) + EPS)
        at = pl.multiple_of(lax.rem(x + NX - k, NX) * 128, 128)
        normed[pl.ds(at, 128), :] = (v * root * gain[...]).astype(BF)
    tail[...] = normed[T - RIM : T, :]


def turn(idx, normed, rim, nfull, mine, other, scr):
    core = idx[2]
    nfull[0:T, :] = normed[...]
    nfull[T:TR, :] = rim[...]
    blank = jnp.zeros((128 - RIM, 128), F32)
    for j in range(D // 128):
        lanes = slice(128 * j, 128 * j + 128)
        scr[lanes, 0:T] = normed[:, lanes].astype(F32).T.astype(BF)
        edge = jnp.concatenate([rim[:, lanes].astype(F32), blank], axis=0)
        scr[lanes, T : T + 128] = edge.T.astype(BF)
    for block in range(16):
        for out, half in ((mine, core), (other, 1 - core)):
            at = pl.multiple_of(96 * block + 48 * half, 16)
            out[48 * block : 48 * block + 48, :] = scr[pl.ds(at, 48), 0:TR]


def project(idx, nfull, mine, other, par, hp, wa, ci, act, dsl, sm, sc, fp, scr):
    x, z, core = idx[0], idx[1], idx[2]
    for step in range(NZ):
        for k in range(NX):
            block = 4 * lax.rem(z + NZ - step, NZ) + lax.rem(x + NX - k, NX)
            for ref, half in ((mine, core), (other, 1 - core)):
                at = pl.multiple_of(96 * block + 48 * half, 16)
                row = 192 * step + 48 * k
                wa[pl.ds(at, 48), :] = ref[row : row + 48, :]

    raw = mm(nfull[0:T, :], wa[:, CC:CA]) + hp[0:1, :]
    held = iota2((T, 128), 1) < HL
    dt = jnp.where(held, jnp.maximum(raw, 0.0) + jnp.log1p(jnp.exp(-jnp.abs(raw))), 0.0)
    sm[0] = dt
    sm[2] = sigmoid(raw)
    decay = -dt * jnp.exp(hp[1:2, :])
    tri = (iota2((L, L), 0) >= iota2((L, L), 1)).astype(F32)
    for c in range(NC):
        sm[1, c * L : c * L + L, :] = mm_high(tri, decay[c * L : c * L + L])

    @pl.loop(0, 4)
    def _(j):
        lanes = pl.ds(pl.multiple_of(j * 256, 256), 256)
        low = mm(nfull[...], wa[:, lanes]).astype(BF)
        ci[:, lanes] = low
        scr[RIM:TR, :] = low[0:T].astype(F32)
        scr[0:RIM, :] = low[T:TR].astype(F32)
        pre = par[4:5, lanes] + par[0:1, lanes] * scr[13 : 13 + T, :]
        for k in range(1, 4):
            pre = pre + par[k : k + 1, lanes] * scr[13 + k : 13 + k + T, :]
        s = sigmoid(pre)
        act[:, lanes] = (pre * s).astype(BF)
        dsl[:, lanes] = (s * (1.0 + pre * (1.0 - s))).astype(BF)

    e = spread_matrix(BF)
    final = jnp.zeros((NS, HW), F32)
    total = jnp.zeros((8, HW), F32)
    for c in range(NC):
        rows = slice(c * L, c * L + L)
        s = sm[1, rows, :]
        last = s[L - 1 : L, :]
        w = spread(jnp.exp(last - s) * sm[0, rows, :], e)
        vw = (act[rows, 0:HW].astype(F32) * w).astype(BF)
        part = mm_tn(act[rows, HW : HW + NS], vw)
        sc[c] = part
        last_e = spread(jnp.broadcast_to(last, (8, 128)), e)
        final = jnp.exp(last_e[0:1]) * final + part
        total = total + last_e
    pack_state(fp, final, total)


def pack_state(fp, state, total):
    hi = total.astype(BF)
    lo = (total - hi.astype(F32)).astype(BF)
    fp[0:NS, :] = state.astype(BF)
    fp[NS : NS + 16, :] = jnp.concatenate(
        [hi.astype(F32), lo.astype(F32)], axis=0
    ).astype(BF)


def incoming(p1, p2, p3):
    t1 = p1[NS : NS + 16, :].astype(F32)
    t2 = p2[NS : NS + 16, :].astype(F32)
    t1 = t1[0:1] + t1[8:9]
    t2 = t2[0:1] + t2[8:9]
    return (
        p1[0:NS, :].astype(F32)
        + jnp.exp(t1) * p2[0:NS, :].astype(F32)
        + jnp.exp(t1 + t2) * p3[0:NS, :].astype(F32)
    )


def gates(idx, nfull, mine, other, cot, gate, gny, wg, wo):
    x, z, core = idx[0], idx[1], idx[2]
    for step in range(NZ):
        to = lax.rem(z + NZ - step, NZ)
        for ref, half in ((mine, core), (other, 1 - core)):
            at = pl.multiple_of(192 * to + 96 * half, 16)
            wo[pl.ds(at, 96), :] = ref[192 * step : 192 * step + 96, :]
            for k in range(NX):
                block = 4 * to + lax.rem(x + NX - k, NX)
                at = pl.multiple_of(96 * block + 48 * half, 16)
                row = 192 * step + 96 + 48 * (k // 2)
                lane = HW * (k % 2)
                wg[pl.ds(at, 48), :] = ref[row : row + 48, lane : lane + HW]

    @pl.loop(0, 3)
    def _(j):
        lanes = pl.ds(pl.multiple_of(j * 256, 256), 256)
        gate[:, lanes] = mm(nfull[0:T, :], wg[:, lanes])
        gny[:, lanes] = mm_nt(cot[...], wo[lanes, :])


def within(idx, act, sm, hp, yi):
    e = spread_matrix(BF)
    skip = spread(jnp.broadcast_to(hp[2:3, :], (8, 128)), e)[0:1]
    left = iota2((L, 128), 1) < PW
    causal = iota2((L, L), 0) >= iota2((L, L), 1)

    @pl.loop(0, NC)
    def _(c):
        rows = pl.ds(pl.multiple_of(c * L, L), L)
        s = sm[1, rows, :]
        s_t = s.T
        v = act[rows, 0:HW].astype(F32)
        u = v * spread(sm[0, rows, :], e)
        scores = mm_nt(act[rows, HW + NS : CC], act[rows, HW : HW + NS])
        for j in range(HL // 2):
            parts = []
            for h in (2 * j, 2 * j + 1):
                gap = s[:, h : h + 1] - s_t[h : h + 1, :]
                parts.append((scores * jnp.exp(jnp.where(causal, gap, -1e30))).astype(BF))
            pair = u[:, 128 * j : 128 * j + 128]
            both = jnp.concatenate(
                [jnp.where(left, pair, 0.0), jnp.where(left, 0.0, pair)], axis=0
            ).astype(BF)
            yi[rows, 128 * j : 128 * j + 128] = mm(jnp.concatenate(parts, axis=1), both)
        yi[rows, :] += skip * v


def mix(idx, yi, act, sm, sc, p1, p2, p3, gate, gny, par, mixed, hin, sums):
    e = spread_matrix(BF)
    ones = jnp.ones((8, HW), BF)

    def rowsum(v):
        hi = v.astype(BF)
        lo = (v - hi.astype(F32)).astype(BF)
        return mm_nt(ones, hi) + mm_nt(ones, lo)

    state = incoming(p1, p2, p3)
    for c in range(NC):
        rows = slice(c * L, c * L + L)
        s = sm[1, rows, :]
        low = state.astype(BF)
        hin[c] = low
        y = yi[rows, :] + spread(jnp.exp(s), e) * mm(act[rows, HW + NS : CC], low)
        mixed[rows, :] = y
        z = gate[rows, :]
        g = y * (z * sigmoid(z))
        sq = rowsum(g * g)
        sg = rowsum(g * (gny[rows, :] * par[5:6, 0:HW]))
        sums[:, rows] = jnp.where(iota2((8, L), 0) == 0, sq, sg)
        last = spread(jnp.broadcast_to(s[L - 1 : L, :], (8, 128)), e)[0:1]
        state = jnp.exp(last) * state + sc[c]


def gated(
    idx, mixed, gate, gny, act, sm, s0, s1, s2, s3, wo, par,
    ny, gmix, ggate, bo, rp, small,
):
    e = spread_matrix(BF)
    sums = s0[...] + s1[...] + s2[...] + s3[...]
    gain = par[5:6, 0:HW]
    pick0 = (iota2((8, 128), 0) == 0).astype(F32)
    pick1 = (iota2((8, 128), 0) == 1).astype(F32)
    grad_gain = jnp.zeros((1, HW), F32)
    grad_skip = jnp.zeros((1, HW), F32)
    pulls = []
    totals = []
    for c in range(NC):
        rows = slice(c * L, c * L + L)
        here = sums[:, rows]
        sq = lax.dot_general(
            here, pick0, (((0,), (0,)), ((), ())), precision=HIGH, preferred_element_type=F32
        )
        sg = lax.dot_general(
            here, pick1, (((0,), (0,)), ((), ())), precision=HIGH, preferred_element_type=F32
        )
        r1 = lax.rsqrt(sq * (1.0 / DI) + EPS)
        pull = r1 * r1 * (sg * (1.0 / DI))
        r1 = jnp.concatenate([r1] * 6, axis=1)
        pull = jnp.concatenate([pull] * 6, axis=1)
        y = mixed[rows, :]
        z = gate[rows, :]
        sz = sigmoid(z)
        sil = z * sz
        g = y * sil
        gn = gny[rows, :]
        ghat = g * r1
        ny[rows, :] = (ghat * gain).astype(BF)
        grad_gain = grad_gain + jnp.sum(gn * ghat, axis=0, keepdims=True)
        gg = r1 * (gn * gain - g * pull)
        gm = gg * sil
        gmix[rows, :] = gm.astype(BF)
        ggate[rows, :] = (gg * y * (sz * (1.0 + z * (1.0 - sz)))).astype(BF)
        grad_skip = grad_skip + jnp.sum(gm * act[rows, 0:HW].astype(F32), axis=0, keepdims=True)
        s = sm[1, rows, :]
        pulls.append(mm_tn(act[rows, HW + NS : CC], (gm * spread(jnp.exp(s), e)).astype(BF)))
        totals.append(spread(jnp.broadcast_to(s[L - 1 : L, :], (8, 128)), e))
    state = jnp.zeros((NS, HW), F32)
    total = jnp.zeros((8, HW), F32)
    for c in reversed(range(NC)):
        state = jnp.exp(totals[c][0:1]) * state + pulls[c]
        total = total + totals[c]
    pack_state(rp, state, total)
    small[0:1, :] = grad_gain
    small[1:2, :] = grad_skip

    @pl.loop(0, 6)
    def _(j):
        lanes = pl.ds(pl.multiple_of(j * 256, 256), 256)
        bo[:, lanes] = mm(ny[...], wo[:, lanes]).astype(BF)


def within_back(idx, act, gmix, sm, gu, gbc, dsi, rw):
    left = iota2((L, 128), 1) < PW
    lane = iota2((L, 128), 1)
    causal = iota2((L, L), 1) >= iota2((L, L), 0)
    rw[...] = jnp.zeros_like(rw)

    @pl.loop(0, NC)
    def _(c):
        rows = pl.ds(pl.multiple_of(c * L, L), L)
        s = sm[1, rows, :]
        s_t = s.T
        dt = sm[0, rows, :]
        b = act[rows, HW : HW + NS]
        r = act[rows, HW + NS : CC]
        scores = mm_nt(b, r)
        grad_scores = jnp.zeros((L, L), F32)
        cols = jnp.zeros((L, 128), F32)
        for j in range(HL // 2):
            v = act[rows, 128 * j : 128 * j + 128].astype(F32)
            g = gmix[rows, 128 * j : 128 * j + 128]
            gf = g.astype(F32)
            parts = []
            for i in range(2):
                h = 2 * j + i
                gap = s_t[h : h + 1, :] - s[:, h : h + 1]
                q = jnp.exp(jnp.where(causal, gap, -1e30))
                own = jnp.where(left, v, 0.0) if i == 0 else jnp.where(left, 0.0, v)
                vg = mm_nt(own.astype(BF), g) * (q * dt[:, h : h + 1])
                grad_scores = grad_scores + vg
                w = scores * vg
                rw[h : h + 1, :] = jnp.sum(w, axis=0, keepdims=True)
                cols = jnp.where(lane == h, jnp.sum(w, axis=1, keepdims=True), cols)
                parts.append((scores * q).astype(BF))
            both = jnp.concatenate(
                [jnp.where(left, gf, 0.0), jnp.where(left, 0.0, gf)], axis=0
            ).astype(BF)
            gu[rows, 128 * j : 128 * j + 128] = mm(jnp.concatenate(parts, axis=1), both)
        dsi[rows, :] = rw[...].T - cols
        low = grad_scores.astype(BF)
        gbc[rows, 0:NS] = mm(low, r)
        gbc[rows, NS : 2 * NS] = mm_tn(low, b)


def across_back(
    idx, act, gmix, sm, gu, gbc, dsi, hin, p1, p2, p3, dsl, ci, par, hp,
    gpa, small, hsm, gps, cis,
):
    e = spread_matrix(BF)
    skip = spread(jnp.broadcast_to(hp[2:3, :], (8, 128)), e)[0:1]
    rate = jnp.exp(hp[1:2, :])
    upper = (iota2((L, L), 1) >= iota2((L, L), 0)).astype(F32)
    below = (iota2((L, L), 0) > iota2((L, L), 1)).astype(F32)
    gps[0:RIM, :] = jnp.zeros((RIM, CC), F32)
    gps[RIM + T : RIM + T + 16, :] = jnp.zeros((16, CC), F32)
    state = incoming(p1, p2, p3)
    grad_log = jnp.zeros((1, 128), F32)
    grad_bias = jnp.zeros((1, 128), F32)
    gpa[T:TR, CC:CA] = jnp.zeros((RIM, 128), BF)
    for c in reversed(range(NC)):
        rows = slice(c * L, c * L + L)
        b = act[rows, HW : HW + NS]
        r = act[rows, HW + NS : CC]
        low = state.astype(BF)
        s = sm[1, rows, :]
        dt = sm[0, rows, :]
        last = s[L - 1 : L, :]
        tail_e = spread(jnp.exp(last - s), e)
        dt_e = spread(dt, e)
        grow_e = spread(jnp.exp(s), e)
        last_e = jnp.exp(spread(jnp.broadcast_to(last, (8, 128)), e)[0:1])
        v = act[rows, 0:HW].astype(F32)
        g = gmix[rows, :].astype(F32)
        carried = tail_e * mm(b, low)
        grad_u = gu[rows, :] + carried
        u = v * dt_e
        grad_v = dt_e * grad_u + skip * g
        grad_b = gbc[rows, 0:NS] + mm_nt((u * tail_e).astype(BF), low)
        gs = (g * grow_e).astype(BF)
        h = hin[c]
        grad_c = gbc[rows, NS : 2 * NS] + mm_nt(gs, h)
        inter = head_sums(g * (grow_e * mm(r, h)), e)
        kept = head_sums(u * carried, e)
        grad_step = head_sums(v * grad_u, e)
        cross = jnp.sum(h.astype(F32) * state, axis=0, keepdims=True) * last_e
        cross = head_sums(jnp.broadcast_to(cross, (8, HW)), e)[0:1]
        grad_a = mm_high(upper, dsi[rows, :] + inter) + mm_high(below, kept) + cross
        grad_raw = (grad_step - rate * grad_a) * sm[2, rows, :]
        grad_log = grad_log + jnp.sum(grad_a * dt, axis=0, keepdims=True)
        grad_bias = grad_bias + jnp.sum(grad_raw, axis=0, keepdims=True)
        held = iota2((L, 128), 1) < HL
        gpa[rows, CC:CA] = jnp.where(held, grad_raw, 0.0).astype(BF)
        d = dsl[rows, :].astype(F32)
        to = slice(RIM + c * L, RIM + c * L + L)
        gps[to, 0:HW] = grad_v * d[:, 0:HW]
        gps[to, HW : HW + NS] = grad_b * d[:, HW : HW + NS]
        gps[to, HW + NS : CC] = grad_c * d[:, HW + NS : CC]
        state = last_e * state + mm_tn(r, gs)
    hsm[0:1, :] = grad_bias
    hsm[1:2, :] = -rate * grad_log

    @pl.loop(0, 4)
    def _(j):
        lanes = pl.ds(pl.multiple_of(j * 256, 256), 256)
        cis[RIM:TR, :] = ci[0:T, lanes].astype(F32)
        cis[0:RIM, :] = ci[T:TR, lanes].astype(F32)
        gp = gps[RIM : RIM + T, lanes]
        small[4:5, lanes] = jnp.sum(gp, axis=0, keepdims=True)
        out = par[3:4, lanes] * gps[0:TR, lanes]
        for k in range(4):
            small[k : k + 1, lanes] = jnp.sum(
                gp * cis[13 + k : 13 + k + T, :], axis=0, keepdims=True
            )
            if k < 3:
                out = out + par[k : k + 1, lanes] * gps[3 - k : 3 - k + TR, lanes]
        low = out.astype(BF)
        gpa[0:T, lanes] = low[RIM:TR]
        gpa[T:TR, lanes] = low[0:RIM]


def rim_back(idx, gpa, wa, out):
    out[...] = mm_nt(gpa[T:TR, :], wa[...]).astype(BF)


def normed_back(idx, gpa, ggate, wa, wg, nfull, rim, gain, o0, o1, o2, o3, gsum, acc):
    x = idx[0]

    @pl.loop(0, 6)
    def _(j):
        lanes = pl.ds(pl.multiple_of(j * 256, 256), 256)
        acc[:, lanes] = mm_nt(gpa[0:T, :], wa[lanes, :]) + mm_nt(ggate[...], wg[lanes, :])

    acc[T - RIM : T, :] += rim[...].astype(F32)
    gsum[...] = jnp.broadcast_to(
        jnp.sum(acc[...] * nfull[0:T, :].astype(F32), axis=0, keepdims=True) / gain[...],
        (8, D),
    )
    for k, out in enumerate((o0, o1, o2, o3)):
        at = pl.multiple_of(lax.rem(x + k, NX) * 128, 128)
        out[...] = acc[pl.ds(at, 128), :].astype(out.dtype)


def finish_out(idx, tokens, summed, out):
    out[...] = (tokens[...].astype(F32) + summed[...].astype(F32)).astype(BF)


def finish_back(idx, tokens, cot, g0, g1, g2, g3, gain, out):
    v = tokens[...].astype(F32)
    root = lax.rsqrt(jnp.mean(v * v, axis=1, keepdims=True) + EPS)
    q = (
        g0[...] + g1[...].astype(F32) + g2[...].astype(F32) + g3[...].astype(F32)
    ) * gain[...]
    pull = jnp.mean(q * v, axis=1, keepdims=True)
    out[...] = (cot[...].astype(F32) + root * (q - v * (root * root) * pull)).astype(BF)


def grad_early(idx, ny, cot, ggate, turned, half, out, nyt, rows):
    which = lax.rem(idx[2] + half, 2)
    for j in range(HW // 128):
        lanes = slice(128 * j, 128 * j + 128)
        nyt[lanes, :] = ny[:, lanes].astype(F32).T.astype(BF)
    for z in range(NZ):
        at = pl.multiple_of(192 * z + 96 * which, 16)
        rows[96 * z : 96 * z + 96, :] = nyt[pl.ds(at, 96), :]
    @pl.loop(0, 6)
    def _(j):
        lanes = pl.ds(pl.multiple_of(j * 256, 256), 256)
        part = mm(rows[...], cot[:, lanes])
        for z in range(NZ):
            out[192 * z : 192 * z + 96, lanes] = part[96 * z : 96 * z + 96].astype(BF)
    for z in range(NZ):
        part = mm(turned[192 * z : 192 * z + 192, 0:T], ggate[...]).astype(BF)
        for xp in range(NX):
            at = 192 * z + 96 + 48 * (xp // 2)
            lane = HW * (xp % 2)
            out[at : at + 48, lane : lane + HW] = part[48 * xp : 48 * xp + 48]


def early_other(idx, ny, cot, ggate, turned, out, nyt, rows):
    grad_early(idx, ny, cot, ggate, turned, 1, out, nyt, rows)


def early_mine(idx, ny, cot, ggate, turned, got, out, nyt, rows):
    grad_early(idx, ny, cot, ggate, turned, 0, out, nyt, rows)
    out[...] = (out[...].astype(F32) + got[...].astype(F32)).astype(BF)


def late_other(idx, gpa, turned, out):
    for z in range(NZ):
        rows = slice(192 * z, 192 * z + 192)
        out[rows, :] = mm(turned[rows, :], gpa[...]).astype(BF)


def late_mine(idx, gpa, turned, got, out):
    for z in range(NZ):
        rows = slice(192 * z, 192 * z + 192)
        out[rows, :] = (mm(turned[rows, :], gpa[...]) + got[rows, :].astype(F32)).astype(BF)


def small_pack(idx, gsum, conv, gains, heads, out):
    e = spread_matrix(BF)
    for j in range(3):
        out[j : j + 1, :] = gsum[0:1, 512 * j : 512 * j + 512]
    for k in range(5):
        for j in range(2):
            out[3 + 2 * k + j : 4 + 2 * k + j, :] = conv[k : k + 1, 512 * j : 512 * j + 512]
    out[13:14, :] = gains[0:1, 0:512]
    out[14:15, 0:256] = gains[0:1, 512:768]
    skip = head_sums(jnp.broadcast_to(gains[1:2, :], (8, HW)), e)[0:1]
    out[14:15, 256:384] = skip
    out[14:15, 384:512] = heads[0:1, :]
    out[15:16, 0:128] = heads[1:2, :]
    out[15:16, 128:512] = jnp.zeros((1, 384), F32)


def small_add(idx, a, b, out):
    out[...] = a[...] + b[...]


def halves(v):
    hi = v.astype(BF).astype(F32)
    return jnp.concatenate([hi, v - hi], axis=0).astype(BF)


def joined(v):
    v = v.astype(F32)
    return v[0:16] + v[16:32]


def split_y(idx, late, early, a, b, c, d, o0, o1, o2, o3, scr):
    y = idx[3]
    small = halves(a[...] + b[...] + c[...] + d[...])
    for q in range(4):
        at = 192 * q
        scr[q, 0:192, 0:192] = late[:, at : at + 192]
        scr[q, 0:192, 192:256] = late[:, HW + 64 * q : HW + 64 * q + 64]
        scr[q, 0:192, 448:512] = late[:, CC : CC + 64]
        for xp in range(NX):
            row = 96 + 48 * (xp // 2)
            lane = HW * (xp % 2) + at
            scr[q, 48 * xp : 48 * xp + 48, 256:448] = early[row : row + 48, lane : lane + 192]
        scr[q, 192:288, 0:384] = early[0:96, 384 * q : 384 * q + 384]
        scr[q, 192:288, 384:512] = jnp.zeros((96, 128), BF)
        scr[q, 288:320, :] = small
    for k, out in enumerate((o0, o1, o2, o3)):
        out[...] = scr[lax.rem(y + k, 4)]


def sum_y(idx, a, b, c, d, o0, o1, o2, o3, wo, scr):
    x = idx[0]
    total = a[0:288].astype(F32) + b[0:288].astype(F32)
    total = (total + (c[0:288].astype(F32) + d[0:288].astype(F32))).astype(BF)
    scr[...] = total[0:192]
    wo[...] = total[192:288]
    small = halves(
        joined(a[288:320]) + joined(b[288:320]) + (joined(c[288:320]) + joined(d[288:320]))
    )
    for k, out in enumerate((o0, o1, o2, o3)):
        at = pl.multiple_of(lax.rem(x + k, NX) * 48, 16)
        out[0:48, :] = scr[pl.ds(at, 48), :]
        out[48:80, :] = small


def arrange_x(idx, a, b, c, d, wo, out, gain, conv, ogain, heads, scr):
    x = idx[0]
    shared = jnp.zeros((48, 64), F32)
    for k, ref in enumerate((a, b, c, d)):
        source = lax.rem(x + NX - k, NX)
        out[pl.ds(pl.multiple_of(source * 48, 16), 48), :] = ref[0:48, :]
        shared = shared + ref[0:48, 192:256].astype(F32)
        scr[source] = joined(ref[48:80, :])
    out[0:48, 192:256] = shared.astype(BF)
    out[192:288, :] = wo[...]
    both = scr[0] + scr[1] + (scr[2] + scr[3])
    for j in range(3):
        gain[0:1, 512 * j : 512 * j + 512] = both[j : j + 1, :]
    for k in range(5):
        conv[k : k + 1, DI : DI + 256] = both[4 + 2 * k : 5 + 2 * k, 256:512]
    heads[...] = jnp.zeros_like(heads)
    for xp in range(NX):
        own = scr[xp]
        for q in range(4):
            lane = 768 * q + 192 * xp
            for k in range(5):
                for at, size in pieces(192 * q, 192):
                    conv[k : k + 1, lane + at - 192 * q : lane + at - 192 * q + size] = own[
                        3 + 2 * k + at // 512 : 4 + 2 * k + at // 512, at % 512 : at % 512 + size
                    ]
            for at, size in pieces(192 * q, 192):
                ogain[0:1, lane + at - 192 * q : lane + at - 192 * q + size] = own[
                    13 + at // 512 : 14 + at // 512, at % 512 : at % 512 + size
                ]
            to = slice(12 * q + 3 * xp, 12 * q + 3 * xp + 3)
            heads[0:1, to] = own[14:15, 384 + 3 * q : 387 + 3 * q]
            heads[1:2, to] = own[15:16, 3 * q : 3 * q + 3]
            heads[2:3, to] = own[14:15, 256 + 3 * q : 259 + 3 * q]


def pieces(at, size):
    end = at + size
    while at < end:
        step = min(end, (at // 512 + 1) * 512) - at
        yield at, step
        at += step


def finish_weights(idx, a, b, c, d, other, gmain, gdt, gout, scr):
    y, core = idx[3], idx[2]
    for half in range(2):
        place = lax.rem(core + half, 2)
        for k, ref in enumerate((a, b, c, d)):
            source = lax.rem(y + 4 - k, 4)
            scr[source] = ref[...] if half == 0 else other[288 * k : 288 * k + 288, :]
        rows = pl.ds(pl.multiple_of(48 * place, 16), 48)
        long = pl.ds(pl.multiple_of(96 * place, 16), 96)
        for q in range(4):
            gout[long, 384 * q : 384 * q + 384] = scr[q, 192:288, 0:384].astype(F32)
            gmain[rows, 6144 + 64 * q : 6144 + 64 * q + 64] = scr[q, 0:48, 192:256].astype(F32)
            for xp in range(NX):
                lane = 768 * q + 192 * xp
                part = scr[q, 48 * xp : 48 * xp + 48, :].astype(F32)
                gmain[rows, lane : lane + 192] = part[:, 256:448]
                gmain[rows, DI + lane : DI + lane + 192] = part[:, 0:192]
        for xp in range(NX):
            part = scr[0, 48 * xp : 48 * xp + 48, 448:512].astype(F32)
            for q in range(4):
                gdt[rows, 12 * q + 3 * xp : 12 * q + 3 * xp + 3] = part[:, 3 * q : 3 * q + 3]


def round_shift(v, axis, k, n=4):
    return lax.ppermute(v, axis, [(s, (s + k) % n) for s in range(n)])


def onward(v, k):
    return lax.ppermute(v, "z", [(s, s + k) for s in range(NZ) if 0 <= s + k < NZ])


def around(v, axis, n=4):
    return [v] + [round_shift(v, axis, k, n) for k in range(1, n)]


def after(value, *others):
    return lax.optimization_barrier((value,) + others)[0]


def local(
    tokens, norm_gain, w_main, w_dt, conv_weight, conv_bias, dt_bias, a_log, skip_gain,
    out_gain, w_out, cotangent,
):
    x, z, core, y = (lax.axis_index(name) for name in ("x", "z", "core", "y"))
    idx = jnp.stack([x, z, core, y]).astype(jnp.int32)

    def mine(v):
        shape = v.shape[:-1]
        v = v.reshape(shape + (NZ, NX, v.shape[-1] // 16))
        return lax.dynamic_index_in_dim(v, x, v.ndim - 2, False).reshape(shape + (-1,))

    par = jnp.concatenate(
        [
            jnp.concatenate([mine(conv_weight[:, :DI]), conv_weight[:, DI:]], axis=1),
            jnp.concatenate([mine(conv_bias[:DI]), conv_bias[DI:]])[None],
            jnp.pad(mine(out_gain)[None], ((0, 2), (0, CC - HW))),
        ],
        axis=0,
    )
    hp = jnp.pad(jnp.stack([mine(dt_bias), mine(a_log), mine(skip_gain)]), ((0, 5), (0, 128 - HL)))
    gain = norm_gain[None]

    wd = jnp.pad(
        w_dt.reshape(96, NZ, NX, 3).transpose(2, 0, 1, 3).reshape(NX, 96, HL),
        ((0, 0), (0, 0), (0, 128 - HL)),
    )
    packed = call(
        pack_weights,
        [((48, CA), BF)] * 4 + [((48, HW), BF)] * 4,
        [idx, w_main, wd],
        [((NX, 48, CA), BF), ((NX, 48, HW), BF)],
    )
    wa_x = [packed[0]] + [round_shift(packed[k], "x", k) for k in range(1, 4)]
    wa_z = around(jnp.concatenate(wa_x, axis=0), "z")
    toks = around(after(tokens, wa_x[1], wa_x[2], wa_x[3]), "x")
    wa_mine = jnp.concatenate(wa_z, axis=0)
    wa_other = round_shift(wa_mine, "core", 1, 2)
    late = after(packed[4], *toks[1:])
    wg_x = [late] + [round_shift(packed[4 + k], "x", k) for k in range(1, 4)]
    wo_half = lax.dynamic_slice_in_dim(w_out, core * 96, 96, 0)
    go = jnp.concatenate(
        [
            wo_half,
            jnp.concatenate([wg_x[0], wg_x[1]], axis=1),
            jnp.concatenate([wg_x[2], wg_x[3]], axis=1),
        ],
        axis=0,
    )
    go_mine = jnp.concatenate(around(after(go, *wa_z[1:]), "z"), axis=0)
    go_other = round_shift(go_mine, "core", 1, 2)
    cot = lax.all_gather(after(cotangent, *toks[1:]), "x", axis=0, tiled=True)

    normed, tail = call(
        norm_rows, [((T, D), BF), ((RIM, D), BF)], [idx, *toks, gain], flops=1 << 28
    )
    rim = onward(tail, 1)
    nfull, nt_mine, nt_other = call(
        turn,
        [((TR, D), BF), ((HW, TR), BF), ((HW, TR), BF)],
        [idx, normed, rim],
        [((D, T + 128), BF)],
        flops=1 << 30,
    )
    wa, ci, act, dsl, sm, sc, fp = call(
        project,
        [
            ((D, CA), BF), ((TR, CC), BF), ((T, CC), BF), ((T, CC), BF),
            ((3, T, 128), F32), ((NC, NS, HW), F32), ((NS + 16, HW), BF),
        ],
        [idx, nfull, wa_mine, wa_other, par, hp],
        [((TR, 256), F32)],
        flops=6 << 30,
    )
    states = [onward(fp, k) for k in (1, 2, 3)]
    (yi,) = call(within, [((T, HW), F32)], [idx, act, sm, hp], flops=6 << 30)
    gate, gny, wg, wo = call(
        gates,
        [((T, HW), F32), ((T, HW), F32), ((D, HW), BF), ((HW, D), BF)],
        [idx, nfull, go_mine, go_other, cot],
        flops=6 << 30,
    )
    mixed, hin, sums = call(
        mix,
        [((T, HW), F32), ((NC, NS, HW), BF), ((8, T), F32)],
        [idx, yi, act, sm, sc, *states, gate, gny, par],
        flops=4 << 30,
    )
    ny, gmix, ggate, bo, rp, small_g = call(
        gated,
        [
            ((T, HW), BF), ((T, HW), BF), ((T, HW), BF), ((T, D), BF), ((NS + 16, HW), BF),
            ((8, HW), F32),
        ],
        [idx, mixed, gate, gny, act, sm, *around(sums, "x"), wo, par],
        flops=4 << 30,
    )
    pulls = [onward(rp, -k) for k in (1, 2, 3)]
    gu, gbc, dsi = call(
        within_back,
        [((T, HW), F32), ((T, 2 * NS), F32), ((T, 128), F32)],
        [idx, act, gmix, sm],
        [((128, 128), F32)],
        flops=6 << 30,
    )
    early_scratch = [((HW, T), BF), ((HW // 2, T), BF)]
    (early,) = call(
        early_other, [((HW, D), BF)], [idx, ny, cot, ggate, nt_other], early_scratch, 3 << 30
    )
    got = round_shift(early, "core", 1, 2)
    (early,) = call(
        early_mine, [((HW, D), BF)], [idx, ny, cot, ggate, nt_mine, got], early_scratch, 3 << 30
    )
    early = lax.psum_scatter(early, "z", scatter_dimension=0, tiled=True)
    bo = lax.psum_scatter(bo, "x", scatter_dimension=0, tiled=True)
    gpa, small_c, small_h = call(
        across_back,
        [((TR, CA), BF), ((8, CC), F32), ((8, 128), F32)],
        [idx, act, gmix, sm, gu, gbc, dsi, hin, *pulls, dsl, ci, par, hp],
        [((T + 32, CC), F32), ((TR, 256), F32)],
        flops=8 << 30,
    )
    (late,) = call(late_other, [((HW, CA), BF)], [idx, gpa, nt_other], flops=2 << 30)
    got = round_shift(late, "core", 1, 2)
    (spill,) = call(rim_back, [((RIM, D), BF)], [idx, gpa, wa])
    spill = onward(spill, -1)
    (late,) = call(late_mine, [((HW, CA), BF)], [idx, gpa, nt_mine, got], flops=2 << 30)
    late = lax.psum_scatter(late, "z", scatter_dimension=0, tiled=True)
    gn0, gn1, gn2, gn3, gsum = call(
        normed_back,
        [((128, D), F32), ((128, D), BF), ((128, D), BF), ((128, D), BF), ((8, D), F32)],
        [idx, gpa, ggate, wa, wg, nfull, spill, gain],
        [((T, D), F32)],
        flops=4 << 30,
    )
    gns = [gn0] + [round_shift(b, "x", k) for k, b in ((1, gn1), (2, gn2), (3, gn3))]
    (grad_tokens,) = call(finish_back, [((128, D), BF)], [idx, tokens, cotangent, *gns, gain])
    (block_out,) = call(finish_out, [((128, D), BF)], [idx, tokens, bo])

    (small,) = call(small_pack, [((16, 512), F32)], [idx, gsum, small_c, small_g, small_h])
    (small,) = call(small_add, [((16, 512), F32)], [idx, small, round_shift(small, "core", 1, 2)])
    parts = call(
        split_y,
        [((320, 512), BF)] * 4,
        [idx, late, early, *around(small, "z")],
        [((4, 288 + 32, 512), BF)],
    )
    parts = [parts[0]] + [round_shift(parts[k], "y", k) for k in (1, 2, 3)]
    parts = call(
        sum_y,
        [((80, 512), BF)] * 4 + [((96, 512), BF)],
        [idx, *parts],
        [((192, 512), BF)],
    )
    wo_part = parts[4]
    parts = [parts[0]] + [round_shift(parts[k], "x", k) for k in (1, 2, 3)]
    final, g_gain, g_conv, g_ogain, g_heads = call(
        arrange_x,
        [((288, 512), BF), ((1, D), F32), ((8, DI + 256), F32), ((1, DI), F32), ((8, 128), F32)],
        [idx, *parts, wo_part],
        [((4, 16, 512), F32)],
    )
    finals = around(final, "y")
    other = round_shift(jnp.concatenate(finals, axis=0), "core", 1, 2)
    g_main, g_dt, g_out = call(
        finish_weights,
        [((96, 6400), F32), ((96, 48), F32), ((192, D), F32)],
        [idx, *finals, other],
        [((4, 288, 512), BF)],
    )
    return (
        block_out, grad_tokens, g_gain[0], g_main, g_dt, g_conv[:4], g_conv[4],
        g_heads[0, :48], g_heads[1, :48], g_heads[2, :48], g_ogain[0], g_out,
    )


def solution(mesh):
    grid = Mesh(mesh.devices.reshape(4, 2, 4, 4), ("y", "core", "z", "x"))
    rows = P(("y", "core", "z", "x"), None)
    shard = P(("z", "x"), None)
    whole = P()
    return jax.shard_map(
        local,
        mesh=grid,
        in_specs=(
            rows, whole, shard, shard, whole, whole, whole, whole, whole, whole, shard, rows,
        ),
        out_specs=(
            rows, rows, whole, shard, shard, whole, whole, whole, whole, whole, whole, shard,
        ),
        check_vma=False,
    )
```

```python
import functools

import jax
import jax.numpy as jnp
from jax import lax
from jax.experimental import pallas as pl
from jax.experimental.pallas import tpu as pltpu
from jax.sharding import Mesh, PartitionSpec as P

EPS = 1e-05
BF = jnp.bfloat16
F32 = jnp.float32
HIGH = lax.Precision.HIGHEST
NX = 4
NZ = 4
D = 1536
HL = 12
PW = 64
HW = 768
NS = 128
L = 128
NC = 4
T = 512
LIMIT = 12
RIM = 16
TR = T + RIM
CC = 1024
CA = 1152
DI = 3072


class Kernels:
    def __init__(self, idx):
        self.idx = idx

    def __call__(self, body, outs, ins, scratch=(), limit=LIMIT):
        specs = [pl.BlockSpec(memory_space=pltpu.SMEM)]
        specs += [pl.BlockSpec(memory_space=pltpu.VMEM)] * len(ins)
        got = pl.pallas_call(
            body,
            out_shape=[jax.ShapeDtypeStruct(shape, kind) for shape, kind in outs],
            in_specs=specs,
            out_specs=[pl.BlockSpec(memory_space=pltpu.VMEM)] * len(outs),
            scratch_shapes=[pltpu.VMEM(shape, kind) for shape, kind in scratch],
            compiler_params=pltpu.CompilerParams(vmem_limit_bytes=limit << 20),
            cost_estimate=pl.CostEstimate(
                flops=1 << 36, bytes_accessed=1 << 28, transcendentals=1 << 20
            ),
            name=body.__name__,
        )(self.idx, *ins)
        self.idx, *got = lax.optimization_barrier((self.idx, *got))
        return got


def mm(a, b):
    return lax.dot_general(a, b, (((1,), (0,)), ((), ())), preferred_element_type=F32)


def mm_nt(a, b):
    return lax.dot_general(a, b, (((1,), (1,)), ((), ())), preferred_element_type=F32)


def mm_tn(a, b):
    return lax.dot_general(a, b, (((0,), (0,)), ((), ())), preferred_element_type=F32)


def mm_high(a, b):
    return lax.dot_general(
        a, b, (((1,), (0,)), ((), ())), precision=HIGH, preferred_element_type=F32
    )


def iota2(shape, dim):
    return lax.broadcasted_iota(jnp.int32, shape, dim)


def spread_matrix(kind):
    return (
        lax.shift_right_logical(iota2((128, HW), 1), 6) == iota2((128, HW), 0)
    ).astype(kind)


def spread(v, e):
    hi = v.astype(BF)
    rest = v - hi.astype(F32)
    mid = rest.astype(BF)
    lo = (rest - mid.astype(F32)).astype(BF)
    return mm(hi, e) + mm(mid, e) + mm(lo, e)


def head_sums(v, e):
    hi = v.astype(BF)
    lo = (v - hi.astype(F32)).astype(BF)
    return mm_nt(hi, e) + mm_nt(lo, e)


def sigmoid(v):
    return 1.0 / (1.0 + jnp.exp(-v))


def chunk(ref, c, lanes=slice(None), base=0):
    return ref[pl.ds(pl.multiple_of(base + c * L, 16), L), lanes]


def params(idx, taps, bias, gain, rates, par, hp):
    par[...] = jnp.zeros_like(par)
    hp[...] = jnp.zeros_like(hp)
    par[0:4, HW:CC] = taps[:, DI : DI + 256]
    par[4:5, HW:CC] = bias[:, DI : DI + 256]
    for xp in range(NX):

        @pl.when(idx[0] == xp)
        def _():
            for zp in range(NZ):
                at = 768 * zp + 192 * xp
                to = slice(192 * zp, 192 * zp + 192)
                par[0:4, to] = taps[:, at : at + 192]
                par[4:5, to] = bias[:, at : at + 192]
                par[5:6, to] = gain[:, at : at + 192]
                at = 12 * zp + 3 * xp
                hp[0:3, 3 * zp : 3 * zp + 3] = rates[:, at : at + 3]


def pack_main(idx, wm, wd, o0, o1, o2, o3, scr):
    x, core = idx[0], idx[2]
    rows = pl.ds(pl.multiple_of(core * 48, 16), 48)
    for xp in range(NX):
        scr[xp, :, CC:CA] = jnp.zeros((48, 128), BF)
        for zp in range(NZ):
            at = 768 * zp + 192 * xp
            to = slice(192 * zp, 192 * zp + 192)
            scr[xp, :, to] = wm[rows, DI + at : DI + at + 192]
            scr[xp, :, CA + 192 * zp : CA + 192 * zp + 192] = wm[rows, at : at + 192]
            scr[xp, :, CC + 3 * zp : CC + 3 * zp + 3] = wd[
                rows, 12 * zp + 3 * xp : 12 * zp + 3 * xp + 3
            ]
        scr[xp, :, HW:CC] = wm[rows, 2 * DI : 2 * DI + 256]
    for k, out in enumerate((o0, o1, o2, o3)):
        out[...] = scr[lax.rem(x + k, NX)]


def stack_first(idx, a, b, c, d, out):
    for k, ref in enumerate((a, b, c, d)):
        out[48 * k : 48 * k + 48, :] = ref[:, 0:CA]


def stack_gate(idx, a, b, c, d, out):
    for k, ref in enumerate((a, b, c, d)):
        out[48 * k : 48 * k + 48, :] = ref[:, CA : CA + HW]


def norm_rows(idx, t0, t1, t2, t3, gain, normed, tail):
    x = idx[0]
    for k, piece in enumerate((t0, t1, t2, t3)):
        v = piece[...].astype(F32)
        root = lax.rsqrt(jnp.mean(v * v, axis=1, keepdims=True) + EPS)
        at = pl.multiple_of(lax.rem(x + NX - k, NX) * 128, 128)
        normed[pl.ds(at, 128), :] = (v * root * gain[...]).astype(BF)
    tail[...] = normed[T - RIM : T, :]


def turn(idx, normed, rim, mine, other, scr):
    core = idx[2]
    blank = jnp.zeros((128 - RIM, 128), F32)
    for j in range(D // 128):
        lanes = slice(128 * j, 128 * j + 128)
        scr[lanes, 0:T] = normed[:, lanes].astype(F32).T.astype(BF)
        edge = jnp.concatenate([rim[:, lanes].astype(F32), blank], axis=0)
        scr[lanes, T : T + 128] = edge.T.astype(BF)
    for block in range(16):
        for out, half in ((mine, core), (other, 1 - core)):
            at = pl.multiple_of(96 * block + 48 * half, 16)
            out[48 * block : 48 * block + 48, :] = scr[pl.ds(at, 48), 0:TR]


def place(idx, mine, other, out):
    x, z, core = idx[0], idx[1], idx[2]
    for step in range(NZ):
        for k in range(NX):
            block = 4 * lax.rem(z + NZ - step, NZ) + lax.rem(x + NX - k, NX)
            for refs, half in ((mine, core), (other, 1 - core)):
                at = pl.multiple_of(96 * block + 48 * half, 16)
                row = 48 * k
                ref = refs
                if isinstance(refs, tuple):
                    ref = refs[step]
                else:
                    row = row + 192 * step
                out[pl.ds(at, 48), :] = ref[row : row + 48, :]


def project(
    idx, normed, rim, m0, m1, m2, m3, t0, t1, t2, t3, par, hp,
    nfull, wa, ci, act, dsl, sm, sc, fp, scr,
):
    place(idx, (m0, m1, m2, m3), (t0, t1, t2, t3), wa)
    nfull[0:T, :] = normed[...]
    nfull[T:TR, :] = rim[...]

    raw = mm(nfull[0:T, :], wa[:, CC:CA]) + hp[0:1, :]
    held = iota2((T, 128), 1) < HL
    dt = jnp.where(held, jnp.maximum(raw, 0.0) + jnp.log1p(jnp.exp(-jnp.abs(raw))), 0.0)
    sm[0] = dt
    sm[2] = sigmoid(raw)
    decay = -dt * jnp.exp(hp[1:2, :])
    tri = (iota2((L, L), 0) >= iota2((L, L), 1)).astype(F32)
    for c in range(NC):
        sm[1, c * L : c * L + L, :] = mm_high(tri, decay[c * L : c * L + L])

    @pl.loop(0, 4)
    def _(j):
        lanes = pl.ds(pl.multiple_of(j * 256, 256), 256)
        low = mm(nfull[...], wa[:, lanes]).astype(BF)
        ci[:, lanes] = low
        scr[RIM:TR, :] = low[0:T].astype(F32)
        scr[0:RIM, :] = low[T:TR].astype(F32)
        pre = par[4:5, lanes] + par[0:1, lanes] * scr[13 : 13 + T, :]
        for k in range(1, 4):
            pre = pre + par[k : k + 1, lanes] * scr[13 + k : 13 + k + T, :]
        s = sigmoid(pre)
        act[:, lanes] = (pre * s).astype(BF)
        dsl[:, lanes] = (s * (1.0 + pre * (1.0 - s))).astype(BF)

    e = spread_matrix(BF)
    final = jnp.zeros((NS, HW), F32)
    total = jnp.zeros((8, HW), F32)
    for c in range(NC):
        rows = slice(c * L, c * L + L)
        s = sm[1, rows, :]
        last = s[L - 1 : L, :]
        w = spread(jnp.exp(last - s) * sm[0, rows, :], e)
        vw = (act[rows, 0:HW].astype(F32) * w).astype(BF)
        part = mm_tn(act[rows, HW : HW + NS], vw)
        sc[c] = part
        last_e = spread(jnp.broadcast_to(last, (8, 128)), e)
        final = jnp.exp(last_e[0:1]) * final + part
        total = total + last_e
    pack_state(fp, final, total)


def pack_state(fp, state, total):
    hi = total.astype(BF)
    lo = (total - hi.astype(F32)).astype(BF)
    fp[0:NS, :] = state.astype(BF)
    fp[NS : NS + 16, :] = jnp.concatenate(
        [hi.astype(F32), lo.astype(F32)], axis=0
    ).astype(BF)


def incoming(p1, p2, p3):
    t1 = p1[NS : NS + 16, :].astype(F32)
    t2 = p2[NS : NS + 16, :].astype(F32)
    t1 = t1[0:1] + t1[8:9]
    t2 = t2[0:1] + t2[8:9]
    return (
        p1[0:NS, :].astype(F32)
        + jnp.exp(t1) * p2[0:NS, :].astype(F32)
        + jnp.exp(t1 + t2) * p3[0:NS, :].astype(F32)
    )


def stack(idx, a, b, c, d, out):
    size = a.shape[0]
    for k, ref in enumerate((a, b, c, d)):
        out[size * k : size * k + size, :] = ref[...]


def gates(idx, nfull, gm, gt, om, ot, c0, c1, c2, c3, gate, gny, wg, wo, cot):
    x, core = idx[0], idx[2]
    place(idx, gm, gt, wg)
    for ref, half in ((om, core), (ot, 1 - core)):
        for z in range(NZ):
            at = pl.multiple_of(192 * z + 96 * half, 16)
            wo[pl.ds(at, 96), :] = ref[96 * z : 96 * z + 96, :]
    for k, piece in enumerate((c0, c1, c2, c3)):
        at = pl.multiple_of(lax.rem(x + NX - k, NX) * 128, 128)
        cot[pl.ds(at, 128), :] = piece[...]

    @pl.loop(0, 3)
    def _(j):
        lanes = pl.ds(pl.multiple_of(j * 256, 256), 256)
        gate[:, lanes] = mm(nfull[0:T, :], wg[:, lanes])
        gny[:, lanes] = mm_nt(cot[...], wo[lanes, :])


def within(idx, act, sm, hp, yi):
    e = spread_matrix(BF)
    skip = spread(jnp.broadcast_to(hp[2:3, :], (8, 128)), e)[0:1]
    left = iota2((L, 128), 1) < PW
    causal = iota2((L, L), 0) >= iota2((L, L), 1)

    @pl.loop(0, NC)
    def _(c):
        rows = pl.ds(pl.multiple_of(c * L, L), L)
        s = sm[1, rows, :]
        s_t = s.T
        v = act[rows, 0:HW].astype(F32)
        u = v * spread(sm[0, rows, :], e)
        scores = mm_nt(act[rows, HW + NS : CC], act[rows, HW : HW + NS])
        for j in range(HL // 2):
            parts = []
            for h in (2 * j, 2 * j + 1):
                gap = s[:, h : h + 1] - s_t[h : h + 1, :]
                parts.append((scores * jnp.exp(jnp.where(causal, gap, -1e30))).astype(BF))
            pair = u[:, 128 * j : 128 * j + 128]
            both = jnp.concatenate(
                [jnp.where(left, pair, 0.0), jnp.where(left, 0.0, pair)], axis=0
            ).astype(BF)
            yi[rows, 128 * j : 128 * j + 128] = mm(jnp.concatenate(parts, axis=1), both)
        yi[rows, :] += skip * v


def mix(idx, yi, act, sm, sc, p1, p2, p3, gate, gny, par, mixed, hin, sums):
    e = spread_matrix(BF)
    ones = jnp.ones((8, HW), BF)

    def rowsum(v):
        hi = v.astype(BF)
        lo = (v - hi.astype(F32)).astype(BF)
        return mm_nt(ones, hi) + mm_nt(ones, lo)

    state = incoming(p1, p2, p3)
    for c in range(NC):
        rows = slice(c * L, c * L + L)
        s = sm[1, rows, :]
        low = state.astype(BF)
        hin[c] = low
        y = yi[rows, :] + spread(jnp.exp(s), e) * mm(act[rows, HW + NS : CC], low)
        mixed[rows, :] = y
        z = gate[rows, :]
        g = y * (z * sigmoid(z))
        sq = rowsum(g * g)
        sg = rowsum(g * (gny[rows, :] * par[5:6, 0:HW]))
        sums[:, rows] = jnp.where(iota2((8, L), 0) == 0, sq, sg)
        last = spread(jnp.broadcast_to(s[L - 1 : L, :], (8, 128)), e)[0:1]
        state = jnp.exp(last) * state + sc[c]


def gated(
    idx, mixed, gate, gny, act, sm, s0, s1, s2, s3, wo, par,
    ny, gmix, ggate, bo, rp, small,
):
    e = spread_matrix(BF)
    sums = s0[...] + s1[...] + s2[...] + s3[...]
    gain = par[5:6, 0:HW]
    pick0 = (iota2((8, 128), 0) == 0).astype(F32)
    pick1 = (iota2((8, 128), 0) == 1).astype(F32)
    grad_gain = jnp.zeros((1, HW), F32)
    grad_skip = jnp.zeros((1, HW), F32)
    pulls = []
    totals = []
    for c in range(NC):
        rows = slice(c * L, c * L + L)
        here = sums[:, rows]
        sq = lax.dot_general(
            here, pick0, (((0,), (0,)), ((), ())), precision=HIGH, preferred_element_type=F32
        )
        sg = lax.dot_general(
            here, pick1, (((0,), (0,)), ((), ())), precision=HIGH, preferred_element_type=F32
        )
        r1 = lax.rsqrt(sq * (1.0 / DI) + EPS)
        pull = r1 * r1 * (sg * (1.0 / DI))
        r1 = jnp.concatenate([r1] * 6, axis=1)
        pull = jnp.concatenate([pull] * 6, axis=1)
        y = mixed[rows, :]
        z = gate[rows, :]
        sz = sigmoid(z)
        sil = z * sz
        g = y * sil
        gn = gny[rows, :]
        ghat = g * r1
        ny[rows, :] = (ghat * gain).astype(BF)
        grad_gain = grad_gain + jnp.sum(gn * ghat, axis=0, keepdims=True)
        gg = r1 * (gn * gain - g * pull)
        gm = gg * sil
        gmix[rows, :] = gm.astype(BF)
        ggate[rows, :] = (gg * y * (sz * (1.0 + z * (1.0 - sz)))).astype(BF)
        grad_skip = grad_skip + jnp.sum(gm * act[rows, 0:HW].astype(F32), axis=0, keepdims=True)
        s = sm[1, rows, :]
        pulls.append(mm_tn(act[rows, HW + NS : CC], (gm * spread(jnp.exp(s), e)).astype(BF)))
        totals.append(spread(jnp.broadcast_to(s[L - 1 : L, :], (8, 128)), e))
    state = jnp.zeros((NS, HW), F32)
    total = jnp.zeros((8, HW), F32)
    for c in reversed(range(NC)):
        state = jnp.exp(totals[c][0:1]) * state + pulls[c]
        total = total + totals[c]
    pack_state(rp, state, total)
    small[0:1, :] = grad_gain
    small[1:2, :] = grad_skip

    @pl.loop(0, 6)
    def _(j):
        lanes = pl.ds(pl.multiple_of(j * 256, 256), 256)
        bo[:, lanes] = mm(ny[...], wo[:, lanes]).astype(BF)


def within_back(idx, act, gmix, sm, gu, gbc, dsi, rw):
    left = iota2((L, 128), 1) < PW
    lane = iota2((L, 128), 1)
    causal = iota2((L, L), 1) >= iota2((L, L), 0)
    rw[...] = jnp.zeros_like(rw)

    @pl.loop(0, NC)
    def _(c):
        rows = pl.ds(pl.multiple_of(c * L, L), L)
        s = sm[1, rows, :]
        s_t = s.T
        dt = sm[0, rows, :]
        b = act[rows, HW : HW + NS]
        r = act[rows, HW + NS : CC]
        scores = mm_nt(b, r)
        grad_scores = jnp.zeros((L, L), F32)
        cols = jnp.zeros((L, 128), F32)
        for j in range(HL // 2):
            v = act[rows, 128 * j : 128 * j + 128].astype(F32)
            g = gmix[rows, 128 * j : 128 * j + 128]
            gf = g.astype(F32)
            parts = []
            for i in range(2):
                h = 2 * j + i
                gap = s_t[h : h + 1, :] - s[:, h : h + 1]
                q = jnp.exp(jnp.where(causal, gap, -1e30))
                own = jnp.where(left, v, 0.0) if i == 0 else jnp.where(left, 0.0, v)
                vg = mm_nt(own.astype(BF), g) * (q * dt[:, h : h + 1])
                grad_scores = grad_scores + vg
                w = scores * vg
                rw[h : h + 1, :] = jnp.sum(w, axis=0, keepdims=True)
                cols = jnp.where(lane == h, jnp.sum(w, axis=1, keepdims=True), cols)
                parts.append((scores * q).astype(BF))
            both = jnp.concatenate(
                [jnp.where(left, gf, 0.0), jnp.where(left, 0.0, gf)], axis=0
            ).astype(BF)
            gu[rows, 128 * j : 128 * j + 128] = mm(jnp.concatenate(parts, axis=1), both)
        dsi[rows, :] = rw[...].T - cols
        low = grad_scores.astype(BF)
        gbc[rows, 0:NS] = mm(low, r)
        gbc[rows, NS : 2 * NS] = mm_tn(low, b)


def across_back(
    idx, act, gmix, sm, gu, gbc, dsi, hin, p1, p2, p3, dsl, ci, par, hp, gains, turned,
    ggate, wa, wg, nfull, gain, block, gpa, late, out, gn, small, gps, cis, acc,
):
    e = spread_matrix(BF)
    skip = spread(jnp.broadcast_to(hp[2:3, :], (8, 128)), e)[0:1]
    rate = jnp.exp(hp[1:2, :])
    upper = (iota2((L, L), 1) >= iota2((L, L), 0)).astype(F32)
    below = (iota2((L, L), 0) > iota2((L, L), 1)).astype(F32)
    gps[0:RIM, :] = jnp.zeros((RIM, D), F32)
    gps[RIM + T : RIM + T + 16, :] = jnp.zeros((16, D), F32)
    state = incoming(p1, p2, p3)
    grad_log = jnp.zeros((1, 128), F32)
    grad_bias = jnp.zeros((1, 128), F32)
    gpa[T:TR, CC:CA] = jnp.zeros((RIM, 128), BF)
    for c in reversed(range(NC)):
        rows = slice(c * L, c * L + L)
        b = act[rows, HW : HW + NS]
        r = act[rows, HW + NS : CC]
        low = state.astype(BF)
        s = sm[1, rows, :]
        dt = sm[0, rows, :]
        last = s[L - 1 : L, :]
        tail_e = spread(jnp.exp(last - s), e)
        dt_e = spread(dt, e)
        grow_e = spread(jnp.exp(s), e)
        last_e = jnp.exp(spread(jnp.broadcast_to(last, (8, 128)), e)[0:1])
        v = act[rows, 0:HW].astype(F32)
        g = gmix[rows, :].astype(F32)
        carried = tail_e * mm(b, low)
        grad_u = gu[rows, :] + carried
        u = v * dt_e
        grad_v = dt_e * grad_u + skip * g
        grad_b = gbc[rows, 0:NS] + mm_nt((u * tail_e).astype(BF), low)
        gs = (g * grow_e).astype(BF)
        h = hin[c]
        grad_c = gbc[rows, NS : 2 * NS] + mm_nt(gs, h)
        inter = head_sums(g * (grow_e * mm(r, h)), e)
        kept = head_sums(u * carried, e)
        grad_step = head_sums(v * grad_u, e)
        cross = jnp.sum(h.astype(F32) * state, axis=0, keepdims=True) * last_e
        cross = head_sums(jnp.broadcast_to(cross, (8, HW)), e)[0:1]
        grad_a = mm_high(upper, dsi[rows, :] + inter) + mm_high(below, kept) + cross
        grad_raw = (grad_step - rate * grad_a) * sm[2, rows, :]
        grad_log = grad_log + jnp.sum(grad_a * dt, axis=0, keepdims=True)
        grad_bias = grad_bias + jnp.sum(grad_raw, axis=0, keepdims=True)
        held = iota2((L, 128), 1) < HL
        gpa[rows, CC:CA] = jnp.where(held, grad_raw, 0.0).astype(BF)
        d = dsl[rows, :].astype(F32)
        to = slice(RIM + c * L, RIM + c * L + L)
        gps[to, 0:HW] = grad_v * d[:, 0:HW]
        gps[to, HW : HW + NS] = grad_b * d[:, HW : HW + NS]
        gps[to, HW + NS : CC] = grad_c * d[:, HW + NS : CC]
        state = last_e * state + mm_tn(r, gs)

    @pl.loop(0, 4)
    def _(j):
        lanes = pl.ds(pl.multiple_of(j * 256, 256), 256)
        cis[RIM:TR, :] = ci[0:T, lanes].astype(F32)
        cis[0:RIM, :] = ci[T:TR, lanes].astype(F32)
        gp = gps[RIM : RIM + T, lanes]
        small[4:5, lanes] = jnp.sum(gp, axis=0, keepdims=True)
        out = par[3:4, lanes] * gps[0:TR, lanes]
        for k in range(4):
            small[k : k + 1, lanes] = jnp.sum(
                gp * cis[13 + k : 13 + k + T, :], axis=0, keepdims=True
            )
            if k < 3:
                out = out + par[k : k + 1, lanes] * gps[3 - k : 3 - k + TR, lanes]
        low = out.astype(BF)
        gpa[0:T, lanes] = low[RIM:TR]
        gpa[T:TR, lanes] = low[0:RIM]

    for j in range(0, CA, 384):
        late[:, j : j + 384] = mm(turned[...], gpa[:, j : j + 384]).astype(BF)

    for j in range(0, D, 256):
        lanes = slice(j, j + 256)
        acc[:, lanes] = mm_nt(gpa[...], wa[lanes, :])
        acc[0:T, lanes] += mm_nt(ggate[...], wg[lanes, :])
        gps[0:8, lanes] = jnp.broadcast_to(
            jnp.sum(acc[:, lanes] * nfull[:, lanes].astype(F32), axis=0, keepdims=True)
            / gain[:, lanes],
            (8, 256),
        )

    for k in range(NX):
        rows = slice(128 * k, 128 * k + 128)
        gn[k, 0:128, :] = acc[rows, :].astype(BF)
        gn[k, 128:144, :] = acc[T:TR, :].astype(BF)
        gn[k, 144:272, :] = block[rows, :]

    for j in range(3):
        out[j : j + 1, :] = gps[0:1, 512 * j : 512 * j + 512]
    for k in range(5):
        for j in range(2):
            out[3 + 2 * k + j : 4 + 2 * k + j, :] = small[k : k + 1, 512 * j : 512 * j + 512]
    out[13:14, :] = gains[0:1, 0:512]
    out[14:15, 0:256] = gains[0:1, 512:768]
    out[14:15, 256:384] = head_sums(jnp.broadcast_to(gains[1:2, :], (8, HW)), e)[0:1]
    out[14:15, 384:512] = grad_bias
    out[15:16, 0:128] = -rate * grad_log
    out[15:16, 128:512] = jnp.zeros((1, 384), F32)


def finish_out(idx, tokens, summed, out):
    out[...] = (tokens[...].astype(F32) + summed[144:272].astype(F32)).astype(BF)


def finish_back(idx, tokens, cot, summed, spill, gain, out, acc):
    v = tokens[...].astype(F32)
    root = lax.rsqrt(jnp.mean(v * v, axis=1, keepdims=True) + EPS)
    acc[...] = summed[0:128].astype(F32)
    acc[128 - RIM : 128, :] += spill[...].astype(F32)
    q = acc[...] * gain[...]
    pull = jnp.mean(q * v, axis=1, keepdims=True)
    out[...] = (cot[...].astype(F32) + root * (q - v * (root * root) * pull)).astype(BF)


def grad_early(idx, ny, cot, ggate, tm, tt, mine, other, nyt, rows, part):
    core, y = idx[2], idx[3]
    for j in range(HW // 128):
        lanes = slice(128 * j, 128 * j + 128)
        nyt[lanes, :] = ny[:, lanes].astype(F32).T.astype(BF)
    for half, which in enumerate((core, 1 - core)):
        for z in range(NZ):
            at = pl.multiple_of(192 * z + 96 * which, 16)
            row = 384 * half + 96 * z
            rows[row : row + 96, :] = nyt[pl.ds(at, 96), :]
    for q in range(4):
        k = lax.rem(q + 4 - y, 4)
        part[...] = mm(rows[...], cot[:, 384 * q : 384 * q + 384]).astype(BF)
        for half, (turned, out) in enumerate(((tm, mine), (tt, other))):
            gate = mm(turned[:, 0:T], ggate[:, 192 * q : 192 * q + 192]).astype(BF)
            out[k, :, 0:192] = gate
            for z in range(NZ):
                row = 384 * half + 96 * z
                out[k, 192 * z : 192 * z + 96, 192:384] = part[row : row + 96, 0:192]
                out[k, 192 * z + 96 : 192 * z + 192, 192:384] = part[row : row + 96, 192:384]


def add_early(idx, a, b, o0, o1, o2, o3):
    for k, out in enumerate((o0, o1, o2, o3)):
        out[...] = (a[k].astype(F32) + b[k].astype(F32)).astype(BF)


def sum_early(idx, a, b, c, d, out):
    out[...] = (
        a[...].astype(F32) + b[...].astype(F32) + (c[...].astype(F32) + d[...].astype(F32))
    ).astype(BF)


def late_mine(idx, gpa, turned, got, s0, s1, early, o0, o1, o2, o3, acc):
    z = idx[1]
    for j in range(0, CA, 384):
        lanes = slice(j, j + 384)
        acc[:, lanes] = (mm(turned[...], gpa[:, lanes]) + got[:, lanes].astype(F32)).astype(BF)
    for k, out in enumerate((o0, o1, o2, o3)):
        at = pl.multiple_of(lax.rem(z + k, NZ) * 192, 64)
        out[0:192, :] = acc[pl.ds(at, 192), :]
        out[192:208, 0:CC] = wide(s0[...] + s1[...])
        out[192:208, CC:CA] = jnp.zeros((16, CA - CC), BF)
        for j in range(3):
            out[208:272, 384 * j : 384 * j + 384] = early[
                pl.ds(pl.multiple_of(at + 64 * j, 64), 64), :
            ]


def wide(v):
    hi = v.astype(BF).astype(F32)
    return jnp.concatenate([hi, v - hi], axis=1).astype(BF)


def halves(v):
    hi = v.astype(BF).astype(F32)
    return jnp.concatenate([hi, v - hi], axis=0).astype(BF)


def joined(v):
    v = v.astype(F32)
    return v[0:16] + v[16:32]


def split_y(idx, l0, l1, l2, l3, o0, o1, o2, o3, early, scr, late):
    y = idx[3]
    total = l0[...].astype(F32) + l1[...].astype(F32) + (l2[...].astype(F32) + l3[...].astype(F32))
    late[...] = total[0:192].astype(BF)
    for j in range(3):
        early[64 * j : 64 * j + 64, :] = total[208:272, 384 * j : 384 * j + 384].astype(BF)
    small = total[192:208, 0:512] + total[192:208, 512:1024]
    small = halves(small)
    for q in range(4):
        scr[q, :, 0:192] = late[:, 192 * q : 192 * q + 192]
        scr[q, :, 192:256] = late[:, HW + 64 * q : HW + 64 * q + 64]
        scr[q, :, 256:384] = late[:, CC:CA]
        for j in range(4):
            scr[q, 32 * j : 32 * j + 32, 384:512] = small[:, 128 * j : 128 * j + 128]
        scr[q, 128:192, 384:512] = jnp.zeros((64, 128), BF)
    for k, out in enumerate((o0, o1, o2, o3)):
        out[...] = scr[lax.rem(y + k, 4)]


def sum_y(idx, a, b, c, d, early, o0, o1, o2, o3, scr):
    x = idx[0]
    total = a[:, 0:384].astype(F32) + b[:, 0:384].astype(F32)
    total = total + (c[:, 0:384].astype(F32) + d[:, 0:384].astype(F32))
    scr[:, 0:384] = total.astype(BF)
    scr[:, 384:576] = early[:, 0:192]
    scr[:, 576:640] = jnp.zeros((192, 64), BF)
    small = jnp.concatenate(
        [
            sum(joined(ref[32 * j : 32 * j + 32, 384:512]) for ref in (a, b, c, d))
            for j in range(4)
        ],
        axis=1,
    )
    small = halves(small)
    for k, out in enumerate((o0, o1, o2, o3)):
        at = pl.multiple_of(lax.rem(x + k, NX) * 48, 16)
        out[0:48, :] = scr[pl.ds(at, 48), :]
        out[48:80, 0:512] = small
        out[48:80, 512:640] = jnp.zeros((32, 128), BF)


def arrange_x(idx, a, b, c, d, early, out, gain, conv, ogain, heads, scr):
    x = idx[0]
    shared = jnp.zeros((48, 64), F32)
    for k, ref in enumerate((a, b, c, d)):
        source = lax.rem(x + NX - k, NX)
        rows = pl.ds(pl.multiple_of(source * 48, 16), 48)
        out[rows, 0:256] = ref[0:48, 0:256]
        out[rows, 256:448] = ref[0:48, 384:576]
        out[rows, 448:512] = ref[0:48, 256:320]
        shared = shared + ref[0:48, 192:256].astype(F32)
        scr[source] = joined(ref[48:80, 0:512])
    out[0:48, 192:256] = shared.astype(BF)
    out[:, 512:704] = early[:, 192:384]
    out[:, 704:768] = jnp.zeros((192, 64), BF)
    both = scr[0] + scr[1] + (scr[2] + scr[3])
    for j in range(3):
        gain[0:1, 512 * j : 512 * j + 512] = both[j : j + 1, :]
    for k in range(5):
        conv[k : k + 1, DI : DI + 256] = both[4 + 2 * k : 5 + 2 * k, 256:512]
    heads[...] = jnp.zeros_like(heads)
    for xp in range(NX):
        own = scr[xp]
        for q in range(4):
            lane = 768 * q + 192 * xp
            for k in range(5):
                for at, size in pieces(192 * q, 192):
                    conv[k : k + 1, lane + at - 192 * q : lane + at - 192 * q + size] = own[
                        3 + 2 * k + at // 512 : 4 + 2 * k + at // 512, at % 512 : at % 512 + size
                    ]
            for at, size in pieces(192 * q, 192):
                ogain[0:1, lane + at - 192 * q : lane + at - 192 * q + size] = own[
                    13 + at // 512 : 14 + at // 512, at % 512 : at % 512 + size
                ]
            to = slice(12 * q + 3 * xp, 12 * q + 3 * xp + 3)
            heads[0:1, to] = own[14:15, 384 + 3 * q : 387 + 3 * q]
            heads[1:2, to] = own[15:16, 3 * q : 3 * q + 3]
            heads[2:3, to] = own[14:15, 256 + 3 * q : 259 + 3 * q]


def pieces(at, size):
    end = at + size
    while at < end:
        step = min(end, (at // 512 + 1) * 512) - at
        yield at, step
        at += step


def finish_weights(idx, a, b, c, d, e, f, g, h, gmain, gdt, gout, scr):
    y, core = idx[3], idx[2]
    for half in range(2):
        place = lax.rem(core + half, 2)
        for k, ref in enumerate((a, b, c, d) if half == 0 else (e, f, g, h)):
            scr[lax.rem(y + 4 - k, 4)] = ref[...]
        rows = pl.ds(pl.multiple_of(48 * place, 16), 48)
        long = pl.ds(pl.multiple_of(96 * place, 16), 96)
        for q in range(4):
            gout[long, 384 * q : 384 * q + 192] = scr[q, 0:96, 512:704].astype(F32)
            gout[long, 384 * q + 192 : 384 * q + 384] = scr[q, 96:192, 512:704].astype(F32)
            gmain[rows, 6144 + 64 * q : 6144 + 64 * q + 64] = scr[q, 0:48, 192:256].astype(F32)
            for xp in range(NX):
                lane = 768 * q + 192 * xp
                part = scr[q, 48 * xp : 48 * xp + 48, :].astype(F32)
                gmain[rows, lane : lane + 192] = part[:, 256:448]
                gmain[rows, DI + lane : DI + lane + 192] = part[:, 0:192]
        for xp in range(NX):
            part = scr[0, 48 * xp : 48 * xp + 48, 448:512].astype(F32)
            for q in range(4):
                gdt[rows, 12 * q + 3 * xp : 12 * q + 3 * xp + 3] = part[:, 3 * q : 3 * q + 3]


def round_shift(v, axis, k, n=4):
    return lax.ppermute(v, axis, [(s, (s + k) % n) for s in range(n)])


def onward(v, k):
    return lax.ppermute(v, "z", [(s, s + k) for s in range(NZ) if 0 <= s + k < NZ])


def around(v, axis, n=4):
    return [v] + [round_shift(v, axis, k, n) for k in range(1, n)]


def spread_out(parts, axis, n=4):
    return [parts[0]] + [round_shift(parts[k], axis, k, n) for k in range(1, n)]


def after(value, *others):
    return lax.optimization_barrier((value,) + others)[0]


def after_all(values, *others):
    return list(lax.optimization_barrier(tuple(values) + others)[: len(values)])


def local(
    tokens, norm_gain, w_main, w_dt, conv_weight, conv_bias, dt_bias, a_log, skip_gain,
    out_gain, w_out, cotangent,
):
    x, z, core, y = (lax.axis_index(name) for name in ("x", "z", "core", "y"))
    idx = jnp.stack([x, z, core, y]).astype(jnp.int32)

    gain = norm_gain[None]
    rates = jnp.stack([dt_bias, a_log, skip_gain])

    call = Kernels(idx)
    wo_mine = lax.dynamic_slice(w_out, (core * 96, 0), (96, D))
    wo_mine = lax.all_gather(wo_mine, "z", axis=0, tiled=True)
    first = call(
        pack_main, [((48, CA + HW), BF)] * 4, [w_main, w_dt], [((NX, 48, CA + HW), BF)]
    )
    first = after_all(first)
    first = spread_out(first, "x")
    tok = around(after(tokens, *first[1:]), "x")
    par, hp = call(
        params,
        [((8, CC), F32), ((8, 128), F32)],
        [conv_weight, conv_bias[None], out_gain[None], rates],
    )
    (rows_a,) = call(stack_first, [((192, CA), BF)], first)
    wa_mine = around(rows_a, "z")
    normed, tail = call(norm_rows, [((T, D), BF), ((RIM, D), BF)], [*tok, gain])
    rim = onward(tail, 1)
    first = after_all(first, *wa_mine)
    (rows_g,) = call(stack_gate, [((192, HW), BF)], first)
    wa_other = [round_shift(v, "core", 1, 2) for v in wa_mine]
    wg_mine = around(after(rows_g, *wa_other), "z")
    cots = around(after(cotangent, normed), "x")
    wo_mine = after(wo_mine, rows_g)
    wo_other = round_shift(wo_mine, "core", 1, 2)
    normed, wo_other = after_all([normed, wo_other], tail)
    nt_mine, nt_other = call(
        turn, [((HW, TR), BF), ((HW, TR), BF)], [normed, rim], [((D, T + 128), BF)]
    )
    nfull, wa, ci, act, dsl, sm, sc, fp = call(
        project,
        [
            ((TR, D), BF), ((D, CA), BF), ((TR, CC), BF), ((T, CC), BF), ((T, CC), BF),
            ((3, T, 128), F32), ((NC, NS, HW), F32), ((NS + 16, HW), BF),
        ],
        [normed, rim, *wa_mine, *wa_other, par, hp],
        [((TR, 256), F32)],
            )
    states = [onward(fp, k) for k in (1, 2, 3)]
    wg_mine = after_all(wg_mine, act)
    (wg_mine,) = call(stack, [((HW, HW), BF)], wg_mine)
    wg_other = round_shift(wg_mine, "core", 1, 2)
    (yi,) = call(within, [((T, HW), F32)], [act, sm, hp])
    gate, gny, wg, wo, cot = call(
        gates,
        [((T, HW), F32), ((T, HW), F32), ((D, HW), BF), ((HW, D), BF), ((T, D), BF)],
        [nfull, wg_mine, wg_other, wo_mine, wo_other, *cots],
    )
    mixed, hin, sums = call(
        mix,
        [((T, HW), F32), ((NC, NS, HW), BF), ((8, T), F32)],
        [yi, act, sm, sc, *states, gate, gny, par],
    )
    ny, gmix, ggate, bo, rp, small_g = call(
        gated,
        [((T, HW), BF)] * 3 + [((T, D), BF), ((NS + 16, HW), BF), ((8, HW), F32)],
        [mixed, gate, gny, act, sm, *around(sums, "x"), wo, par],
    )
    pulls = [onward(rp, -k) for k in (1, 2, 3)]
    early, got = call(
        grad_early,
        [((4, HW, 384), BF)] * 2,
        [ny, cot, ggate, nt_mine, nt_other],
        [((HW, T), BF), ((HW, T), BF), ((HW, 384), BF)],
    )
    got = round_shift(got, "core", 1, 2)
    gu, gbc, dsi = call(
        within_back,
        [((T, HW), F32), ((T, 2 * NS), F32), ((T, 128), F32)],
        [act, gmix, sm],
        [((128, 128), F32)],
    )
    got, *pulls = after_all([got, *pulls], gu)
    early = call(add_early, [((HW, 384), BF)] * 4, [after(early, *pulls), got])
    early = spread_out(early, "y")
    gpa, late, small, gn = call(
        across_back,
        [((TR, CA), BF), ((HW, CA), BF), ((16, 512), F32), ((NX, 272, D), BF)],
        [
            act, gmix, sm, gu, gbc, dsi, hin, *pulls, dsl, ci, par, hp, small_g, nt_other,
            ggate, wa, wg, nfull, gain, bo,
        ],
        [((8, CC), F32), ((T + 32, D), F32), ((TR, 256), F32), ((TR, D), F32)],
        limit=24,
    )
    got = round_shift(late, "core", 1, 2)
    small_got = round_shift(small, "core", 1, 2)
    (early,) = call(sum_early, [((HW, 384), BF)], early)
    late = call(
        late_mine,
        [((272, CA), BF)] * 4,
        [gpa, nt_mine, got, small, small_got, early],
        [((HW, CA), BF)],
    )
    late = spread_out(late, "z")
    gn = lax.psum_scatter(gn, "x", scatter_dimension=0, tiled=True).reshape(272, D)
    *late, gn = after_all([*late, gn])
    *parts, early = call(
        split_y,
        [((192, 512), BF)] * 4 + [((192, 384), BF)],
        late,
        [((4, 192, 512), BF), ((192, CA), BF)],
    )
    parts = spread_out(parts, "y")
    parts = call(
        sum_y,
        [((80, 640), BF)] * 4,
        [*parts, early],
        [((192, 640), BF)],
    )
    parts = spread_out(parts, "x")
    gn = after(gn, parts[0])
    spill = lax.ppermute(
        gn[128:144], ("z", "x"), [(4 * s + 3, 4 * s - 1) for s in range(1, NZ)]
    )
    (block_out,) = call(finish_out, [((128, D), BF)], [tokens, gn])
    final, g_gain, g_conv, g_ogain, g_heads = call(
        arrange_x,
        [((192, HW), BF), ((1, D), F32), ((8, DI + 256), F32), ((1, DI), F32), ((8, 128), F32)],
        [*parts, early],
        [((4, 16, 512), F32)],
    )
    finals = around(final, "y")
    (grad_tokens,) = call(
        finish_back,
        [((128, D), BF)],
        [tokens, cotangent, gn, spill, gain],
        [((128, D), F32)],
    )
    others = [round_shift(v, "core", 1, 2) for v in finals]
    g_main, g_dt, g_out = call(
        finish_weights,
        [((96, 6400), F32), ((96, 48), F32), ((192, D), F32)],
        [*finals, *others],
        [((4, 192, HW), BF)],
    )
    return (
        block_out, grad_tokens, g_gain[0], g_main, g_dt, g_conv[:4], g_conv[4],
        g_heads[0, :48], g_heads[1, :48], g_heads[2, :48], g_ogain[0], g_out,
    )


def solution(mesh):
    grid = Mesh(mesh.devices.reshape(4, 2, 4, 4), ("y", "core", "z", "x"))
    rows = P(("y", "core", "z", "x"), None)
    shard = P(("z", "x"), None)
    whole = P()
    return jax.shard_map(
        local,
        mesh=grid,
        in_specs=(
            rows, whole, shard, shard, whole, whole, whole, whole, whole, whole, shard, rows,
        ),
        out_specs=(
            rows, rows, whole, shard, shard, whole, whole, whole, whole, whole, whole, shard,
        ),
        check_vma=False,
    )
```

```python
import functools

import jax
import jax.numpy as jnp
from jax import lax
from jax.experimental import pallas as pl
from jax.experimental.pallas import tpu as pltpu
from jax.sharding import Mesh, PartitionSpec as P

EPS = 1e-05
BF = jnp.bfloat16
F32 = jnp.float32
HIGH = lax.Precision.HIGHEST
NX = 4
NZ = 4
D = 1536
HL = 12
PW = 64
HW = 768
NS = 128
L = 128
NC = 4
T = 512
LIMIT = 12
RIM = 16
TR = T + RIM
CC = 1024
HALF = 144
CA = 1152
DI = 3072


class Kernels:
    def __init__(self, idx):
        self.idx = idx

    def __call__(self, body, outs, ins, scratch=(), limit=LIMIT, light=False):
        specs = [pl.BlockSpec(memory_space=pltpu.SMEM)]
        specs += [pl.BlockSpec(memory_space=pltpu.VMEM)] * len(ins)
        got = pl.pallas_call(
            body,
            out_shape=[jax.ShapeDtypeStruct(shape, kind) for shape, kind in outs],
            in_specs=specs,
            out_specs=[pl.BlockSpec(memory_space=pltpu.VMEM)] * len(outs),
            scratch_shapes=[pltpu.VMEM(shape, kind) for shape, kind in scratch],
            compiler_params=pltpu.CompilerParams(vmem_limit_bytes=limit << 20),
            cost_estimate=pl.CostEstimate(
                flops=1 if light else 1 << 36,
                bytes_accessed=1 if light else 1 << 28,
                transcendentals=1 if light else 1 << 20,
            ),
            name=body.__name__,
        )(self.idx, *ins)
        self.idx, *got = lax.optimization_barrier((self.idx, *got))
        return got


def mm(a, b):
    return lax.dot_general(a, b, (((1,), (0,)), ((), ())), preferred_element_type=F32)


def mm_nt(a, b):
    return lax.dot_general(a, b, (((1,), (1,)), ((), ())), preferred_element_type=F32)


def mm_tn(a, b):
    return lax.dot_general(a, b, (((0,), (0,)), ((), ())), preferred_element_type=F32)


def mm_high(a, b):
    return lax.dot_general(
        a, b, (((1,), (0,)), ((), ())), precision=HIGH, preferred_element_type=F32
    )


def iota2(shape, dim):
    return lax.broadcasted_iota(jnp.int32, shape, dim)


def spread_matrix(kind):
    return (
        lax.shift_right_logical(iota2((128, HW), 1), 6) == iota2((128, HW), 0)
    ).astype(kind)


def spread(v, e):
    hi = v.astype(BF)
    rest = v - hi.astype(F32)
    mid = rest.astype(BF)
    lo = (rest - mid.astype(F32)).astype(BF)
    return mm(hi, e) + mm(mid, e) + mm(lo, e)


def head_sums(v, e):
    hi = v.astype(BF)
    lo = (v - hi.astype(F32)).astype(BF)
    return mm_nt(hi, e) + mm_nt(lo, e)


def sigmoid(v):
    return 1.0 / (1.0 + jnp.exp(-v))


def chunk(ref, c, lanes=slice(None), base=0):
    return ref[pl.ds(pl.multiple_of(base + c * L, 16), L), lanes]


def params(idx, taps, bias, gain, rates, par, hp):
    par[...] = jnp.zeros_like(par)
    hp[...] = jnp.zeros_like(hp)
    par[0:4, HW:CC] = taps[:, DI : DI + 256]
    par[4:5, HW:CC] = bias[:, DI : DI + 256]
    for xp in range(NX):

        @pl.when(idx[0] == xp)
        def _():
            for zp in range(NZ):
                at = 768 * zp + 192 * xp
                to = slice(192 * zp, 192 * zp + 192)
                par[0:4, to] = taps[:, at : at + 192]
                par[4:5, to] = bias[:, at : at + 192]
                par[5:6, to] = gain[:, at : at + 192]
                at = 12 * zp + 3 * xp
                hp[0:3, 3 * zp : 3 * zp + 3] = rates[:, at : at + 3]


def pack_main(idx, wm, wd, o0, o1, o2, o3, scr):
    x, core = idx[0], idx[2]
    rows = pl.ds(pl.multiple_of(core * 48, 16), 48)
    for xp in range(NX):
        scr[xp, :, CC:CA] = jnp.zeros((48, 128), BF)
        for zp in range(NZ):
            at = 768 * zp + 192 * xp
            to = slice(192 * zp, 192 * zp + 192)
            scr[xp, :, to] = wm[rows, DI + at : DI + at + 192]
            scr[xp, :, CA + 192 * zp : CA + 192 * zp + 192] = wm[rows, at : at + 192]
            scr[xp, :, CC + 3 * zp : CC + 3 * zp + 3] = wd[
                rows, 12 * zp + 3 * xp : 12 * zp + 3 * xp + 3
            ]
        scr[xp, :, HW:CC] = wm[rows, 2 * DI : 2 * DI + 256]
    for k, out in enumerate((o0, o1, o2, o3)):
        out[...] = scr[lax.rem(x + k, NX)]


def stack(idx, a, b, c, d, out):
    size = a.shape[0]
    for k, ref in enumerate((a, b, c, d)):
        out[size * k : size * k + size, :] = ref[...]


def norm_rows(idx, both, gain, normed, tail, cot):
    for k in range(NX):
        v = both[256 * k : 256 * k + 128, :].astype(F32)
        root = lax.rsqrt(jnp.mean(v * v, axis=1, keepdims=True) + EPS)
        normed[128 * k : 128 * k + 128, :] = (v * root * gain[...]).astype(BF)
        cot[128 * k : 128 * k + 128, :] = both[256 * k + 128 : 256 * k + 256, :]
    tail[...] = normed[T - RIM : T, :]


def turn(idx, nfull, mine, other, scr):
    core = idx[2]
    blank = jnp.zeros((128 - RIM, 128), F32)
    for j in range(D // 128):
        lanes = slice(128 * j, 128 * j + 128)
        scr[lanes, 0:T] = nfull[0:T, lanes].astype(F32).T.astype(BF)
        edge = jnp.concatenate([nfull[T:TR, lanes].astype(F32), blank], axis=0)
        scr[lanes, T : T + 128] = edge.T.astype(BF)
    for block in range(16):
        for out, half in ((mine, core), (other, 1 - core)):
            at = pl.multiple_of(96 * block + 48 * half, 16)
            out[48 * block : 48 * block + 48, :] = scr[pl.ds(at, 48), 0:TR]


def place(idx, mine, other, lanes, out):
    x, z, core = idx[0], idx[1], idx[2]
    for step in range(NZ):
        for k in range(NX):
            block = 4 * lax.rem(z + NZ - step, NZ) + lax.rem(x + NX - k, NX)
            for refs, half in ((mine, core), (other, 1 - core)):
                at = pl.multiple_of(96 * block + 48 * half, 16)
                out[pl.ds(at, 48), :] = refs[step][48 * k : 48 * k + 48, lanes]


def project(
    idx, normed, rim, m0, m1, m2, m3, t0, t1, t2, t3, par, hp,
    nfull, wa, ci, act, dsl, sm, sc, fp, scr, state, total,
):
    place(idx, (m0, m1, m2, m3), (t0, t1, t2, t3), slice(0, CA), wa)
    nfull[0:T, :] = normed[...]
    nfull[T:TR, :] = rim[...]

    raw = mm(nfull[0:T, :], wa[:, CC:CA]) + hp[0:1, :]
    held = iota2((T, 128), 1) < HL
    dt = jnp.where(held, jnp.maximum(raw, 0.0) + jnp.log1p(jnp.exp(-jnp.abs(raw))), 0.0)
    sm[0] = dt
    sm[2] = sigmoid(raw)
    @pl.loop(0, 4)
    def _(j):
        lanes = pl.ds(pl.multiple_of(j * 256, 256), 256)
        low = mm(nfull[...], wa[:, lanes]).astype(BF)
        ci[:, lanes] = low
        scr[RIM:TR, :] = low[0:T].astype(F32)
        scr[0:RIM, :] = low[T:TR].astype(F32)
        pre = par[4:5, lanes] + par[0:1, lanes] * scr[13 : 13 + T, :]
        for k in range(1, 4):
            pre = pre + par[k : k + 1, lanes] * scr[13 + k : 13 + k + T, :]
        s = sigmoid(pre)
        act[:, lanes] = (pre * s).astype(BF)
        dsl[:, lanes] = (s * (1.0 + pre * (1.0 - s))).astype(BF)

    e = spread_matrix(BF)
    tri = (iota2((L, L), 0) >= iota2((L, L), 1)).astype(F32)
    state[...] = jnp.zeros_like(state)
    total[...] = jnp.zeros_like(total)

    @pl.loop(0, NC, unroll=True)
    def _(c):
        rows = pl.ds(pl.multiple_of(c * L, L), L)
        dt = sm[0, rows, :]
        s = mm_high(tri, -dt * jnp.exp(hp[1:2, :]))
        sm[1, rows, :] = s
        last = s[L - 1 : L, :]
        w = spread(jnp.exp(last - s) * dt, e)
        vw = (act[rows, 0:HW].astype(F32) * w).astype(BF)
        part = mm_tn(act[rows, HW : HW + NS], vw)
        sc[c] = part
        last_e = spread(jnp.broadcast_to(last, (8, 128)), e)
        state[...] = jnp.exp(last_e[0:1]) * state[...] + part
        total[...] += last_e

    pack_state(fp, state[...], total[...])


def pack_state(fp, state, total):
    hi = total.astype(BF)
    lo = (total - hi.astype(F32)).astype(BF)
    fp[0:NS, :] = state.astype(BF)
    fp[NS : NS + 16, :] = jnp.concatenate(
        [hi.astype(F32), lo.astype(F32)], axis=0
    ).astype(BF)


def incoming(p1, p2, p3):
    t1 = p1[NS : NS + 16, :].astype(F32)
    t2 = p2[NS : NS + 16, :].astype(F32)
    t1 = t1[0:1] + t1[8:9]
    t2 = t2[0:1] + t2[8:9]
    return (
        p1[0:NS, :].astype(F32)
        + jnp.exp(t1) * p2[0:NS, :].astype(F32)
        + jnp.exp(t1 + t2) * p3[0:NS, :].astype(F32)
    )


def gates(
    idx, nfull, m0, m1, m2, m3, t0, t1, t2, t3, held, near, far, near_t, far_t, cot,
    gate, gny, wg, wo,
):
    z, core = idx[1], idx[2]
    place(idx, (m0, m1, m2, m3), (t0, t1, t2, t3), slice(CA, CA + HW), wg)
    for ref, block in ((held, z), (near, z + 3 - 2 * core), (near_t, z + 1 + 2 * core)):
        wo[pl.ds(pl.multiple_of(192 * lax.rem(block, NZ), 64), 192), :] = ref[...]
    for ref, half in ((far, core), (far_t, 1 - core)):
        at = pl.multiple_of(192 * lax.rem(z + 2, NZ) + 96 * half, 16)
        wo[pl.ds(at, 96), :] = ref[...]

    @pl.loop(0, 3)
    def _(j):
        lanes = pl.ds(pl.multiple_of(j * 256, 256), 256)
        gate[:, lanes] = mm(nfull[0:T, :], wg[:, lanes])
        gny[:, lanes] = mm_nt(cot[...], wo[lanes, :])


def within(idx, act, sm, hp, yi):
    e = spread_matrix(BF)
    skip = spread(jnp.broadcast_to(hp[2:3, :], (8, 128)), e)[0:1]
    left = iota2((L, 128), 1) < PW
    causal = iota2((L, L), 0) >= iota2((L, L), 1)

    @pl.loop(0, NC)
    def _(c):
        rows = pl.ds(pl.multiple_of(c * L, L), L)
        s = sm[1, rows, :]
        s_t = s.T
        v = act[rows, 0:HW].astype(F32)
        u = v * spread(sm[0, rows, :], e)
        scores = mm_nt(act[rows, HW + NS : CC], act[rows, HW : HW + NS])
        for j in range(HL // 2):
            parts = []
            for h in (2 * j, 2 * j + 1):
                gap = s[:, h : h + 1] - s_t[h : h + 1, :]
                parts.append((scores * jnp.exp(jnp.where(causal, gap, -1e30))).astype(BF))
            pair = u[:, 128 * j : 128 * j + 128]
            both = jnp.concatenate(
                [jnp.where(left, pair, 0.0), jnp.where(left, 0.0, pair)], axis=0
            ).astype(BF)
            yi[rows, 128 * j : 128 * j + 128] = mm(jnp.concatenate(parts, axis=1), both)
        yi[rows, :] += skip * v


def mix(idx, yi, act, sm, sc, p1, p2, p3, gate, gny, par, mixed, hin, sums, state):
    e = spread_matrix(BF)
    ones = jnp.ones((8, HW), BF)

    def rowsum(v):
        hi = v.astype(BF)
        lo = (v - hi.astype(F32)).astype(BF)
        return mm_nt(ones, hi) + mm_nt(ones, lo)

    state[...] = incoming(p1, p2, p3)

    @pl.loop(0, NC, unroll=True)
    def _(c):
        rows = pl.ds(pl.multiple_of(c * L, L), L)
        s = sm[1, rows, :]
        low = state[...].astype(BF)
        hin[c] = low
        y = yi[rows, :] + spread(jnp.exp(s), e) * mm(act[rows, HW + NS : CC], low)
        mixed[rows, :] = y
        z = gate[rows, :]
        g = y * (z * sigmoid(z))
        sq = rowsum(g * g)
        sg = rowsum(g * (gny[rows, :] * par[5:6, 0:HW]))
        sums[:, rows] = jnp.where(iota2((8, L), 0) == 0, sq, sg)
        last = spread(jnp.broadcast_to(s[L - 1 : L, :], (8, 128)), e)[0:1]
        state[...] = jnp.exp(last) * state[...] + sc[c]


def gated(
    idx, mixed, gate, gny, act, sm, s0, s1, s2, s3, wo, par,
    ny, gmix, ggate, bo, rp, small, state, total,
):
    e = spread_matrix(BF)
    gain = par[5:6, 0:HW]
    pick0 = (iota2((8, 128), 0) == 0).astype(F32)
    pick1 = (iota2((8, 128), 0) == 1).astype(F32)
    state[...] = jnp.zeros_like(state)
    total[...] = jnp.zeros_like(total)
    small[...] = jnp.zeros_like(small)

    @pl.loop(0, NC, unroll=True)
    def _(i):
        rows = pl.ds(pl.multiple_of((NC - 1 - i) * L, L), L)
        here = s0[:, rows] + s1[:, rows] + s2[:, rows] + s3[:, rows]
        sq = lax.dot_general(
            here, pick0, (((0,), (0,)), ((), ())), precision=HIGH, preferred_element_type=F32
        )
        sg = lax.dot_general(
            here, pick1, (((0,), (0,)), ((), ())), precision=HIGH, preferred_element_type=F32
        )
        r1 = lax.rsqrt(sq * (1.0 / DI) + EPS)
        pull = r1 * r1 * (sg * (1.0 / DI))
        r1 = jnp.concatenate([r1] * 6, axis=1)
        pull = jnp.concatenate([pull] * 6, axis=1)
        y = mixed[rows, :]
        z = gate[rows, :]
        sz = sigmoid(z)
        sil = z * sz
        g = y * sil
        gn = gny[rows, :]
        ghat = g * r1
        ny[rows, :] = (ghat * gain).astype(BF)
        gg = r1 * (gn * gain - g * pull)
        gm = gg * sil
        gmix[rows, :] = gm.astype(BF)
        ggate[rows, :] = (gg * y * (sz * (1.0 + z * (1.0 - sz)))).astype(BF)
        small[0:1, :] += jnp.sum(gn * ghat, axis=0, keepdims=True)
        small[1:2, :] += jnp.sum(gm * act[rows, 0:HW].astype(F32), axis=0, keepdims=True)
        s = sm[1, rows, :]
        part = mm_tn(act[rows, HW + NS : CC], (gm * spread(jnp.exp(s), e)).astype(BF))
        last_e = spread(jnp.broadcast_to(s[L - 1 : L, :], (8, 128)), e)
        state[...] = jnp.exp(last_e[0:1]) * state[...] + part
        total[...] += last_e

    pack_state(rp, state[...], total[...])

    @pl.loop(0, 6)
    def _(j):
        lanes = pl.ds(pl.multiple_of(j * 256, 256), 256)
        bo[:, lanes] = mm(ny[...], wo[:, lanes]).astype(BF)


def within_back(idx, act, gmix, sm, gu, gbc, dsi, rw):
    left = iota2((L, 128), 1) < PW
    lane = iota2((L, 128), 1)
    causal = iota2((L, L), 1) >= iota2((L, L), 0)
    rw[...] = jnp.zeros_like(rw)

    @pl.loop(0, NC)
    def _(c):
        rows = pl.ds(pl.multiple_of(c * L, L), L)
        s = sm[1, rows, :]
        s_t = s.T
        dt = sm[0, rows, :]
        b = act[rows, HW : HW + NS]
        r = act[rows, HW + NS : CC]
        scores = mm_nt(b, r)
        grad_scores = jnp.zeros((L, L), F32)
        cols = jnp.zeros((L, 128), F32)
        for j in range(HL // 2):
            v = act[rows, 128 * j : 128 * j + 128].astype(F32)
            g = gmix[rows, 128 * j : 128 * j + 128]
            gf = g.astype(F32)
            parts = []
            for i in range(2):
                h = 2 * j + i
                gap = s_t[h : h + 1, :] - s[:, h : h + 1]
                q = jnp.exp(jnp.where(causal, gap, -1e30))
                own = jnp.where(left, v, 0.0) if i == 0 else jnp.where(left, 0.0, v)
                vg = mm_nt(own.astype(BF), g) * (q * dt[:, h : h + 1])
                grad_scores = grad_scores + vg
                w = scores * vg
                rw[h : h + 1, :] = jnp.sum(w, axis=0, keepdims=True)
                cols = jnp.where(lane == h, jnp.sum(w, axis=1, keepdims=True), cols)
                parts.append((scores * q).astype(BF))
            both = jnp.concatenate(
                [jnp.where(left, gf, 0.0), jnp.where(left, 0.0, gf)], axis=0
            ).astype(BF)
            gu[rows, 128 * j : 128 * j + 128] = mm(jnp.concatenate(parts, axis=1), both)
        dsi[rows, :] = rw[...].T - cols
        low = grad_scores.astype(BF)
        gbc[rows, 0:NS] = mm(low, r)
        gbc[rows, NS : 2 * NS] = mm_tn(low, b)


def across_back(
    idx, act, gmix, sm, gu, gbc, dsi, hin, p1, p2, p3, dsl, ci, par, hp, gains, turned,
    gpa, late, out, small, gps, cis, state, sums,
):
    e = spread_matrix(BF)
    skip = spread(jnp.broadcast_to(hp[2:3, :], (8, 128)), e)[0:1]
    rate = jnp.exp(hp[1:2, :])
    upper = (iota2((L, L), 1) >= iota2((L, L), 0)).astype(F32)
    below = (iota2((L, L), 0) > iota2((L, L), 1)).astype(F32)
    held = iota2((L, 128), 1) < HL
    gps[0:RIM, :] = jnp.zeros((RIM, CC), F32)
    gps[RIM + T : RIM + T + 16, :] = jnp.zeros((16, CC), F32)
    gpa[T:TR, CC:CA] = jnp.zeros((RIM, 128), BF)
    state[...] = incoming(p1, p2, p3)
    sums[...] = jnp.zeros_like(sums)

    @pl.loop(0, NC)
    def _(i):
        c = NC - 1 - i
        rows = pl.ds(pl.multiple_of(c * L, L), L)
        b = act[rows, HW : HW + NS]
        r = act[rows, HW + NS : CC]
        old = state[...]
        low = old.astype(BF)
        s = sm[1, rows, :]
        dt = sm[0, rows, :]
        last = s[L - 1 : L, :]
        tail_e = spread(jnp.exp(last - s), e)
        dt_e = spread(dt, e)
        grow_e = spread(jnp.exp(s), e)
        last_e = jnp.exp(spread(jnp.broadcast_to(last, (8, 128)), e)[0:1])
        v = act[rows, 0:HW].astype(F32)
        g = gmix[rows, :].astype(F32)
        carried = tail_e * mm(b, low)
        grad_u = gu[rows, :] + carried
        u = v * dt_e
        grad_v = dt_e * grad_u + skip * g
        grad_b = gbc[rows, 0:NS] + mm_nt((u * tail_e).astype(BF), low)
        gs = (g * grow_e).astype(BF)
        h = hin[c]
        grad_c = gbc[rows, NS : 2 * NS] + mm_nt(gs, h)
        inter = head_sums(g * (grow_e * mm(r, h)), e)
        kept = head_sums(u * carried, e)
        grad_step = head_sums(v * grad_u, e)
        cross = jnp.sum(h.astype(F32) * old, axis=0, keepdims=True) * last_e
        cross = head_sums(jnp.broadcast_to(cross, (8, HW)), e)[0:1]
        grad_a = mm_high(upper, dsi[rows, :] + inter) + mm_high(below, kept) + cross
        grad_raw = (grad_step - rate * grad_a) * sm[2, rows, :]
        sums[0:1, :] += jnp.sum(grad_raw, axis=0, keepdims=True)
        sums[1:2, :] += jnp.sum(grad_a * dt, axis=0, keepdims=True)
        gpa[rows, CC:CA] = jnp.where(held, grad_raw, 0.0).astype(BF)
        d = dsl[rows, :].astype(F32)
        to = pl.ds(pl.multiple_of(RIM + c * L, 16), L)
        gps[to, 0:HW] = grad_v * d[:, 0:HW]
        gps[to, HW : HW + NS] = grad_b * d[:, HW : HW + NS]
        gps[to, HW + NS : CC] = grad_c * d[:, HW + NS : CC]
        state[...] = last_e * old + mm_tn(r, gs)

    @pl.loop(0, 4)
    def _(j):
        lanes = pl.ds(pl.multiple_of(j * 256, 256), 256)
        cis[RIM:TR, :] = ci[0:T, lanes].astype(F32)
        cis[0:RIM, :] = ci[T:TR, lanes].astype(F32)
        gp = gps[RIM : RIM + T, lanes]
        small[4:5, lanes] = jnp.sum(gp, axis=0, keepdims=True)
        res = par[3:4, lanes] * gps[0:TR, lanes]
        for k in range(4):
            small[k : k + 1, lanes] = jnp.sum(
                gp * cis[13 + k : 13 + k + T, :], axis=0, keepdims=True
            )
            if k < 3:
                res = res + par[k : k + 1, lanes] * gps[3 - k : 3 - k + TR, lanes]
        low = res.astype(BF)
        gpa[0:T, lanes] = low[RIM:TR]
        gpa[T:TR, lanes] = low[0:RIM]

    for j in range(0, CA, 384):
        late[:, j : j + 384] = mm(turned[...], gpa[:, j : j + 384]).astype(BF)

    out[0:3, :] = jnp.zeros((3, 512), F32)
    for k in range(5):
        for j in range(2):
            out[3 + 2 * k + j : 4 + 2 * k + j, :] = small[k : k + 1, 512 * j : 512 * j + 512]
    out[13:14, :] = gains[0:1, 0:512]
    out[14:15, 0:256] = gains[0:1, 512:768]
    out[14:15, 256:384] = head_sums(jnp.broadcast_to(gains[1:2, :], (8, HW)), e)[0:1]
    out[14:15, 384:512] = sums[0:1, :]
    out[15:16, 0:128] = -rate * sums[1:2, :]
    out[15:16, 128:512] = jnp.zeros((1, 384), F32)


def normed_back(
    idx, gpa, ggate, wa, wg, nfull, gain, block, own, part, gn, late, small, acc, gsum
):
    @pl.loop(0, 6)
    def _(j):
        lanes = pl.ds(pl.multiple_of(j * 256, 256), 256)
        acc[:, lanes] = mm_nt(gpa[...], wa[lanes, :])
        acc[0:T, lanes] += mm_nt(ggate[...], wg[lanes, :])
        gsum[:, lanes] = jnp.broadcast_to(
            jnp.sum(acc[:, lanes] * nfull[:, lanes].astype(F32), axis=0, keepdims=True)
            / gain[:, lanes],
            (8, 256),
        )

    for j in range(0, CA, 384):
        late[:, j : j + 384] = mm(own[...], gpa[:, j : j + 384]).astype(BF)
    for k in range(NX):
        rows = slice(128 * k, 128 * k + 128)
        gn[k, 0:128, :] = acc[rows, :].astype(BF)
        gn[k, 128:144, :] = acc[T:TR, :].astype(BF)
        gn[k, 144:272, :] = block[rows, :]
    small[...] = part[...]
    for j in range(3):
        small[j : j + 1, :] = gsum[0:1, 512 * j : 512 * j + 512]


def finish_out(idx, tokens, summed, out):
    out[...] = (tokens[...].astype(F32) + summed[144:272].astype(F32)).astype(BF)


def finish_back(idx, tokens, cot, summed, spill, gain, out, acc):
    v = tokens[...].astype(F32)
    root = lax.rsqrt(jnp.mean(v * v, axis=1, keepdims=True) + EPS)
    acc[...] = summed[0:128].astype(F32)
    acc[128 - RIM : 128, :] += spill[...].astype(F32)
    q = acc[...] * gain[...]
    pull = jnp.mean(q * v, axis=1, keepdims=True)
    out[...] = (cot[...].astype(F32) + root * (q - v * (root * root) * pull)).astype(BF)


def grad_early(idx, ny, cot, ggate, tm, tt, mine, other, nyt, rows, part):
    core, y = idx[2], idx[3]
    for j in range(HW // 128):
        lanes = slice(128 * j, 128 * j + 128)
        nyt[lanes, :] = ny[:, lanes].astype(F32).T.astype(BF)
    for half, which in enumerate((core, 1 - core)):
        for z in range(NZ):
            at = pl.multiple_of(192 * z + 96 * which, 16)
            row = 384 * half + 96 * z
            rows[row : row + 96, :] = nyt[pl.ds(at, 96), :]
    for q in range(4):
        k = lax.rem(q + 4 - y, 4)
        part[...] = mm(rows[...], cot[:, 384 * q : 384 * q + 384]).astype(BF)
        for half, (turned, out) in enumerate(((tm, mine), (tt, other))):
            gate = mm(turned[:, 0:T], ggate[:, 192 * q : 192 * q + 192]).astype(BF)
            out[k, :, 0:192] = gate
            for z in range(NZ):
                row = 384 * half + 96 * z
                out[k, 192 * z : 192 * z + 96, 192:384] = part[row : row + 96, 0:192]
                out[k, 192 * z + 96 : 192 * z + 192, 192:384] = part[row : row + 96, 192:384]


def add_early(idx, a, b, o0, o1, o2, o3):
    for k, out in enumerate((o0, o1, o2, o3)):
        out[...] = (a[k].astype(F32) + b[k].astype(F32)).astype(BF)


def sum_early(idx, a, b, c, d, out):
    out[...] = (
        a[...].astype(F32) + b[...].astype(F32) + (c[...].astype(F32) + d[...].astype(F32))
    ).astype(BF)


def split_z(idx, late, got, s0, s1, early, o0, o1, o3, oa, ob, o2):
    z = idx[1]
    small = wide(s0[...] + s1[...])
    for k, out in enumerate((o0, o1, o2, o3)):
        at = pl.multiple_of(lax.rem(z + k, NZ) * 192, 64)
        rows = pl.ds(at, 192)
        out[0:192, :] = (late[rows, :].astype(F32) + got[rows, :].astype(F32)).astype(BF)
        out[192:208, 0:CC] = small
        out[192:208, CC:CA] = jnp.zeros((16, CA - CC), BF)
        for j in range(3):
            rows = pl.ds(pl.multiple_of(at + 64 * j, 64), 64)
            out[208:272, 384 * j : 384 * j + 384] = early[rows, :]
    oa[...] = o2[0:HALF, :]
    ob[...] = o2[HALF:272, :]


def relay_z(idx, o1, o3, a, b, up, down):
    up[0:HALF, :] = (o1[0:HALF].astype(F32) + a[...].astype(F32)).astype(BF)
    up[HALF:272, :] = o1[HALF:272, :]
    down[0:HALF, :] = o3[0:HALF, :]
    down[HALF:272, :] = (o3[HALF:272].astype(F32) + b[...].astype(F32)).astype(BF)


def wide(v):
    hi = v.astype(BF).astype(F32)
    return jnp.concatenate([hi, v - hi], axis=1).astype(BF)


def halves(v):
    hi = v.astype(BF).astype(F32)
    return jnp.concatenate([hi, v - hi], axis=0).astype(BF)


def joined(v):
    v = v.astype(F32)
    return v[0:16] + v[16:32]


def split_y(idx, l0, l1, l2, o0, o1, o2, o3, early, scr, late):
    y = idx[3]
    total = l0[...].astype(F32) + l1[...].astype(F32) + l2[...].astype(F32)
    late[...] = total[0:192].astype(BF)
    for j in range(3):
        early[64 * j : 64 * j + 64, :] = total[208:272, 384 * j : 384 * j + 384].astype(BF)
    small = halves(total[192:208, 0:512] + total[192:208, 512:1024])
    for q in range(4):
        scr[q, :, 0:192] = late[:, 192 * q : 192 * q + 192]
        scr[q, :, 192:256] = late[:, HW + 64 * q : HW + 64 * q + 64]
        for j in range(4):
            scr[q, 32 * j : 32 * j + 32, 256:384] = small[:, 128 * j : 128 * j + 128]
        scr[q, 128:192, 256:384] = jnp.zeros((64, 128), BF)
        for j in range(4):
            scr[q, 128:176, 256 + 16 * j : 272 + 16 * j] = late[48 * j : 48 * j + 48, CC : CC + 16]
    for k, out in enumerate((o0, o1, o2, o3)):
        out[...] = scr[lax.rem(y + k, 4)]


def sum_y(idx, a, b, c, d, early, o0, o1, o2, o3, scr):
    x = idx[0]
    total = a[...].astype(F32) + b[...].astype(F32) + (c[...].astype(F32) + d[...].astype(F32))
    total = total.astype(BF)
    scr[:, 0:256] = total[:, 0:256]
    scr[:, 256:448] = early[:, 0:192]
    scr[:, 448:512] = jnp.zeros((192, 64), BF)
    for j in range(4):
        scr[48 * j : 48 * j + 48, 448:464] = total[128:176, 256 + 16 * j : 272 + 16 * j]
    small = jnp.concatenate(
        [
            sum(joined(ref[32 * j : 32 * j + 32, 256:384]) for ref in (a, b, c, d))
            for j in range(4)
        ],
        axis=1,
    )
    small = halves(small)
    for k, out in enumerate((o0, o1, o2, o3)):
        at = pl.multiple_of(lax.rem(x + k, NX) * 48, 16)
        out[0:48, :] = scr[pl.ds(at, 48), :]
        out[48:80, :] = small


def arrange_x(idx, a, b, c, d, early, out, gain, conv, ogain, heads, scr, steps):
    x = idx[0]
    shared = jnp.zeros((48, 64), F32)
    for k, ref in enumerate((a, b, c, d)):
        source = lax.rem(x + NX - k, NX)
        rows = pl.ds(pl.multiple_of(source * 48, 16), 48)
        out[rows, 0:192] = ref[0:48, 0:192]
        out[rows, 256:448] = ref[0:48, 256:448]
        shared = shared + ref[0:48, 192:256].astype(F32)
        scr[source] = joined(ref[48:80, :])
        steps[source] = ref[0:48, 448:464]
    out[:, 192:256] = jnp.zeros((192, 64), BF)
    out[0:48, 192:256] = shared.astype(BF)
    for xp in range(NX):
        out[48:96, 192 + 16 * xp : 208 + 16 * xp] = steps[xp]
    out[:, 448:640] = early[:, 192:384]
    both = scr[0] + scr[1] + (scr[2] + scr[3])
    for j in range(3):
        gain[0:1, 512 * j : 512 * j + 512] = both[j : j + 1, :]
    for k in range(5):
        conv[k : k + 1, DI : DI + 256] = both[4 + 2 * k : 5 + 2 * k, 256:512]
    heads[...] = jnp.zeros_like(heads)
    for xp in range(NX):
        own = scr[xp]
        for q in range(4):
            lane = 768 * q + 192 * xp
            for k in range(5):
                for at, size in pieces(192 * q, 192):
                    conv[k : k + 1, lane + at - 192 * q : lane + at - 192 * q + size] = own[
                        3 + 2 * k + at // 512 : 4 + 2 * k + at // 512, at % 512 : at % 512 + size
                    ]
            for at, size in pieces(192 * q, 192):
                ogain[0:1, lane + at - 192 * q : lane + at - 192 * q + size] = own[
                    13 + at // 512 : 14 + at // 512, at % 512 : at % 512 + size
                ]
            to = slice(12 * q + 3 * xp, 12 * q + 3 * xp + 3)
            heads[0:1, to] = own[14:15, 384 + 3 * q : 387 + 3 * q]
            heads[1:2, to] = own[15:16, 3 * q : 3 * q + 3]
            heads[2:3, to] = own[14:15, 256 + 3 * q : 259 + 3 * q]


def pieces(at, size):
    end = at + size
    while at < end:
        step = min(end, (at // 512 + 1) * 512) - at
        yield at, step
        at += step


def finish_weights(idx, a, b, c, d, e, f, g, h, gmain, gdt, gout, scr):
    y, core = idx[3], idx[2]
    for half in range(2):
        place = lax.rem(core + half, 2)
        for k, ref in enumerate((a, b, c, d) if half == 0 else (e, f, g, h)):
            scr[lax.rem(y + 4 - k, 4)] = ref[...]
        rows = pl.ds(pl.multiple_of(48 * place, 16), 48)
        long = pl.ds(pl.multiple_of(96 * place, 16), 96)
        for q in range(4):
            gout[long, 384 * q : 384 * q + 192] = scr[q, 0:96, 448:640].astype(F32)
            gout[long, 384 * q + 192 : 384 * q + 384] = scr[q, 96:192, 448:640].astype(F32)
            gmain[rows, 6144 + 64 * q : 6144 + 64 * q + 64] = scr[q, 0:48, 192:256].astype(F32)
            for xp in range(NX):
                lane = 768 * q + 192 * xp
                part = scr[q, 48 * xp : 48 * xp + 48, :].astype(F32)
                gmain[rows, lane : lane + 192] = part[:, 256:448]
                gmain[rows, DI + lane : DI + lane + 192] = part[:, 0:192]
        for xp in range(NX):
            part = scr[0, 48:96, 192 + 16 * xp : 208 + 16 * xp].astype(F32)
            for q in range(4):
                gdt[rows, 12 * q + 3 * xp : 12 * q + 3 * xp + 3] = part[:, 3 * q : 3 * q + 3]


def round_shift(v, axis, k, n=4):
    return lax.ppermute(v, axis, [(s, (s + k) % n) for s in range(n)])


def onward(v, k):
    return lax.ppermute(v, "z", [(s, s + k) for s in range(NZ) if 0 <= s + k < NZ])


def around(v, axis, n=4):
    return [v] + [round_shift(v, axis, k, n) for k in range(1, n)]


def spread_out(parts, axis, n=4):
    return [parts[0]] + [round_shift(parts[k], axis, k, n) for k in range(1, n)]


def after(value, *others):
    return lax.optimization_barrier((value,) + others)[0]


def after_all(values, *others):
    return list(lax.optimization_barrier(tuple(values) + others)[: len(values)])


def local(
    tokens, norm_gain, w_main, w_dt, conv_weight, conv_bias, dt_bias, a_log, skip_gain,
    out_gain, w_out, cotangent,
):
    x, z, core, y = (lax.axis_index(name) for name in ("x", "z", "core", "y"))
    idx = jnp.stack([x, z, core, y]).astype(jnp.int32)

    gain = norm_gain[None]
    rates = jnp.stack([dt_bias, a_log, skip_gain])

    call = Kernels(idx)
    both = jnp.concatenate([tokens, cotangent], axis=0)
    both = lax.all_gather(both, "x", axis=0, tiled=True)
    first = call(
        pack_main, [((48, CA + HW), BF)] * 4, [w_main, w_dt], [((NX, 48, CA + HW), BF)]
    )
    first = after_all(first)
    held = after(w_out, first[0])
    near = lax.ppermute(
        held,
        ("core", "z"),
        [(s, (s + 1) % 4) for s in range(4)] + [(4 + s, 4 + (s + 3) % 4) for s in range(4)],
    )
    far = round_shift(lax.dynamic_slice(held, (core * 96, 0), (96, D)), "z", 2)
    first = spread_out(first, "x")
    par, hp = call(
        params,
        [((8, CC), F32), ((8, 128), F32)],
        [conv_weight, conv_bias[None], out_gain[None], rates],
    )
    (rows,) = call(stack, [((192, CA + HW), BF)], first, light=True)
    w_mine = around(rows, "z")
    normed, tail, cot = call(
        norm_rows,
        [((T, D), BF), ((RIM, D), BF), ((T, D), BF)],
        [after(both, near, far), gain],
    )
    rim = onward(tail, 1)
    w_mine = after_all(w_mine, tail)
    w_other = [round_shift(v, "core", 1, 2) for v in w_mine]
    near, far = after_all([near, far], tail)
    near_t, far_t = (round_shift(v, "core", 1, 2) for v in (near, far))
    nfull, wa, ci, act, dsl, sm, sc, fp = call(
        project,
        [
            ((TR, D), BF), ((D, CA), BF), ((TR, CC), BF), ((T, CC), BF), ((T, CC), BF),
            ((3, T, 128), F32), ((NC, NS, HW), F32), ((NS + 16, HW), BF),
        ],
        [normed, rim, *w_mine, *w_other, par, hp],
        [((TR, 256), F32), ((NS, HW), F32), ((8, HW), F32)],
            )
    states = [onward(fp, k) for k in (1, 2, 3)]
    (yi,) = call(within, [((T, HW), F32)], [act, sm, hp])
    gate, gny, wg, wo = call(
        gates,
        [((T, HW), F32), ((T, HW), F32), ((D, HW), BF), ((HW, D), BF)],
        [nfull, *w_mine, *w_other, held, near, far, near_t, far_t, cot],
    )
    mixed, hin, sums = call(
        mix,
        [((T, HW), F32), ((NC, NS, HW), BF), ((8, T), F32)],
        [yi, act, sm, sc, *states, gate, gny, par],
        [((NS, HW), F32)],
    )
    nt_mine, nt_other = call(
        turn, [((HW, TR), BF), ((HW, TR), BF)], [nfull], [((D, T + 128), BF)]
    )
    ny, gmix, ggate, bo, rp, small_g = call(
        gated,
        [((T, HW), BF)] * 3 + [((T, D), BF), ((NS + 16, HW), BF), ((8, HW), F32)],
        [mixed, gate, gny, act, sm, *around(sums, "x"), wo, par],
        [((NS, HW), F32), ((8, HW), F32)],
    )
    pulls = [onward(rp, -k) for k in (1, 2, 3)]
    early, got = call(
        grad_early,
        [((4, HW, 384), BF)] * 2,
        [ny, cot, ggate, nt_mine, nt_other],
        [((HW, T), BF), ((HW, T), BF), ((HW, 384), BF)],
    )
    got = round_shift(got, "core", 1, 2)
    gu, gbc, dsi = call(
        within_back,
        [((T, HW), F32), ((T, 2 * NS), F32), ((T, 128), F32)],
        [act, gmix, sm],
        [((128, 128), F32)],
    )
    got, *pulls = after_all([got, *pulls], gu)
    early = call(add_early, [((HW, 384), BF)] * 4, [after(early, *pulls), got])
    early = spread_out(early, "y")
    gpa, late, small = call(
        across_back,
        [((TR, CA), BF), ((HW, CA), BF), ((16, 512), F32)],
        [act, gmix, sm, gu, gbc, dsi, hin, *pulls, dsl, ci, par, hp, small_g, nt_other],
        [
            ((8, CC), F32), ((T + 32, CC), F32), ((TR, 256), F32), ((NS, HW), F32),
            ((8, 128), F32),
        ],
    )
    got = round_shift(late, "core", 1, 2)
    gn, late_own, small = call(
        normed_back,
        [((NX, 272, D), BF), ((HW, CA), BF), ((16, 512), F32)],
        [gpa, ggate, wa, wg, nfull, gain, bo, nt_mine, small],
        [((TR, D), F32), ((8, D), F32)],
        light=True,
    )
    small_got = round_shift(small, "core", 1, 2)
    (early,) = call(sum_early, [((HW, 384), BF)], early)
    here, up, down, far_up, far_down = call(
        split_z,
        [((272, CA), BF)] * 3 + [((HALF, CA), BF), ((272 - HALF, CA), BF)],
        [late_own, got, small, small_got, early],
        [((272, CA), BF)],
        light=True,
    )
    far_up = round_shift(far_up, "z", 1)
    far_down = round_shift(far_down, "z", 3)
    up, down = call(relay_z, [((272, CA), BF)] * 2, [up, down, far_up, far_down], light=True)
    late = [here, round_shift(up, "z", 1), round_shift(down, "z", 3)]
    gn = lax.psum_scatter(gn, "x", scatter_dimension=0, tiled=True).reshape(272, D)
    *parts, early = call(
        split_y,
        [((192, 384), BF)] * 5,
        late,
        [((4, 192, 384), BF), ((192, CA), BF)],
        light=True,
    )
    parts = spread_out(parts, "y")
    *parts, gn = after_all([*parts, gn])
    parts = call(
        sum_y,
        [((80, 512), BF)] * 4,
        [*parts, early],
        [((192, 512), BF)],
        light=True,
    )
    parts = spread_out(parts, "x")
    gn = after(gn, parts[0])
    spill = lax.ppermute(
        gn[128:144], ("z", "x"), [(4 * s + 3, 4 * s - 1) for s in range(1, NZ)]
    )
    (block_out,) = call(finish_out, [((128, D), BF)], [tokens, gn])
    final, g_gain, g_conv, g_ogain, g_heads = call(
        arrange_x,
        [((192, 640), BF), ((1, D), F32), ((8, DI + 256), F32), ((1, DI), F32), ((8, 128), F32)],
        [*parts, early],
        [((4, 16, 512), F32), ((4, 48, 16), BF)],
    )
    finals = around(final, "y")
    (grad_tokens,) = call(
        finish_back,
        [((128, D), BF)],
        [tokens, cotangent, gn, spill, gain],
        [((128, D), F32)],
    )
    others = [round_shift(v, "core", 1, 2) for v in finals]
    g_main, g_dt, g_out = call(
        finish_weights,
        [((96, 6400), F32), ((96, 48), F32), ((192, D), F32)],
        [*finals, *others],
        [((4, 192, 640), BF)],
    )
    return (
        block_out, grad_tokens, g_gain[0], g_main, g_dt, g_conv[:4], g_conv[4],
        g_heads[0, :48], g_heads[1, :48], g_heads[2, :48], g_ogain[0], g_out,
    )


def solution(mesh):
    grid = Mesh(mesh.devices.reshape(4, 2, 4, 4), ("y", "core", "z", "x"))
    rows = P(("y", "core", "z", "x"), None)
    shard = P(("z", "x"), None)
    whole = P()
    return jax.shard_map(
        local,
        mesh=grid,
        in_specs=(
            rows, whole, shard, shard, whole, whole, whole, whole, whole, whole, shard, rows,
        ),
        out_specs=(
            rows, rows, whole, shard, shard, whole, whole, whole, whole, whole, whole, shard,
        ),
        check_vma=False,
    )
```

```python
import functools

import jax
import jax.numpy as jnp
from jax import lax
from jax.experimental import pallas as pl
from jax.experimental.pallas import tpu as pltpu
from jax.sharding import Mesh, PartitionSpec as P

EPS = 1e-05
BF = jnp.bfloat16
F32 = jnp.float32
HIGH = lax.Precision.HIGHEST
NX = 4
NZ = 4
D = 1536
HL = 12
PW = 64
HW = 768
NS = 128
L = 128
NC = 4
T = 512
LIMIT = 12
RIM = 16
TR = T + RIM
CC = 1024
HALF = 144
CA = 1152
DI = 3072


class Kernels:
    def __init__(self, idx):
        self.idx = idx

    def __call__(self, body, outs, ins, scratch=(), limit=LIMIT, light=False):
        specs = [pl.BlockSpec(memory_space=pltpu.SMEM)]
        specs += [pl.BlockSpec(memory_space=pltpu.VMEM)] * len(ins)
        got = pl.pallas_call(
            body,
            out_shape=[jax.ShapeDtypeStruct(shape, kind) for shape, kind in outs],
            in_specs=specs,
            out_specs=[pl.BlockSpec(memory_space=pltpu.VMEM)] * len(outs),
            scratch_shapes=[pltpu.VMEM(shape, kind) for shape, kind in scratch],
            compiler_params=pltpu.CompilerParams(vmem_limit_bytes=limit << 20),
            cost_estimate=pl.CostEstimate(
                flops=1 if light else 1 << 36,
                bytes_accessed=1 if light else 1 << 28,
                transcendentals=1 if light else 1 << 20,
            ),
            name=body.__name__,
        )(self.idx, *ins)
        self.idx, *got = lax.optimization_barrier((self.idx, *got))
        return got


def mm(a, b):
    return lax.dot_general(a, b, (((1,), (0,)), ((), ())), preferred_element_type=F32)


def mm_nt(a, b):
    return lax.dot_general(a, b, (((1,), (1,)), ((), ())), preferred_element_type=F32)


def mm_tn(a, b):
    return lax.dot_general(a, b, (((0,), (0,)), ((), ())), preferred_element_type=F32)


def mm_high(a, b):
    return lax.dot_general(
        a, b, (((1,), (0,)), ((), ())), precision=HIGH, preferred_element_type=F32
    )


def iota2(shape, dim):
    return lax.broadcasted_iota(jnp.int32, shape, dim)


def spread_matrix(kind):
    return (
        lax.shift_right_logical(iota2((128, HW), 1), 6) == iota2((128, HW), 0)
    ).astype(kind)


def spread(v, e):
    hi = v.astype(BF)
    rest = v - hi.astype(F32)
    mid = rest.astype(BF)
    lo = (rest - mid.astype(F32)).astype(BF)
    return mm(hi, e) + mm(mid, e) + mm(lo, e)


def head_sums(v, e):
    hi = v.astype(BF)
    lo = (v - hi.astype(F32)).astype(BF)
    return mm_nt(hi, e) + mm_nt(lo, e)


def sigmoid(v):
    return 1.0 / (1.0 + jnp.exp(-v))


def chunk(ref, c, lanes=slice(None), base=0):
    return ref[pl.ds(pl.multiple_of(base + c * L, 16), L), lanes]


def params(idx, taps, bias, gain, rates, par, hp):
    par[...] = jnp.zeros_like(par)
    hp[...] = jnp.zeros_like(hp)
    par[0:4, HW:CC] = taps[:, DI : DI + 256]
    par[4:5, HW:CC] = bias[:, DI : DI + 256]
    for xp in range(NX):

        @pl.when(idx[0] == xp)
        def _():
            for zp in range(NZ):
                at = 768 * zp + 192 * xp
                to = slice(192 * zp, 192 * zp + 192)
                par[0:4, to] = taps[:, at : at + 192]
                par[4:5, to] = bias[:, at : at + 192]
                par[5:6, to] = gain[:, at : at + 192]
                at = 12 * zp + 3 * xp
                hp[0:3, 3 * zp : 3 * zp + 3] = rates[:, at : at + 3]


def pack_main(idx, wm, wd, o0, o1, o2, o3, scr, steps):
    x, core = idx[0], idx[2]
    rows = pl.ds(pl.multiple_of(core * 48, 16), 48)
    steps[...] = jnp.zeros_like(steps)
    steps[0:48, 0:96] = wd[...].astype(F32)
    steps[...] = steps[...].T
    for xp in range(NX):
        scr[xp, :, CC:CA] = jnp.zeros((48, 128), BF)
        for zp in range(NZ):
            at = 768 * zp + 192 * xp
            to = slice(192 * zp, 192 * zp + 192)
            scr[xp, :, to] = wm[rows, DI + at : DI + at + 192]
            scr[xp, :, CA + 192 * zp : CA + 192 * zp + 192] = wm[rows, at : at + 192]
            scr[xp, :, CC + 3 * zp : CC + 3 * zp + 3] = steps[
                rows, 12 * zp + 3 * xp : 12 * zp + 3 * xp + 3
            ].astype(BF)
        scr[xp, :, HW:CC] = wm[rows, 2 * DI : 2 * DI + 256]
    for k, out in enumerate((o0, o1, o2, o3)):
        out[...] = scr[lax.rem(x + k, NX)]


def stack(idx, a, b, c, d, out, part):
    y = idx[3]
    for k, ref in enumerate((a, b, c, d)):
        out[48 * k : 48 * k + 48, :] = ref[...]
    part[...] = out[pl.ds(pl.multiple_of(48 * y, 16), 48), :]


def stack_far(idx, a, b, c, d, out):
    y = idx[3]
    for k, ref in enumerate((a, b, c, d)):
        at = pl.multiple_of(48 * lax.rem(y + 4 - k, 4), 16)
        out[pl.ds(at, 48), :] = ref[...]


def norm_rows(idx, both, gain, normed, tail, cot):
    for k in range(NX):
        v = both[256 * k : 256 * k + 128, :].astype(F32)
        root = lax.rsqrt(jnp.mean(v * v, axis=1, keepdims=True) + EPS)
        normed[128 * k : 128 * k + 128, :] = (v * root * gain[...]).astype(BF)
        cot[128 * k : 128 * k + 128, :] = both[256 * k + 128 : 256 * k + 256, :]
    tail[...] = normed[T - RIM : T, :]


def turn(idx, nfull, mine, other, scr):
    core = idx[2]
    blank = jnp.zeros((128 - RIM, 128), F32)
    for j in range(D // 128):
        lanes = slice(128 * j, 128 * j + 128)
        scr[lanes, 0:T] = nfull[0:T, lanes].astype(F32).T.astype(BF)
        edge = jnp.concatenate([nfull[T:TR, lanes].astype(F32), blank], axis=0)
        scr[lanes, T : T + 128] = edge.T.astype(BF)
    for block in range(16):
        for out, half in ((mine, core), (other, 1 - core)):
            at = pl.multiple_of(96 * block + 48 * half, 16)
            out[48 * block : 48 * block + 48, :] = scr[pl.ds(at, 48), 0:TR]


def place(idx, mine, other, lanes, out):
    x, z, core = idx[0], idx[1], idx[2]
    for step in range(NZ):
        for k in range(NX):
            block = 4 * lax.rem(z + NZ - step, NZ) + lax.rem(x + NX - k, NX)
            for refs, half in ((mine, core), (other, 1 - core)):
                at = pl.multiple_of(96 * block + 48 * half, 16)
                out[pl.ds(at, 48), :] = refs[step][48 * k : 48 * k + 48, lanes]


def project(
    idx, normed, rim, m0, m1, m2, m3, t0, t1, t2, t3, par, hp,
    nfull, wa, ci, act, dsl, sm, sc, fp, scr, state, total,
):
    place(idx, (m0, m1, m2, m3), (t0, t1, t2, t3), slice(0, CA), wa)
    nfull[0:T, :] = normed[...]
    nfull[T:TR, :] = rim[...]

    raw = mm(nfull[0:T, :], wa[:, CC:CA]) + hp[0:1, :]
    held = iota2((T, 128), 1) < HL
    dt = jnp.where(held, jnp.maximum(raw, 0.0) + jnp.log1p(jnp.exp(-jnp.abs(raw))), 0.0)
    sm[0] = dt
    sm[2] = sigmoid(raw)
    @pl.loop(0, 4)
    def _(j):
        lanes = pl.ds(pl.multiple_of(j * 256, 256), 256)
        low = mm(nfull[...], wa[:, lanes]).astype(BF)
        ci[:, lanes] = low
        scr[RIM:TR, :] = low[0:T].astype(F32)
        scr[0:RIM, :] = low[T:TR].astype(F32)
        pre = par[4:5, lanes] + par[0:1, lanes] * scr[13 : 13 + T, :]
        for k in range(1, 4):
            pre = pre + par[k : k + 1, lanes] * scr[13 + k : 13 + k + T, :]
        s = sigmoid(pre)
        act[:, lanes] = (pre * s).astype(BF)
        dsl[:, lanes] = (s * (1.0 + pre * (1.0 - s))).astype(BF)

    e = spread_matrix(BF)
    tri = (iota2((L, L), 0) >= iota2((L, L), 1)).astype(F32)
    state[...] = jnp.zeros_like(state)
    total[...] = jnp.zeros_like(total)

    @pl.loop(0, NC, unroll=True)
    def _(c):
        rows = pl.ds(pl.multiple_of(c * L, L), L)
        dt = sm[0, rows, :]
        s = mm_high(tri, -dt * jnp.exp(hp[1:2, :]))
        sm[1, rows, :] = s
        last = s[L - 1 : L, :]
        w = spread(jnp.exp(last - s) * dt, e)
        vw = (act[rows, 0:HW].astype(F32) * w).astype(BF)
        part = mm_tn(act[rows, HW : HW + NS], vw)
        sc[c] = part
        last_e = spread(jnp.broadcast_to(last, (8, 128)), e)
        state[...] = jnp.exp(last_e[0:1]) * state[...] + part
        total[...] += last_e

    pack_state(fp, state[...], total[...])


def pack_state(fp, state, total):
    hi = total.astype(BF)
    lo = (total - hi.astype(F32)).astype(BF)
    fp[0:NS, :] = state.astype(BF)
    fp[NS : NS + 16, :] = jnp.concatenate(
        [hi.astype(F32), lo.astype(F32)], axis=0
    ).astype(BF)


def incoming(p1, p2, p3):
    t1 = p1[NS : NS + 16, :].astype(F32)
    t2 = p2[NS : NS + 16, :].astype(F32)
    t1 = t1[0:1] + t1[8:9]
    t2 = t2[0:1] + t2[8:9]
    return (
        p1[0:NS, :].astype(F32)
        + jnp.exp(t1) * p2[0:NS, :].astype(F32)
        + jnp.exp(t1 + t2) * p3[0:NS, :].astype(F32)
    )


def gates(
    idx, nfull, m0, m1, m2, m3, t0, t1, t2, t3, held, near, far, near_t, far_t, cot,
    gate, gny, wg, wo,
):
    z, core = idx[1], idx[2]
    place(idx, (m0, m1, m2, m3), (t0, t1, t2, t3), slice(CA, CA + HW), wg)
    for ref, block in ((held, z), (near, z + 3 - 2 * core), (near_t, z + 1 + 2 * core)):
        wo[pl.ds(pl.multiple_of(192 * lax.rem(block, NZ), 64), 192), :] = ref[...]
    for ref, half in ((far, core), (far_t, 1 - core)):
        at = pl.multiple_of(192 * lax.rem(z + 2, NZ) + 96 * half, 16)
        wo[pl.ds(at, 96), :] = ref[...]

    @pl.loop(0, 3)
    def _(j):
        lanes = pl.ds(pl.multiple_of(j * 256, 256), 256)
        gate[:, lanes] = mm(nfull[0:T, :], wg[:, lanes])
        gny[:, lanes] = mm_nt(cot[...], wo[lanes, :])


def within(idx, act, sm, hp, yi):
    e = spread_matrix(BF)
    skip = spread(jnp.broadcast_to(hp[2:3, :], (8, 128)), e)[0:1]
    left = iota2((L, 128), 1) < PW
    causal = iota2((L, L), 0) >= iota2((L, L), 1)

    @pl.loop(0, NC)
    def _(c):
        rows = pl.ds(pl.multiple_of(c * L, L), L)
        s = sm[1, rows, :]
        s_t = s.T
        v = act[rows, 0:HW].astype(F32)
        u = v * spread(sm[0, rows, :], e)
        scores = mm_nt(act[rows, HW + NS : CC], act[rows, HW : HW + NS])
        for j in range(HL // 2):
            parts = []
            for h in (2 * j, 2 * j + 1):
                gap = s[:, h : h + 1] - s_t[h : h + 1, :]
                parts.append((scores * jnp.exp(jnp.where(causal, gap, -1e30))).astype(BF))
            pair = u[:, 128 * j : 128 * j + 128]
            both = jnp.concatenate(
                [jnp.where(left, pair, 0.0), jnp.where(left, 0.0, pair)], axis=0
            ).astype(BF)
            yi[rows, 128 * j : 128 * j + 128] = mm(jnp.concatenate(parts, axis=1), both)
        yi[rows, :] += skip * v


def mix(idx, yi, act, sm, sc, p1, p2, p3, gate, gny, par, mixed, hin, sums, state):
    e = spread_matrix(BF)
    ones = jnp.ones((8, HW), BF)

    def rowsum(v):
        hi = v.astype(BF)
        lo = (v - hi.astype(F32)).astype(BF)
        return mm_nt(ones, hi) + mm_nt(ones, lo)

    state[...] = incoming(p1, p2, p3)

    @pl.loop(0, NC, unroll=True)
    def _(c):
        rows = pl.ds(pl.multiple_of(c * L, L), L)
        s = sm[1, rows, :]
        low = state[...].astype(BF)
        hin[c] = low
        y = yi[rows, :] + spread(jnp.exp(s), e) * mm(act[rows, HW + NS : CC], low)
        mixed[rows, :] = y
        z = gate[rows, :]
        g = y * (z * sigmoid(z))
        sq = rowsum(g * g)
        sg = rowsum(g * (gny[rows, :] * par[5:6, 0:HW]))
        sums[:, rows] = jnp.where(iota2((8, L), 0) == 0, sq, sg)
        last = spread(jnp.broadcast_to(s[L - 1 : L, :], (8, 128)), e)[0:1]
        state[...] = jnp.exp(last) * state[...] + sc[c]


def gated(
    idx, mixed, gate, gny, act, sm, s0, s1, s2, s3, wo, par,
    ny, gmix, ggate, bo, rp, small, state, total,
):
    e = spread_matrix(BF)
    gain = par[5:6, 0:HW]
    pick0 = (iota2((8, 128), 0) == 0).astype(F32)
    pick1 = (iota2((8, 128), 0) == 1).astype(F32)
    state[...] = jnp.zeros_like(state)
    total[...] = jnp.zeros_like(total)
    small[...] = jnp.zeros_like(small)

    @pl.loop(0, NC, unroll=True)
    def _(i):
        rows = pl.ds(pl.multiple_of((NC - 1 - i) * L, L), L)
        here = s0[:, rows] + s1[:, rows] + s2[:, rows] + s3[:, rows]
        sq = lax.dot_general(
            here, pick0, (((0,), (0,)), ((), ())), precision=HIGH, preferred_element_type=F32
        )
        sg = lax.dot_general(
            here, pick1, (((0,), (0,)), ((), ())), precision=HIGH, preferred_element_type=F32
        )
        r1 = lax.rsqrt(sq * (1.0 / DI) + EPS)
        pull = r1 * r1 * (sg * (1.0 / DI))
        r1 = jnp.concatenate([r1] * 6, axis=1)
        pull = jnp.concatenate([pull] * 6, axis=1)
        y = mixed[rows, :]
        z = gate[rows, :]
        sz = sigmoid(z)
        sil = z * sz
        g = y * sil
        gn = gny[rows, :]
        ghat = g * r1
        ny[rows, :] = (ghat * gain).astype(BF)
        gg = r1 * (gn * gain - g * pull)
        gm = gg * sil
        gmix[rows, :] = gm.astype(BF)
        ggate[rows, :] = (gg * y * (sz * (1.0 + z * (1.0 - sz)))).astype(BF)
        small[0:1, :] += jnp.sum(gn * ghat, axis=0, keepdims=True)
        small[1:2, :] += jnp.sum(gm * act[rows, 0:HW].astype(F32), axis=0, keepdims=True)
        s = sm[1, rows, :]
        part = mm_tn(act[rows, HW + NS : CC], (gm * spread(jnp.exp(s), e)).astype(BF))
        last_e = spread(jnp.broadcast_to(s[L - 1 : L, :], (8, 128)), e)
        state[...] = jnp.exp(last_e[0:1]) * state[...] + part
        total[...] += last_e

    pack_state(rp, state[...], total[...])

    @pl.loop(0, 6)
    def _(j):
        lanes = pl.ds(pl.multiple_of(j * 256, 256), 256)
        bo[:, lanes] = mm(ny[...], wo[:, lanes]).astype(BF)


def within_back(idx, act, gmix, sm, gu, gbc, dsi, rw):
    left = iota2((L, 128), 1) < PW
    lane = iota2((L, 128), 1)
    causal = iota2((L, L), 1) >= iota2((L, L), 0)
    rw[...] = jnp.zeros_like(rw)

    @pl.loop(0, NC)
    def _(c):
        rows = pl.ds(pl.multiple_of(c * L, L), L)
        s = sm[1, rows, :]
        s_t = s.T
        dt = sm[0, rows, :]
        b = act[rows, HW : HW + NS]
        r = act[rows, HW + NS : CC]
        scores = mm_nt(b, r)
        grad_scores = jnp.zeros((L, L), F32)
        cols = jnp.zeros((L, 128), F32)
        for j in range(HL // 2):
            v = act[rows, 128 * j : 128 * j + 128].astype(F32)
            g = gmix[rows, 128 * j : 128 * j + 128]
            gf = g.astype(F32)
            parts = []
            for i in range(2):
                h = 2 * j + i
                gap = s_t[h : h + 1, :] - s[:, h : h + 1]
                q = jnp.exp(jnp.where(causal, gap, -1e30))
                own = jnp.where(left, v, 0.0) if i == 0 else jnp.where(left, 0.0, v)
                vg = mm_nt(own.astype(BF), g) * (q * dt[:, h : h + 1])
                grad_scores = grad_scores + vg
                w = scores * vg
                rw[h : h + 1, :] = jnp.sum(w, axis=0, keepdims=True)
                cols = jnp.where(lane == h, jnp.sum(w, axis=1, keepdims=True), cols)
                parts.append((scores * q).astype(BF))
            both = jnp.concatenate(
                [jnp.where(left, gf, 0.0), jnp.where(left, 0.0, gf)], axis=0
            ).astype(BF)
            gu[rows, 128 * j : 128 * j + 128] = mm(jnp.concatenate(parts, axis=1), both)
        dsi[rows, :] = rw[...].T - cols
        low = grad_scores.astype(BF)
        gbc[rows, 0:NS] = mm(low, r)
        gbc[rows, NS : 2 * NS] = mm_tn(low, b)


def across_back(
    idx, act, gmix, sm, gu, gbc, dsi, hin, p1, p2, p3, dsl, ci, par, hp, gains, turned,
    gpa, late, out, small, gps, cis, state, sums,
):
    e = spread_matrix(BF)
    skip = spread(jnp.broadcast_to(hp[2:3, :], (8, 128)), e)[0:1]
    rate = jnp.exp(hp[1:2, :])
    upper = (iota2((L, L), 1) >= iota2((L, L), 0)).astype(F32)
    below = (iota2((L, L), 0) > iota2((L, L), 1)).astype(F32)
    held = iota2((L, 128), 1) < HL
    gps[0:RIM, :] = jnp.zeros((RIM, CC), F32)
    gps[RIM + T : RIM + T + 16, :] = jnp.zeros((16, CC), F32)
    gpa[T:TR, CC:CA] = jnp.zeros((RIM, 128), BF)
    state[...] = incoming(p1, p2, p3)
    sums[...] = jnp.zeros_like(sums)

    @pl.loop(0, NC)
    def _(i):
        c = NC - 1 - i
        rows = pl.ds(pl.multiple_of(c * L, L), L)
        b = act[rows, HW : HW + NS]
        r = act[rows, HW + NS : CC]
        old = state[...]
        low = old.astype(BF)
        s = sm[1, rows, :]
        dt = sm[0, rows, :]
        last = s[L - 1 : L, :]
        tail_e = spread(jnp.exp(last - s), e)
        dt_e = spread(dt, e)
        grow_e = spread(jnp.exp(s), e)
        last_e = jnp.exp(spread(jnp.broadcast_to(last, (8, 128)), e)[0:1])
        v = act[rows, 0:HW].astype(F32)
        g = gmix[rows, :].astype(F32)
        carried = tail_e * mm(b, low)
        grad_u = gu[rows, :] + carried
        u = v * dt_e
        grad_v = dt_e * grad_u + skip * g
        grad_b = gbc[rows, 0:NS] + mm_nt((u * tail_e).astype(BF), low)
        gs = (g * grow_e).astype(BF)
        h = hin[c]
        grad_c = gbc[rows, NS : 2 * NS] + mm_nt(gs, h)
        inter = head_sums(g * (grow_e * mm(r, h)), e)
        kept = head_sums(u * carried, e)
        grad_step = head_sums(v * grad_u, e)
        cross = jnp.sum(h.astype(F32) * old, axis=0, keepdims=True) * last_e
        cross = head_sums(jnp.broadcast_to(cross, (8, HW)), e)[0:1]
        grad_a = mm_high(upper, dsi[rows, :] + inter) + mm_high(below, kept) + cross
        grad_raw = (grad_step - rate * grad_a) * sm[2, rows, :]
        sums[0:1, :] += jnp.sum(grad_raw, axis=0, keepdims=True)
        sums[1:2, :] += jnp.sum(grad_a * dt, axis=0, keepdims=True)
        gpa[rows, CC:CA] = jnp.where(held, grad_raw, 0.0).astype(BF)
        d = dsl[rows, :].astype(F32)
        to = pl.ds(pl.multiple_of(RIM + c * L, 16), L)
        gps[to, 0:HW] = grad_v * d[:, 0:HW]
        gps[to, HW : HW + NS] = grad_b * d[:, HW : HW + NS]
        gps[to, HW + NS : CC] = grad_c * d[:, HW + NS : CC]
        state[...] = last_e * old + mm_tn(r, gs)

    @pl.loop(0, 4)
    def _(j):
        lanes = pl.ds(pl.multiple_of(j * 256, 256), 256)
        cis[RIM:TR, :] = ci[0:T, lanes].astype(F32)
        cis[0:RIM, :] = ci[T:TR, lanes].astype(F32)
        gp = gps[RIM : RIM + T, lanes]
        small[4:5, lanes] = jnp.sum(gp, axis=0, keepdims=True)
        res = par[3:4, lanes] * gps[0:TR, lanes]
        for k in range(4):
            small[k : k + 1, lanes] = jnp.sum(
                gp * cis[13 + k : 13 + k + T, :], axis=0, keepdims=True
            )
            if k < 3:
                res = res + par[k : k + 1, lanes] * gps[3 - k : 3 - k + TR, lanes]
        low = res.astype(BF)
        gpa[0:T, lanes] = low[RIM:TR]
        gpa[T:TR, lanes] = low[0:RIM]

    for j in range(0, CA, 384):
        late[:, j : j + 384] = mm(turned[...], gpa[:, j : j + 384]).astype(BF)

    out[0:3, :] = jnp.zeros((3, 512), F32)
    for k in range(5):
        for j in range(2):
            out[3 + 2 * k + j : 4 + 2 * k + j, :] = small[k : k + 1, 512 * j : 512 * j + 512]
    out[13:14, :] = gains[0:1, 0:512]
    out[14:15, 0:256] = gains[0:1, 512:768]
    out[14:15, 256:384] = head_sums(jnp.broadcast_to(gains[1:2, :], (8, HW)), e)[0:1]
    out[14:15, 384:512] = sums[0:1, :]
    out[15:16, 0:128] = -rate * sums[1:2, :]
    out[15:16, 128:512] = jnp.zeros((1, 384), F32)


def normed_back(
    idx, gpa, ggate, wa, wg, nfull, gain, block, own, part, gn, late, small, acc, gsum
):
    @pl.loop(0, 6)
    def _(j):
        lanes = pl.ds(pl.multiple_of(j * 256, 256), 256)
        acc[:, lanes] = mm_nt(gpa[...], wa[lanes, :])
        acc[0:T, lanes] += mm_nt(ggate[...], wg[lanes, :])
        gsum[:, lanes] = jnp.broadcast_to(
            jnp.sum(acc[:, lanes] * nfull[:, lanes].astype(F32), axis=0, keepdims=True)
            / gain[:, lanes],
            (8, 256),
        )

    for j in range(0, CA, 384):
        late[:, j : j + 384] = mm(own[...], gpa[:, j : j + 384]).astype(BF)
    for k in range(NX):
        rows = slice(128 * k, 128 * k + 128)
        gn[k, 0:128, :] = acc[rows, :].astype(BF)
        gn[k, 128:144, :] = acc[T:TR, :].astype(BF)
        gn[k, 144:272, :] = block[rows, :]
    small[...] = part[...]
    for j in range(3):
        small[j : j + 1, :] = gsum[0:1, 512 * j : 512 * j + 512]


def finish_out(idx, tokens, summed, out):
    out[...] = (tokens[...].astype(F32) + summed[144:272].astype(F32)).astype(BF)


def finish_back(idx, tokens, cot, summed, spill, gain, out, acc):
    v = tokens[...].astype(F32)
    root = lax.rsqrt(jnp.mean(v * v, axis=1, keepdims=True) + EPS)
    acc[...] = summed[0:128].astype(F32)
    acc[128 - RIM : 128, :] += spill[...].astype(F32)
    q = acc[...] * gain[...]
    pull = jnp.mean(q * v, axis=1, keepdims=True)
    out[...] = (cot[...].astype(F32) + root * (q - v * (root * root) * pull)).astype(BF)


def grad_early(idx, ny, cot, ggate, tm, tt, mine, other, nyt, rows, part):
    core, y = idx[2], idx[3]
    for j in range(HW // 128):
        lanes = slice(128 * j, 128 * j + 128)
        nyt[lanes, :] = ny[:, lanes].astype(F32).T.astype(BF)
    for half, which in enumerate((core, 1 - core)):
        for z in range(NZ):
            at = pl.multiple_of(192 * z + 96 * which, 16)
            row = 384 * half + 96 * z
            rows[row : row + 96, :] = nyt[pl.ds(at, 96), :]
    for q in range(4):
        k = lax.rem(q + 4 - y, 4)
        part[...] = mm(rows[...], cot[:, 384 * q : 384 * q + 384]).astype(BF)
        for half, (turned, out) in enumerate(((tm, mine), (tt, other))):
            gate = mm(turned[:, 0:T], ggate[:, 192 * q : 192 * q + 192]).astype(BF)
            out[k, :, 0:192] = gate
            for z in range(NZ):
                row = 384 * half + 96 * z
                out[k, 192 * z : 192 * z + 96, 192:384] = part[row : row + 96, 0:192]
                out[k, 192 * z + 96 : 192 * z + 192, 192:384] = part[row : row + 96, 192:384]


def add_early(idx, a, b, o0, o1, o2, o3):
    for k, out in enumerate((o0, o1, o2, o3)):
        out[...] = (a[k].astype(F32) + b[k].astype(F32)).astype(BF)


def sum_early(idx, a, b, c, d, out):
    out[...] = (
        a[...].astype(F32) + b[...].astype(F32) + (c[...].astype(F32) + d[...].astype(F32))
    ).astype(BF)


def split_z(idx, late, got, s0, s1, early, o0, o1, o3, oa, ob, o2):
    z = idx[1]
    small = wide(s0[...] + s1[...])
    for k, out in enumerate((o0, o1, o2, o3)):
        at = pl.multiple_of(lax.rem(z + k, NZ) * 192, 64)
        rows = pl.ds(at, 192)
        out[0:192, :] = (late[rows, :].astype(F32) + got[rows, :].astype(F32)).astype(BF)
        out[192:208, 0:CC] = small
        out[192:208, CC:CA] = jnp.zeros((16, CA - CC), BF)
        for j in range(3):
            rows = pl.ds(pl.multiple_of(at + 64 * j, 64), 64)
            out[208:272, 384 * j : 384 * j + 384] = early[rows, :]
    oa[...] = o2[0:HALF, :]
    ob[...] = o2[HALF:272, :]


def relay_z(idx, o1, o3, a, b, up, down):
    up[0:HALF, :] = (o1[0:HALF].astype(F32) + a[...].astype(F32)).astype(BF)
    up[HALF:272, :] = o1[HALF:272, :]
    down[0:HALF, :] = o3[0:HALF, :]
    down[HALF:272, :] = (o3[HALF:272].astype(F32) + b[...].astype(F32)).astype(BF)


def wide(v):
    hi = v.astype(BF).astype(F32)
    return jnp.concatenate([hi, v - hi], axis=1).astype(BF)


def halves(v):
    hi = v.astype(BF).astype(F32)
    return jnp.concatenate([hi, v - hi], axis=0).astype(BF)


def joined(v):
    v = v.astype(F32)
    return v[0:16] + v[16:32]


def split_y(idx, l0, l1, l2, o0, o1, o2, o3, early, scr, late):
    y = idx[3]
    total = l0[...].astype(F32) + l1[...].astype(F32) + l2[...].astype(F32)
    late[...] = total[0:192].astype(BF)
    for j in range(3):
        early[64 * j : 64 * j + 64, :] = total[208:272, 384 * j : 384 * j + 384].astype(BF)
    small = halves(total[192:208, 0:512] + total[192:208, 512:1024])
    for q in range(4):
        scr[q, :, 0:192] = late[:, 192 * q : 192 * q + 192]
        scr[q, :, 192:256] = late[:, HW + 64 * q : HW + 64 * q + 64]
        for j in range(4):
            scr[q, 32 * j : 32 * j + 32, 256:384] = small[:, 128 * j : 128 * j + 128]
        scr[q, 128:192, 256:384] = jnp.zeros((64, 128), BF)
        for j in range(4):
            scr[q, 128:176, 256 + 16 * j : 272 + 16 * j] = late[48 * j : 48 * j + 48, CC : CC + 16]
    for k, out in enumerate((o0, o1, o2, o3)):
        out[...] = scr[lax.rem(y + k, 4)]


def sum_y(idx, a, b, c, d, early, o0, o1, o2, o3, scr):
    x = idx[0]
    total = a[...].astype(F32) + b[...].astype(F32) + (c[...].astype(F32) + d[...].astype(F32))
    total = total.astype(BF)
    scr[:, 0:256] = total[:, 0:256]
    scr[:, 256:448] = early[:, 0:192]
    scr[:, 448:512] = jnp.zeros((192, 64), BF)
    for j in range(4):
        scr[48 * j : 48 * j + 48, 448:464] = total[128:176, 256 + 16 * j : 272 + 16 * j]
    small = jnp.concatenate(
        [
            sum(joined(ref[32 * j : 32 * j + 32, 256:384]) for ref in (a, b, c, d))
            for j in range(4)
        ],
        axis=1,
    )
    small = halves(small)
    for k, out in enumerate((o0, o1, o2, o3)):
        at = pl.multiple_of(lax.rem(x + k, NX) * 48, 16)
        out[0:48, :] = scr[pl.ds(at, 48), :]
        out[48:80, :] = small


def arrange_x(idx, a, b, c, d, early, out, gain, conv, ogain, heads, scr, steps):
    x = idx[0]
    shared = jnp.zeros((48, 64), F32)
    for k, ref in enumerate((a, b, c, d)):
        source = lax.rem(x + NX - k, NX)
        rows = pl.ds(pl.multiple_of(source * 48, 16), 48)
        out[rows, 0:192] = ref[0:48, 0:192]
        out[rows, 256:448] = ref[0:48, 256:448]
        shared = shared + ref[0:48, 192:256].astype(F32)
        scr[source] = joined(ref[48:80, :])
        steps[source] = ref[0:48, 448:464]
    out[:, 192:256] = jnp.zeros((192, 64), BF)
    out[0:48, 192:256] = shared.astype(BF)
    for xp in range(NX):
        out[48:96, 192 + 16 * xp : 208 + 16 * xp] = steps[xp]
    out[:, 448:640] = early[:, 192:384]
    both = scr[0] + scr[1] + (scr[2] + scr[3])
    for j in range(3):
        gain[0:1, 512 * j : 512 * j + 512] = both[j : j + 1, :]
    for k in range(5):
        conv[k : k + 1, DI : DI + 256] = both[4 + 2 * k : 5 + 2 * k, 256:512]
    heads[...] = jnp.zeros_like(heads)
    for xp in range(NX):
        own = scr[xp]
        for q in range(4):
            lane = 768 * q + 192 * xp
            for k in range(5):
                for at, size in pieces(192 * q, 192):
                    conv[k : k + 1, lane + at - 192 * q : lane + at - 192 * q + size] = own[
                        3 + 2 * k + at // 512 : 4 + 2 * k + at // 512, at % 512 : at % 512 + size
                    ]
            for at, size in pieces(192 * q, 192):
                ogain[0:1, lane + at - 192 * q : lane + at - 192 * q + size] = own[
                    13 + at // 512 : 14 + at // 512, at % 512 : at % 512 + size
                ]
            to = slice(12 * q + 3 * xp, 12 * q + 3 * xp + 3)
            heads[0:1, to] = own[14:15, 384 + 3 * q : 387 + 3 * q]
            heads[1:2, to] = own[15:16, 3 * q : 3 * q + 3]
            heads[2:3, to] = own[14:15, 256 + 3 * q : 259 + 3 * q]


def pieces(at, size):
    end = at + size
    while at < end:
        step = min(end, (at // 512 + 1) * 512) - at
        yield at, step
        at += step


def finish_weights(idx, a, b, c, d, e, f, g, h, gmain, gdt, gout, scr, steps):
    y, core = idx[3], idx[2]
    steps[...] = jnp.zeros_like(steps)
    for half in range(2):
        place = lax.rem(core + half, 2)
        for k, ref in enumerate((a, b, c, d) if half == 0 else (e, f, g, h)):
            scr[lax.rem(y + 4 - k, 4)] = ref[...]
        rows = pl.ds(pl.multiple_of(48 * place, 16), 48)
        long = pl.ds(pl.multiple_of(96 * place, 16), 96)
        for q in range(4):
            gout[long, 384 * q : 384 * q + 192] = scr[q, 0:96, 448:640].astype(F32)
            gout[long, 384 * q + 192 : 384 * q + 384] = scr[q, 96:192, 448:640].astype(F32)
            gmain[rows, 6144 + 64 * q : 6144 + 64 * q + 64] = scr[q, 0:48, 192:256].astype(F32)
            for xp in range(NX):
                lane = 768 * q + 192 * xp
                part = scr[q, 48 * xp : 48 * xp + 48, :].astype(F32)
                gmain[rows, lane : lane + 192] = part[:, 256:448]
                gmain[rows, DI + lane : DI + lane + 192] = part[:, 0:192]
        for xp in range(NX):
            part = scr[0, 48:96, 192 + 16 * xp : 208 + 16 * xp].astype(F32)
            for q in range(4):
                steps[rows, 12 * q + 3 * xp : 12 * q + 3 * xp + 3] = part[:, 3 * q : 3 * q + 3]
    gdt[...] = steps[...].T[0:48, 0:96]


def round_shift(v, axis, k, n=4):
    return lax.ppermute(v, axis, [(s, (s + k) % n) for s in range(n)])


def onward(v, k):
    return lax.ppermute(v, "z", [(s, s + k) for s in range(NZ) if 0 <= s + k < NZ])


def around(v, axis, n=4):
    return [v] + [round_shift(v, axis, k, n) for k in range(1, n)]


def spread_out(parts, axis, n=4):
    return [parts[0]] + [round_shift(parts[k], axis, k, n) for k in range(1, n)]


def after(value, *others):
    return lax.optimization_barrier((value,) + others)[0]


def after_all(values, *others):
    return list(lax.optimization_barrier(tuple(values) + others)[: len(values)])


def local(
    tokens, norm_gain, w_main, w_dt, conv_weight, conv_bias, dt_bias, a_log, skip_gain,
    out_gain, w_out, cotangent,
):
    x, z, core, y = (lax.axis_index(name) for name in ("x", "z", "core", "y"))
    idx = jnp.stack([x, z, core, y]).astype(jnp.int32)

    gain = norm_gain[None]
    rates = jnp.stack([dt_bias, a_log, skip_gain])

    call = Kernels(idx)
    both = jnp.concatenate([tokens, cotangent], axis=0)
    both = lax.all_gather(both, "x", axis=0, tiled=True)
    first = call(
        pack_main, [((48, CA + HW), BF)] * 4,
        [w_main, w_dt.T],
        [((NX, 48, CA + HW), BF), ((128, 128), F32)],
    )
    first = after_all(first)
    held = after(w_out, first[0])
    near = lax.ppermute(
        held,
        ("core", "z"),
        [(s, (s + 1) % 4) for s in range(4)] + [(4 + s, 4 + (s + 3) % 4) for s in range(4)],
    )
    first = spread_out(first, "x")
    far = lax.dynamic_slice(after(held, first[1]), (core * 96, 0), (96, D))
    far = round_shift(far, "z", 2)
    par, hp = call(
        params,
        [((8, CC), F32), ((8, 128), F32)],
        [conv_weight, conv_bias[None], out_gain[None], rates],
    )
    *first, near = after_all([*first, near])
    rows, part = call(
        stack, [((192, CA + HW), BF), ((48, CA + HW), BF)], first, light=True
    )
    part = round_shift(part, "z", 2)
    behind = after(rows, part)
    up, down = round_shift(behind, "z", 1), round_shift(behind, "z", 3)
    part = around(part, "y")
    normed, tail, cot = call(
        norm_rows,
        [((T, D), BF), ((RIM, D), BF), ((T, D), BF)],
        [after(both, near, far), gain],
    )
    rim = onward(tail, 1)
    part = after_all(part, tail)
    (beyond,) = call(stack_far, [((192, CA + HW), BF)], part, light=True)
    w_mine = [rows, up, beyond, down]
    w_other = [round_shift(v, "core", 1, 2) for v in w_mine]
    near, far = after_all([near, far], tail)
    near_t, far_t = (round_shift(v, "core", 1, 2) for v in (near, far))
    nfull, wa, ci, act, dsl, sm, sc, fp = call(
        project,
        [
            ((TR, D), BF), ((D, CA), BF), ((TR, CC), BF), ((T, CC), BF), ((T, CC), BF),
            ((3, T, 128), F32), ((NC, NS, HW), F32), ((NS + 16, HW), BF),
        ],
        [normed, rim, *w_mine, *w_other, par, hp],
        [((TR, 256), F32), ((NS, HW), F32), ((8, HW), F32)],
            )
    states = [onward(fp, k) for k in (1, 2, 3)]
    (yi,) = call(within, [((T, HW), F32)], [act, sm, hp])
    gate, gny, wg, wo = call(
        gates,
        [((T, HW), F32), ((T, HW), F32), ((D, HW), BF), ((HW, D), BF)],
        [nfull, *w_mine, *w_other, held, near, far, near_t, far_t, cot],
    )
    mixed, hin, sums = call(
        mix,
        [((T, HW), F32), ((NC, NS, HW), BF), ((8, T), F32)],
        [yi, act, sm, sc, *states, gate, gny, par],
        [((NS, HW), F32)],
    )
    nt_mine, nt_other = call(
        turn, [((HW, TR), BF), ((HW, TR), BF)], [nfull], [((D, T + 128), BF)]
    )
    ny, gmix, ggate, bo, rp, small_g = call(
        gated,
        [((T, HW), BF)] * 3 + [((T, D), BF), ((NS + 16, HW), BF), ((8, HW), F32)],
        [mixed, gate, gny, act, sm, *around(sums, "x"), wo, par],
        [((NS, HW), F32), ((8, HW), F32)],
    )
    pulls = [onward(rp, -k) for k in (1, 2, 3)]
    early, got = call(
        grad_early,
        [((4, HW, 384), BF)] * 2,
        [ny, cot, ggate, nt_mine, nt_other],
        [((HW, T), BF), ((HW, T), BF), ((HW, 384), BF)],
    )
    got = round_shift(got, "core", 1, 2)
    gu, gbc, dsi = call(
        within_back,
        [((T, HW), F32), ((T, 2 * NS), F32), ((T, 128), F32)],
        [act, gmix, sm],
        [((128, 128), F32)],
    )
    got, *pulls = after_all([got, *pulls], gu)
    early = call(add_early, [((HW, 384), BF)] * 4, [after(early, *pulls), got])
    early = spread_out(early, "y")
    gpa, late, small = call(
        across_back,
        [((TR, CA), BF), ((HW, CA), BF), ((16, 512), F32)],
        [act, gmix, sm, gu, gbc, dsi, hin, *pulls, dsl, ci, par, hp, small_g, nt_other],
        [
            ((8, CC), F32), ((T + 32, CC), F32), ((TR, 256), F32), ((NS, HW), F32),
            ((8, 128), F32),
        ],
    )
    got = round_shift(late, "core", 1, 2)
    gn, late_own, small = call(
        normed_back,
        [((NX, 272, D), BF), ((HW, CA), BF), ((16, 512), F32)],
        [gpa, ggate, wa, wg, nfull, gain, bo, nt_mine, small],
        [((TR, D), F32), ((8, D), F32)],
        light=True,
    )
    small_got = round_shift(small, "core", 1, 2)
    (early,) = call(sum_early, [((HW, 384), BF)], early)
    here, up, down, far_up, far_down = call(
        split_z,
        [((272, CA), BF)] * 3 + [((HALF, CA), BF), ((272 - HALF, CA), BF)],
        [late_own, got, small, small_got, early],
        [((272, CA), BF)],
        light=True,
    )
    far_up = round_shift(far_up, "z", 1)
    far_down = round_shift(far_down, "z", 3)
    up, down = call(relay_z, [((272, CA), BF)] * 2, [up, down, far_up, far_down], light=True)
    late = [here, round_shift(up, "z", 1), round_shift(down, "z", 3)]
    gn = lax.psum_scatter(gn, "x", scatter_dimension=0, tiled=True).reshape(272, D)
    *parts, early = call(
        split_y,
        [((192, 384), BF)] * 5,
        late,
        [((4, 192, 384), BF), ((192, CA), BF)],
        light=True,
    )
    parts = spread_out(parts, "y")
    parts = call(
        sum_y,
        [((80, 512), BF)] * 4,
        [*parts, early],
        [((192, 512), BF)],
        light=True,
    )
    parts = spread_out(parts, "x")
    *parts, gn = after_all([*parts, gn])
    final, g_gain, g_conv, g_ogain, g_heads = call(
        arrange_x,
        [((192, 640), BF), ((1, D), F32), ((8, DI + 256), F32), ((1, DI), F32), ((8, 128), F32)],
        [*parts, early],
        [((4, 16, 512), F32), ((4, 48, 16), BF)],
    )
    finals = around(final, "y")
    gn = after(gn, final)
    spill = lax.ppermute(
        gn[128:144], ("z", "x"), [(4 * s + 3, 4 * s - 1) for s in range(1, NZ)]
    )
    (block_out,) = call(finish_out, [((128, D), BF)], [tokens, gn])
    small = [
        g_gain[0], g_conv[:4], g_conv[4], g_heads[0, :48], g_heads[1, :48], g_heads[2, :48],
        g_ogain[0],
    ]
    spill, *small = after_all([spill, *small])
    (grad_tokens,) = call(
        finish_back,
        [((128, D), BF)],
        [tokens, cotangent, gn, spill, gain],
        [((128, D), F32)],
    )
    others = [round_shift(v, "core", 1, 2) for v in finals]
    g_main, g_dt, g_out = call(
        finish_weights,
        [((96, 6400), F32), ((48, 96), F32), ((192, D), F32)],
        [*finals, *others],
        [((4, 192, 640), BF), ((128, 128), F32)],
    )
    return (
        block_out, grad_tokens, small[0], g_main, g_dt.T, *small[1:], g_out,
    )


def solution(mesh):
    grid = Mesh(mesh.devices.reshape(4, 2, 4, 4), ("y", "core", "z", "x"))
    rows = P(("y", "core", "z", "x"), None)
    shard = P(("z", "x"), None)
    whole = P()
    return jax.shard_map(
        local,
        mesh=grid,
        in_specs=(
            rows, whole, shard, shard, whole, whole, whole, whole, whole, whole, shard, rows,
        ),
        out_specs=(
            rows, rows, whole, shard, shard, whole, whole, whole, whole, whole, whole, shard,
        ),
        check_vma=False,
    )
```

```python
import functools

import jax
import jax.numpy as jnp
from jax import lax
from jax.experimental import pallas as pl
from jax.experimental.pallas import tpu as pltpu
from jax.sharding import Mesh, PartitionSpec as P

EPS = 1e-05
BF = jnp.bfloat16
F32 = jnp.float32
HIGH = lax.Precision.HIGHEST
NX = 4
NZ = 4
D = 1536
HL = 12
PW = 64
HW = 768
NS = 128
L = 128
NC = 4
T = 512
LIMIT = 12
RIM = 16
TR = T + RIM
CC = 1024
HALF = 144
CA = 1152
DI = 3072


class Kernels:
    def __init__(self, idx):
        self.idx = idx

    def __call__(self, body, outs, ins, scratch=(), limit=LIMIT, light=False):
        specs = [pl.BlockSpec(memory_space=pltpu.SMEM)]
        specs += [pl.BlockSpec(memory_space=pltpu.VMEM)] * len(ins)
        got = pl.pallas_call(
            body,
            out_shape=[jax.ShapeDtypeStruct(shape, kind) for shape, kind in outs],
            in_specs=specs,
            out_specs=[pl.BlockSpec(memory_space=pltpu.VMEM)] * len(outs),
            scratch_shapes=[pltpu.VMEM(shape, kind) for shape, kind in scratch],
            compiler_params=pltpu.CompilerParams(vmem_limit_bytes=limit << 20),
            cost_estimate=pl.CostEstimate(
                flops=1 if light else 1 << 36,
                bytes_accessed=1 if light else 1 << 28,
                transcendentals=1 if light else 1 << 20,
            ),
            name=body.__name__,
        )(self.idx, *ins)
        self.idx, *got = lax.optimization_barrier((self.idx, *got))
        return got


def mm(a, b):
    return lax.dot_general(a, b, (((1,), (0,)), ((), ())), preferred_element_type=F32)


def mm_nt(a, b):
    return lax.dot_general(a, b, (((1,), (1,)), ((), ())), preferred_element_type=F32)


def mm_tn(a, b):
    return lax.dot_general(a, b, (((0,), (0,)), ((), ())), preferred_element_type=F32)


def mm_high(a, b):
    return lax.dot_general(
        a, b, (((1,), (0,)), ((), ())), precision=HIGH, preferred_element_type=F32
    )


def iota2(shape, dim):
    return lax.broadcasted_iota(jnp.int32, shape, dim)


def spread_matrix(kind):
    return (
        lax.shift_right_logical(iota2((128, HW), 1), 6) == iota2((128, HW), 0)
    ).astype(kind)


def spread(v, e):
    hi = v.astype(BF)
    rest = v - hi.astype(F32)
    mid = rest.astype(BF)
    lo = (rest - mid.astype(F32)).astype(BF)
    return mm(hi, e) + mm(mid, e) + mm(lo, e)


def head_sums(v, e):
    hi = v.astype(BF)
    lo = (v - hi.astype(F32)).astype(BF)
    return mm_nt(hi, e) + mm_nt(lo, e)


def sigmoid(v):
    return 1.0 / (1.0 + jnp.exp(-v))


def chunk(ref, c, lanes=slice(None), base=0):
    return ref[pl.ds(pl.multiple_of(base + c * L, 16), L), lanes]


def params(idx, taps, bias, gain, rates, par, hp):
    par[...] = jnp.zeros_like(par)
    hp[...] = jnp.zeros_like(hp)
    par[0:4, HW:CC] = taps[:, DI : DI + 256]
    par[4:5, HW:CC] = bias[:, DI : DI + 256]
    for xp in range(NX):

        @pl.when(idx[0] == xp)
        def _():
            for zp in range(NZ):
                at = 768 * zp + 192 * xp
                to = slice(192 * zp, 192 * zp + 192)
                par[0:4, to] = taps[:, at : at + 192]
                par[4:5, to] = bias[:, at : at + 192]
                par[5:6, to] = gain[:, at : at + 192]
                at = 12 * zp + 3 * xp
                hp[0:3, 3 * zp : 3 * zp + 3] = rates[:, at : at + 3]


def pack_main(idx, wm, wd, o0, o1, o2, o3, scr, steps):
    x, core = idx[0], idx[2]
    rows = pl.ds(pl.multiple_of(core * 48, 16), 48)
    steps[...] = jnp.zeros_like(steps)
    steps[0:48, 0:96] = wd[...].astype(F32)
    steps[...] = steps[...].T
    for xp in range(NX):
        scr[xp, :, CC:CA] = jnp.zeros((48, 128), BF)
        for zp in range(NZ):
            at = 768 * zp + 192 * xp
            to = slice(192 * zp, 192 * zp + 192)
            scr[xp, :, to] = wm[rows, DI + at : DI + at + 192]
            scr[xp, :, CA + 192 * zp : CA + 192 * zp + 192] = wm[rows, at : at + 192]
            scr[xp, :, CC + 3 * zp : CC + 3 * zp + 3] = steps[
                rows, 12 * zp + 3 * xp : 12 * zp + 3 * xp + 3
            ].astype(BF)
        scr[xp, :, HW:CC] = wm[rows, 2 * DI : 2 * DI + 256]
    for k, out in enumerate((o0, o1, o2, o3)):
        out[...] = scr[lax.rem(x + k, NX)]


def stack(idx, a, b, c, d, out, part):
    y = idx[3]
    for k, ref in enumerate((a, b, c, d)):
        out[48 * k : 48 * k + 48, :] = ref[...]
    part[...] = out[pl.ds(pl.multiple_of(48 * y, 16), 48), :]


def stack_far(idx, a, b, c, d, out):
    y = idx[3]
    for k, ref in enumerate((a, b, c, d)):
        at = pl.multiple_of(48 * lax.rem(y + 4 - k, 4), 16)
        out[pl.ds(at, 48), :] = ref[...]


def norm_rows(idx, both, gain, normed, tail, cot):
    for k in range(NX):
        v = both[256 * k : 256 * k + 128, :].astype(F32)
        root = lax.rsqrt(jnp.mean(v * v, axis=1, keepdims=True) + EPS)
        normed[128 * k : 128 * k + 128, :] = (v * root * gain[...]).astype(BF)
        cot[128 * k : 128 * k + 128, :] = both[256 * k + 128 : 256 * k + 256, :]
    tail[...] = normed[T - RIM : T, :]


def turn(idx, nfull, mine, other, scr):
    core = idx[2]
    blank = jnp.zeros((128 - RIM, 128), F32)
    for j in range(D // 128):
        lanes = slice(128 * j, 128 * j + 128)
        scr[lanes, 0:T] = nfull[0:T, lanes].astype(F32).T.astype(BF)
        edge = jnp.concatenate([nfull[T:TR, lanes].astype(F32), blank], axis=0)
        scr[lanes, T : T + 128] = edge.T.astype(BF)
    for block in range(16):
        for out, half in ((mine, core), (other, 1 - core)):
            at = pl.multiple_of(96 * block + 48 * half, 16)
            out[48 * block : 48 * block + 48, :] = scr[pl.ds(at, 48), 0:TR]


def place(idx, mine, other, lanes, out):
    x, z, core = idx[0], idx[1], idx[2]
    for step in range(NZ):
        for k in range(NX):
            block = 4 * lax.rem(z + NZ - step, NZ) + lax.rem(x + NX - k, NX)
            for refs, half in ((mine, core), (other, 1 - core)):
                at = pl.multiple_of(96 * block + 48 * half, 16)
                out[pl.ds(at, 48), :] = refs[step][48 * k : 48 * k + 48, lanes]


def project(
    idx, normed, rim, m0, m1, m2, m3, t0, t1, t2, t3, par, hp,
    nfull, wa, ci, act, dsl, sm, sc, fp, scr, state, total,
):
    place(idx, (m0, m1, m2, m3), (t0, t1, t2, t3), slice(0, CA), wa)
    nfull[0:T, :] = normed[...]
    nfull[T:TR, :] = rim[...]

    raw = mm(nfull[0:T, :], wa[:, CC:CA]) + hp[0:1, :]
    held = iota2((T, 128), 1) < HL
    dt = jnp.where(held, jnp.maximum(raw, 0.0) + jnp.log1p(jnp.exp(-jnp.abs(raw))), 0.0)
    sm[0] = dt
    sm[2] = sigmoid(raw)
    @pl.loop(0, 4)
    def _(j):
        lanes = pl.ds(pl.multiple_of(j * 256, 256), 256)
        low = mm(nfull[...], wa[:, lanes]).astype(BF)
        ci[:, lanes] = low
        scr[RIM:TR, :] = low[0:T].astype(F32)
        scr[0:RIM, :] = low[T:TR].astype(F32)
        pre = par[4:5, lanes] + par[0:1, lanes] * scr[13 : 13 + T, :]
        for k in range(1, 4):
            pre = pre + par[k : k + 1, lanes] * scr[13 + k : 13 + k + T, :]
        s = sigmoid(pre)
        act[:, lanes] = (pre * s).astype(BF)
        dsl[:, lanes] = (s * (1.0 + pre * (1.0 - s))).astype(BF)

    e = spread_matrix(BF)
    tri = (iota2((L, L), 0) >= iota2((L, L), 1)).astype(F32)
    state[...] = jnp.zeros_like(state)
    total[...] = jnp.zeros_like(total)

    @pl.loop(0, NC, unroll=True)
    def _(c):
        rows = pl.ds(pl.multiple_of(c * L, L), L)
        dt = sm[0, rows, :]
        s = mm_high(tri, -dt * jnp.exp(hp[1:2, :]))
        sm[1, rows, :] = s
        last = s[L - 1 : L, :]
        w = spread(jnp.exp(last - s) * dt, e)
        vw = (act[rows, 0:HW].astype(F32) * w).astype(BF)
        part = mm_tn(act[rows, HW : HW + NS], vw)
        sc[c] = part
        last_e = spread(jnp.broadcast_to(last, (8, 128)), e)
        state[...] = jnp.exp(last_e[0:1]) * state[...] + part
        total[...] += last_e

    pack_state(fp, state[...], total[...])


def pack_state(fp, state, total):
    hi = total.astype(BF)
    lo = (total - hi.astype(F32)).astype(BF)
    fp[0:NS, :] = state.astype(BF)
    fp[NS : NS + 16, :] = jnp.concatenate(
        [hi.astype(F32), lo.astype(F32)], axis=0
    ).astype(BF)


def incoming(p1, p2, p3):
    t1 = p1[NS : NS + 16, :].astype(F32)
    t2 = p2[NS : NS + 16, :].astype(F32)
    t1 = t1[0:1] + t1[8:9]
    t2 = t2[0:1] + t2[8:9]
    return (
        p1[0:NS, :].astype(F32)
        + jnp.exp(t1) * p2[0:NS, :].astype(F32)
        + jnp.exp(t1 + t2) * p3[0:NS, :].astype(F32)
    )


def gates(
    idx, nfull, m0, m1, m2, m3, t0, t1, t2, t3, held, near, far, near_t, far_t, cot,
    gate, gny, wg, wo,
):
    z, core = idx[1], idx[2]
    place(idx, (m0, m1, m2, m3), (t0, t1, t2, t3), slice(CA, CA + HW), wg)
    for ref, block in ((held, z), (near, z + 3 - 2 * core), (near_t, z + 1 + 2 * core)):
        wo[pl.ds(pl.multiple_of(192 * lax.rem(block, NZ), 64), 192), :] = ref[...]
    for ref, half in ((far, core), (far_t, 1 - core)):
        at = pl.multiple_of(192 * lax.rem(z + 2, NZ) + 96 * half, 16)
        wo[pl.ds(at, 96), :] = ref[...]

    @pl.loop(0, 3)
    def _(j):
        lanes = pl.ds(pl.multiple_of(j * 256, 256), 256)
        gate[:, lanes] = mm(nfull[0:T, :], wg[:, lanes])
        gny[:, lanes] = mm_nt(cot[...], wo[lanes, :])


def within(idx, act, sm, hp, yi):
    e = spread_matrix(BF)
    skip = spread(jnp.broadcast_to(hp[2:3, :], (8, 128)), e)[0:1]
    left = iota2((L, 128), 1) < PW
    causal = iota2((L, L), 0) >= iota2((L, L), 1)

    @pl.loop(0, NC)
    def _(c):
        rows = pl.ds(pl.multiple_of(c * L, L), L)
        s = sm[1, rows, :]
        s_t = s.T
        v = act[rows, 0:HW].astype(F32)
        u = v * spread(sm[0, rows, :], e)
        scores = mm_nt(act[rows, HW + NS : CC], act[rows, HW : HW + NS])
        for j in range(HL // 2):
            parts = []
            for h in (2 * j, 2 * j + 1):
                gap = s[:, h : h + 1] - s_t[h : h + 1, :]
                parts.append((scores * jnp.exp(jnp.where(causal, gap, -1e30))).astype(BF))
            pair = u[:, 128 * j : 128 * j + 128]
            both = jnp.concatenate(
                [jnp.where(left, pair, 0.0), jnp.where(left, 0.0, pair)], axis=0
            ).astype(BF)
            yi[rows, 128 * j : 128 * j + 128] = mm(jnp.concatenate(parts, axis=1), both)
        yi[rows, :] += skip * v


def mix(idx, yi, act, sm, sc, p1, p2, p3, gate, gny, par, mixed, hin, sums, state):
    e = spread_matrix(BF)
    ones = jnp.ones((8, HW), BF)

    def rowsum(v):
        hi = v.astype(BF)
        lo = (v - hi.astype(F32)).astype(BF)
        return mm_nt(ones, hi) + mm_nt(ones, lo)

    state[...] = incoming(p1, p2, p3)

    @pl.loop(0, NC, unroll=True)
    def _(c):
        rows = pl.ds(pl.multiple_of(c * L, L), L)
        s = sm[1, rows, :]
        low = state[...].astype(BF)
        hin[c] = low
        y = yi[rows, :] + spread(jnp.exp(s), e) * mm(act[rows, HW + NS : CC], low)
        mixed[rows, :] = y
        z = gate[rows, :]
        g = y * (z * sigmoid(z))
        sq = rowsum(g * g)
        sg = rowsum(g * (gny[rows, :] * par[5:6, 0:HW]))
        sums[:, rows] = jnp.where(iota2((8, L), 0) == 0, sq, sg)
        last = spread(jnp.broadcast_to(s[L - 1 : L, :], (8, 128)), e)[0:1]
        state[...] = jnp.exp(last) * state[...] + sc[c]


def gated(
    idx, mixed, gate, gny, act, sm, s0, s1, s2, s3, wo, par,
    ny, gmix, ggate, bo, rp, small, state, total,
):
    e = spread_matrix(BF)
    gain = par[5:6, 0:HW]
    pick0 = (iota2((8, 128), 0) == 0).astype(F32)
    pick1 = (iota2((8, 128), 0) == 1).astype(F32)
    state[...] = jnp.zeros_like(state)
    total[...] = jnp.zeros_like(total)
    small[...] = jnp.zeros_like(small)

    @pl.loop(0, NC, unroll=True)
    def _(i):
        rows = pl.ds(pl.multiple_of((NC - 1 - i) * L, L), L)
        here = s0[:, rows] + s1[:, rows] + s2[:, rows] + s3[:, rows]
        sq = lax.dot_general(
            here, pick0, (((0,), (0,)), ((), ())), precision=HIGH, preferred_element_type=F32
        )
        sg = lax.dot_general(
            here, pick1, (((0,), (0,)), ((), ())), precision=HIGH, preferred_element_type=F32
        )
        r1 = lax.rsqrt(sq * (1.0 / DI) + EPS)
        pull = r1 * r1 * (sg * (1.0 / DI))
        r1 = jnp.concatenate([r1] * 6, axis=1)
        pull = jnp.concatenate([pull] * 6, axis=1)
        y = mixed[rows, :]
        z = gate[rows, :]
        sz = sigmoid(z)
        sil = z * sz
        g = y * sil
        gn = gny[rows, :]
        ghat = g * r1
        ny[rows, :] = (ghat * gain).astype(BF)
        gg = r1 * (gn * gain - g * pull)
        gm = gg * sil
        gmix[rows, :] = gm.astype(BF)
        ggate[rows, :] = (gg * y * (sz * (1.0 + z * (1.0 - sz)))).astype(BF)
        small[0:1, :] += jnp.sum(gn * ghat, axis=0, keepdims=True)
        small[1:2, :] += jnp.sum(gm * act[rows, 0:HW].astype(F32), axis=0, keepdims=True)
        s = sm[1, rows, :]
        part = mm_tn(act[rows, HW + NS : CC], (gm * spread(jnp.exp(s), e)).astype(BF))
        last_e = spread(jnp.broadcast_to(s[L - 1 : L, :], (8, 128)), e)
        state[...] = jnp.exp(last_e[0:1]) * state[...] + part
        total[...] += last_e

    pack_state(rp, state[...], total[...])

    @pl.loop(0, 6)
    def _(j):
        lanes = pl.ds(pl.multiple_of(j * 256, 256), 256)
        bo[:, lanes] = mm(ny[...], wo[:, lanes]).astype(BF)


def within_back(idx, act, gmix, sm, gu, gbc, dsi, rw):
    left = iota2((L, 128), 1) < PW
    lane = iota2((L, 128), 1)
    causal = iota2((L, L), 1) >= iota2((L, L), 0)
    rw[...] = jnp.zeros_like(rw)

    @pl.loop(0, NC)
    def _(c):
        rows = pl.ds(pl.multiple_of(c * L, L), L)
        s = sm[1, rows, :]
        s_t = s.T
        dt = sm[0, rows, :]
        b = act[rows, HW : HW + NS]
        r = act[rows, HW + NS : CC]
        scores = mm_nt(b, r)
        grad_scores = jnp.zeros((L, L), F32)
        cols = jnp.zeros((L, 128), F32)
        for j in range(HL // 2):
            v = act[rows, 128 * j : 128 * j + 128].astype(F32)
            g = gmix[rows, 128 * j : 128 * j + 128]
            gf = g.astype(F32)
            parts = []
            for i in range(2):
                h = 2 * j + i
                gap = s_t[h : h + 1, :] - s[:, h : h + 1]
                q = jnp.exp(jnp.where(causal, gap, -1e30))
                own = jnp.where(left, v, 0.0) if i == 0 else jnp.where(left, 0.0, v)
                vg = mm_nt(own.astype(BF), g) * (q * dt[:, h : h + 1])
                grad_scores = grad_scores + vg
                w = scores * vg
                rw[h : h + 1, :] = jnp.sum(w, axis=0, keepdims=True)
                cols = jnp.where(lane == h, jnp.sum(w, axis=1, keepdims=True), cols)
                parts.append((scores * q).astype(BF))
            both = jnp.concatenate(
                [jnp.where(left, gf, 0.0), jnp.where(left, 0.0, gf)], axis=0
            ).astype(BF)
            gu[rows, 128 * j : 128 * j + 128] = mm(jnp.concatenate(parts, axis=1), both)
        dsi[rows, :] = rw[...].T - cols
        low = grad_scores.astype(BF)
        gbc[rows, 0:NS] = mm(low, r)
        gbc[rows, NS : 2 * NS] = mm_tn(low, b)


def across_back(
    idx, act, gmix, sm, gu, gbc, dsi, hin, p1, p2, p3, dsl, ci, par, hp, gains, turned,
    gpa, late, out, small, gps, cis, state, sums,
):
    e = spread_matrix(BF)
    skip = spread(jnp.broadcast_to(hp[2:3, :], (8, 128)), e)[0:1]
    rate = jnp.exp(hp[1:2, :])
    upper = (iota2((L, L), 1) >= iota2((L, L), 0)).astype(F32)
    below = (iota2((L, L), 0) > iota2((L, L), 1)).astype(F32)
    held = iota2((L, 128), 1) < HL
    gps[0:RIM, :] = jnp.zeros((RIM, CC), F32)
    gps[RIM + T : RIM + T + 16, :] = jnp.zeros((16, CC), F32)
    gpa[T:TR, CC:CA] = jnp.zeros((RIM, 128), BF)
    state[...] = incoming(p1, p2, p3)
    sums[...] = jnp.zeros_like(sums)

    @pl.loop(0, NC)
    def _(i):
        c = NC - 1 - i
        rows = pl.ds(pl.multiple_of(c * L, L), L)
        b = act[rows, HW : HW + NS]
        r = act[rows, HW + NS : CC]
        old = state[...]
        low = old.astype(BF)
        s = sm[1, rows, :]
        dt = sm[0, rows, :]
        last = s[L - 1 : L, :]
        tail_e = spread(jnp.exp(last - s), e)
        dt_e = spread(dt, e)
        grow_e = spread(jnp.exp(s), e)
        last_e = jnp.exp(spread(jnp.broadcast_to(last, (8, 128)), e)[0:1])
        v = act[rows, 0:HW].astype(F32)
        g = gmix[rows, :].astype(F32)
        carried = tail_e * mm(b, low)
        grad_u = gu[rows, :] + carried
        u = v * dt_e
        grad_v = dt_e * grad_u + skip * g
        grad_b = gbc[rows, 0:NS] + mm_nt((u * tail_e).astype(BF), low)
        gs = (g * grow_e).astype(BF)
        h = hin[c]
        grad_c = gbc[rows, NS : 2 * NS] + mm_nt(gs, h)
        inter = head_sums(g * (grow_e * mm(r, h)), e)
        kept = head_sums(u * carried, e)
        grad_step = head_sums(v * grad_u, e)
        cross = jnp.sum(h.astype(F32) * old, axis=0, keepdims=True) * last_e
        cross = head_sums(jnp.broadcast_to(cross, (8, HW)), e)[0:1]
        grad_a = mm_high(upper, dsi[rows, :] + inter) + mm_high(below, kept) + cross
        grad_raw = (grad_step - rate * grad_a) * sm[2, rows, :]
        sums[0:1, :] += jnp.sum(grad_raw, axis=0, keepdims=True)
        sums[1:2, :] += jnp.sum(grad_a * dt, axis=0, keepdims=True)
        gpa[rows, CC:CA] = jnp.where(held, grad_raw, 0.0).astype(BF)
        d = dsl[rows, :].astype(F32)
        to = pl.ds(pl.multiple_of(RIM + c * L, 16), L)
        gps[to, 0:HW] = grad_v * d[:, 0:HW]
        gps[to, HW : HW + NS] = grad_b * d[:, HW : HW + NS]
        gps[to, HW + NS : CC] = grad_c * d[:, HW + NS : CC]
        state[...] = last_e * old + mm_tn(r, gs)

    @pl.loop(0, 4)
    def _(j):
        lanes = pl.ds(pl.multiple_of(j * 256, 256), 256)
        cis[RIM:TR, :] = ci[0:T, lanes].astype(F32)
        cis[0:RIM, :] = ci[T:TR, lanes].astype(F32)
        gp = gps[RIM : RIM + T, lanes]
        small[4:5, lanes] = jnp.sum(gp, axis=0, keepdims=True)
        res = par[3:4, lanes] * gps[0:TR, lanes]
        for k in range(4):
            small[k : k + 1, lanes] = jnp.sum(
                gp * cis[13 + k : 13 + k + T, :], axis=0, keepdims=True
            )
            if k < 3:
                res = res + par[k : k + 1, lanes] * gps[3 - k : 3 - k + TR, lanes]
        low = res.astype(BF)
        gpa[0:T, lanes] = low[RIM:TR]
        gpa[T:TR, lanes] = low[0:RIM]

    for j in range(0, CA, 384):
        late[:, j : j + 384] = mm(turned[...], gpa[:, j : j + 384]).astype(BF)

    out[0:3, :] = jnp.zeros((3, 512), F32)
    for k in range(5):
        for j in range(2):
            out[3 + 2 * k + j : 4 + 2 * k + j, :] = small[k : k + 1, 512 * j : 512 * j + 512]
    out[13:14, :] = gains[0:1, 0:512]
    out[14:15, 0:256] = gains[0:1, 512:768]
    out[14:15, 256:384] = head_sums(jnp.broadcast_to(gains[1:2, :], (8, HW)), e)[0:1]
    out[14:15, 384:512] = sums[0:1, :]
    out[15:16, 0:128] = -rate * sums[1:2, :]
    out[15:16, 128:512] = jnp.zeros((1, 384), F32)


def normed_back(
    idx, gpa, ggate, wa, wg, nfull, gain, block, own, part, gn, late, small, acc, gsum
):
    @pl.loop(0, 6)
    def _(j):
        lanes = pl.ds(pl.multiple_of(j * 256, 256), 256)
        acc[:, lanes] = mm_nt(gpa[...], wa[lanes, :])
        acc[0:T, lanes] += mm_nt(ggate[...], wg[lanes, :])
        gsum[:, lanes] = jnp.broadcast_to(
            jnp.sum(acc[:, lanes] * nfull[:, lanes].astype(F32), axis=0, keepdims=True)
            / gain[:, lanes],
            (8, 256),
        )

    for j in range(0, CA, 384):
        late[:, j : j + 384] = mm(own[...], gpa[:, j : j + 384]).astype(BF)
    for k in range(NX):
        rows = slice(128 * k, 128 * k + 128)
        gn[k, 0:128, :] = acc[rows, :].astype(BF)
        gn[k, 128:144, :] = acc[T:TR, :].astype(BF)
        gn[k, 144:272, :] = block[rows, :]
    small[...] = part[...]
    for j in range(3):
        small[j : j + 1, :] = gsum[0:1, 512 * j : 512 * j + 512]


def finish_out(idx, tokens, summed, out):
    out[...] = (tokens[...].astype(F32) + summed[144:272].astype(F32)).astype(BF)


def finish_back(idx, tokens, cot, summed, spill, gain, out, acc):
    v = tokens[...].astype(F32)
    root = lax.rsqrt(jnp.mean(v * v, axis=1, keepdims=True) + EPS)
    acc[...] = summed[0:128].astype(F32)
    acc[128 - RIM : 128, :] += spill[...].astype(F32)
    q = acc[...] * gain[...]
    pull = jnp.mean(q * v, axis=1, keepdims=True)
    out[...] = (cot[...].astype(F32) + root * (q - v * (root * root) * pull)).astype(BF)


def grad_early(idx, ny, cot, ggate, tm, tt, mine, other, nyt, rows, part):
    core, y = idx[2], idx[3]
    for j in range(HW // 128):
        lanes = slice(128 * j, 128 * j + 128)
        nyt[lanes, :] = ny[:, lanes].astype(F32).T.astype(BF)
    for half, which in enumerate((core, 1 - core)):
        for z in range(NZ):
            at = pl.multiple_of(192 * z + 96 * which, 16)
            row = 384 * half + 96 * z
            rows[row : row + 96, :] = nyt[pl.ds(at, 96), :]
    for q in range(4):
        k = lax.rem(q + 4 - y, 4)
        part[...] = mm(rows[...], cot[:, 384 * q : 384 * q + 384]).astype(BF)
        for half, (turned, out) in enumerate(((tm, mine), (tt, other))):
            gate = mm(turned[:, 0:T], ggate[:, 192 * q : 192 * q + 192]).astype(BF)
            out[k, :, 0:192] = gate
            for z in range(NZ):
                row = 384 * half + 96 * z
                out[k, 192 * z : 192 * z + 96, 192:384] = part[row : row + 96, 0:192]
                out[k, 192 * z + 96 : 192 * z + 192, 192:384] = part[row : row + 96, 192:384]


def add_early(idx, a, b, o0, o1, o2, o3):
    for k, out in enumerate((o0, o1, o2, o3)):
        out[...] = a[k] + b[k]


def sum_early(idx, a, b, c, d, out):
    out[...] = (
        a[...].astype(F32) + b[...].astype(F32) + (c[...].astype(F32) + d[...].astype(F32))
    ).astype(BF)


def split_z(idx, late, got, s0, s1, early, o0, o1, o3, oa, ob, o2):
    z = idx[1]
    small = wide(s0[...] + s1[...])
    for k, out in enumerate((o0, o1, o2, o3)):
        at = pl.multiple_of(lax.rem(z + k, NZ) * 192, 64)
        rows = pl.ds(at, 192)
        out[0:192, :] = late[rows, :] + got[rows, :]
        out[192:208, 0:CC] = small
        out[192:208, CC:CA] = jnp.zeros((16, CA - CC), BF)
        for j in range(3):
            rows = pl.ds(pl.multiple_of(at + 64 * j, 64), 64)
            out[208:272, 384 * j : 384 * j + 384] = early[rows, :]
    oa[...] = o2[0:HALF, :]
    ob[...] = o2[HALF:272, :]


def relay_z(idx, o1, o3, a, b, up, down):
    up[0:HALF, :] = o1[0:HALF, :] + a[...]
    up[HALF:272, :] = o1[HALF:272, :]
    down[0:HALF, :] = o3[0:HALF, :]
    down[HALF:272, :] = o3[HALF:272, :] + b[...]


def wide(v):
    hi = v.astype(BF).astype(F32)
    return jnp.concatenate([hi, v - hi], axis=1).astype(BF)


def halves(v):
    hi = v.astype(BF).astype(F32)
    return jnp.concatenate([hi, v - hi], axis=0).astype(BF)


def joined(v):
    v = v.astype(F32)
    return v[0:16] + v[16:32]


def split_y(idx, l0, l1, l2, o0, o1, o2, o3, early, scr, late):
    y = idx[3]
    total = l0[...].astype(F32) + l1[...].astype(F32) + l2[...].astype(F32)
    late[...] = total[0:192].astype(BF)
    for j in range(3):
        early[64 * j : 64 * j + 64, :] = total[208:272, 384 * j : 384 * j + 384].astype(BF)
    small = halves(total[192:208, 0:512] + total[192:208, 512:1024])
    for q in range(4):
        scr[q, :, 0:192] = late[:, 192 * q : 192 * q + 192]
        scr[q, :, 192:256] = late[:, HW + 64 * q : HW + 64 * q + 64]
        for j in range(4):
            scr[q, 32 * j : 32 * j + 32, 256:384] = small[:, 128 * j : 128 * j + 128]
        scr[q, 128:192, 256:384] = jnp.zeros((64, 128), BF)
        for j in range(4):
            scr[q, 128:176, 256 + 16 * j : 272 + 16 * j] = late[48 * j : 48 * j + 48, CC : CC + 16]
    for k, out in enumerate((o0, o1, o2, o3)):
        out[...] = scr[lax.rem(y + k, 4)]


def sum_y(idx, a, b, c, d, early, o0, o1, o2, o3, scr):
    x = idx[0]
    total = a[...].astype(F32) + b[...].astype(F32) + (c[...].astype(F32) + d[...].astype(F32))
    total = total.astype(BF)
    scr[:, 0:256] = total[:, 0:256]
    scr[:, 256:448] = early[:, 0:192]
    scr[:, 448:512] = jnp.zeros((192, 64), BF)
    for j in range(4):
        scr[48 * j : 48 * j + 48, 448:464] = total[128:176, 256 + 16 * j : 272 + 16 * j]
    small = jnp.concatenate(
        [
            sum(joined(ref[32 * j : 32 * j + 32, 256:384]) for ref in (a, b, c, d))
            for j in range(4)
        ],
        axis=1,
    )
    small = halves(small)
    for k, out in enumerate((o0, o1, o2, o3)):
        at = pl.multiple_of(lax.rem(x + k, NX) * 48, 16)
        out[0:48, :] = scr[pl.ds(at, 48), :]
        out[48:80, :] = small


def arrange_x(idx, a, b, c, d, early, out, gain, conv, ogain, heads, scr, steps):
    x = idx[0]
    shared = jnp.zeros((48, 64), F32)
    for k, ref in enumerate((a, b, c, d)):
        source = lax.rem(x + NX - k, NX)
        rows = pl.ds(pl.multiple_of(source * 48, 16), 48)
        out[rows, 0:192] = ref[0:48, 0:192]
        out[rows, 256:448] = ref[0:48, 256:448]
        shared = shared + ref[0:48, 192:256].astype(F32)
        scr[source] = joined(ref[48:80, :])
        steps[source] = ref[0:48, 448:464]
    out[:, 192:256] = jnp.zeros((192, 64), BF)
    out[0:48, 192:256] = shared.astype(BF)
    for xp in range(NX):
        out[48:96, 192 + 16 * xp : 208 + 16 * xp] = steps[xp]
    out[:, 448:640] = early[:, 192:384]
    both = scr[0] + scr[1] + (scr[2] + scr[3])
    for j in range(3):
        gain[0:1, 512 * j : 512 * j + 512] = both[j : j + 1, :]
    for k in range(5):
        conv[k : k + 1, DI : DI + 256] = both[4 + 2 * k : 5 + 2 * k, 256:512]
    heads[...] = jnp.zeros_like(heads)
    for xp in range(NX):
        own = scr[xp]
        for q in range(4):
            lane = 768 * q + 192 * xp
            for k in range(5):
                for at, size in pieces(192 * q, 192):
                    conv[k : k + 1, lane + at - 192 * q : lane + at - 192 * q + size] = own[
                        3 + 2 * k + at // 512 : 4 + 2 * k + at // 512, at % 512 : at % 512 + size
                    ]
            for at, size in pieces(192 * q, 192):
                ogain[0:1, lane + at - 192 * q : lane + at - 192 * q + size] = own[
                    13 + at // 512 : 14 + at // 512, at % 512 : at % 512 + size
                ]
            to = slice(12 * q + 3 * xp, 12 * q + 3 * xp + 3)
            heads[0:1, to] = own[14:15, 384 + 3 * q : 387 + 3 * q]
            heads[1:2, to] = own[15:16, 3 * q : 3 * q + 3]
            heads[2:3, to] = own[14:15, 256 + 3 * q : 259 + 3 * q]


def pieces(at, size):
    end = at + size
    while at < end:
        step = min(end, (at // 512 + 1) * 512) - at
        yield at, step
        at += step


def finish_weights(idx, a, b, c, d, e, f, g, h, gmain, gdt, gout, scr, steps):
    y, core = idx[3], idx[2]
    steps[...] = jnp.zeros_like(steps)
    for half in range(2):
        place = lax.rem(core + half, 2)
        for k, ref in enumerate((a, b, c, d) if half == 0 else (e, f, g, h)):
            scr[lax.rem(y + 4 - k, 4)] = ref[...]
        rows = pl.ds(pl.multiple_of(48 * place, 16), 48)
        long = pl.ds(pl.multiple_of(96 * place, 16), 96)
        for q in range(4):
            gout[long, 384 * q : 384 * q + 192] = scr[q, 0:96, 448:640].astype(F32)
            gout[long, 384 * q + 192 : 384 * q + 384] = scr[q, 96:192, 448:640].astype(F32)
            gmain[rows, 6144 + 64 * q : 6144 + 64 * q + 64] = scr[q, 0:48, 192:256].astype(F32)
            for xp in range(NX):
                lane = 768 * q + 192 * xp
                part = scr[q, 48 * xp : 48 * xp + 48, :].astype(F32)
                gmain[rows, lane : lane + 192] = part[:, 256:448]
                gmain[rows, DI + lane : DI + lane + 192] = part[:, 0:192]
        for xp in range(NX):
            part = scr[0, 48:96, 192 + 16 * xp : 208 + 16 * xp].astype(F32)
            for q in range(4):
                steps[rows, 12 * q + 3 * xp : 12 * q + 3 * xp + 3] = part[:, 3 * q : 3 * q + 3]
    gdt[...] = steps[...].T[0:48, 0:96]


def round_shift(v, axis, k, n=4):
    return lax.ppermute(v, axis, [(s, (s + k) % n) for s in range(n)])


def onward(v, k):
    return lax.ppermute(v, "z", [(s, s + k) for s in range(NZ) if 0 <= s + k < NZ])


def around(v, axis, n=4):
    return [v] + [round_shift(v, axis, k, n) for k in range(1, n)]


def spread_out(parts, axis, n=4):
    return [parts[0]] + [round_shift(parts[k], axis, k, n) for k in range(1, n)]


def after(value, *others):
    return lax.optimization_barrier((value,) + others)[0]


def after_all(values, *others):
    return list(lax.optimization_barrier(tuple(values) + others)[: len(values)])


def local(
    tokens, norm_gain, w_main, w_dt, conv_weight, conv_bias, dt_bias, a_log, skip_gain,
    out_gain, w_out, cotangent,
):
    x, z, core, y = (lax.axis_index(name) for name in ("x", "z", "core", "y"))
    idx = jnp.stack([x, z, core, y]).astype(jnp.int32)

    gain = norm_gain[None]
    rates = jnp.stack([dt_bias, a_log, skip_gain])

    call = Kernels(idx)
    both = jnp.concatenate([tokens, cotangent], axis=0)
    both = lax.all_gather(both, "x", axis=0, tiled=True)
    first = call(
        pack_main, [((48, CA + HW), BF)] * 4,
        [w_main, w_dt.T],
        [((NX, 48, CA + HW), BF), ((128, 128), F32)],
    )
    first = after_all(first)
    held = after(w_out, first[0])
    near = lax.ppermute(
        held,
        ("core", "z"),
        [(s, (s + 1) % 4) for s in range(4)] + [(4 + s, 4 + (s + 3) % 4) for s in range(4)],
    )
    first = spread_out(first, "x")
    far = lax.dynamic_slice(after(held, first[1]), (core * 96, 0), (96, D))
    far = round_shift(far, "z", 2)
    par, hp = call(
        params,
        [((8, CC), F32), ((8, 128), F32)],
        [conv_weight, conv_bias[None], out_gain[None], rates],
    )
    *first, near = after_all([*first, near])
    rows, part = call(
        stack, [((192, CA + HW), BF), ((48, CA + HW), BF)], first, light=True
    )
    part = round_shift(part, "z", 2)
    behind = after(rows, part)
    up, down = round_shift(behind, "z", 1), round_shift(behind, "z", 3)
    part = around(part, "y")
    normed, tail, cot = call(
        norm_rows,
        [((T, D), BF), ((RIM, D), BF), ((T, D), BF)],
        [after(both, near, far), gain],
    )
    rim = onward(tail, 1)
    part = after_all(part, tail)
    (beyond,) = call(stack_far, [((192, CA + HW), BF)], part, light=True)
    w_mine = [rows, up, beyond, down]
    w_other = [round_shift(v, "core", 1, 2) for v in w_mine]
    near, far = after_all([near, far], tail)
    near_t, far_t = (round_shift(v, "core", 1, 2) for v in (near, far))
    nfull, wa, ci, act, dsl, sm, sc, fp = call(
        project,
        [
            ((TR, D), BF), ((D, CA), BF), ((TR, CC), BF), ((T, CC), BF), ((T, CC), BF),
            ((3, T, 128), F32), ((NC, NS, HW), F32), ((NS + 16, HW), BF),
        ],
        [normed, rim, *w_mine, *w_other, par, hp],
        [((TR, 256), F32), ((NS, HW), F32), ((8, HW), F32)],
            )
    states = [onward(fp, k) for k in (1, 2, 3)]
    (yi,) = call(within, [((T, HW), F32)], [act, sm, hp])
    gate, gny, wg, wo = call(
        gates,
        [((T, HW), F32), ((T, HW), F32), ((D, HW), BF), ((HW, D), BF)],
        [nfull, *w_mine, *w_other, held, near, far, near_t, far_t, cot],
    )
    mixed, hin, sums = call(
        mix,
        [((T, HW), F32), ((NC, NS, HW), BF), ((8, T), F32)],
        [yi, act, sm, sc, *states, gate, gny, par],
        [((NS, HW), F32)],
    )
    nt_mine, nt_other = call(
        turn, [((HW, TR), BF), ((HW, TR), BF)], [nfull], [((D, T + 128), BF)]
    )
    ny, gmix, ggate, bo, rp, small_g = call(
        gated,
        [((T, HW), BF)] * 3 + [((T, D), BF), ((NS + 16, HW), BF), ((8, HW), F32)],
        [mixed, gate, gny, act, sm, *around(sums, "x"), wo, par],
        [((NS, HW), F32), ((8, HW), F32)],
    )
    pulls = [onward(rp, -k) for k in (1, 2, 3)]
    early, got = call(
        grad_early,
        [((4, HW, 384), BF)] * 2,
        [ny, cot, ggate, nt_mine, nt_other],
        [((HW, T), BF), ((HW, T), BF), ((HW, 384), BF)],
    )
    got = round_shift(got, "core", 1, 2)
    gu, gbc, dsi = call(
        within_back,
        [((T, HW), F32), ((T, 2 * NS), F32), ((T, 128), F32)],
        [act, gmix, sm],
        [((128, 128), F32)],
    )
    got, *pulls = after_all([got, *pulls], gu)
    early = call(add_early, [((HW, 384), BF)] * 4, [after(early, *pulls), got])
    early = spread_out(early, "y")
    gpa, late, small = call(
        across_back,
        [((TR, CA), BF), ((HW, CA), BF), ((16, 512), F32)],
        [act, gmix, sm, gu, gbc, dsi, hin, *pulls, dsl, ci, par, hp, small_g, nt_other],
        [
            ((8, CC), F32), ((T + 32, CC), F32), ((TR, 256), F32), ((NS, HW), F32),
            ((8, 128), F32),
        ],
    )
    got = round_shift(late, "core", 1, 2)
    gn, late_own, small = call(
        normed_back,
        [((NX, 272, D), BF), ((HW, CA), BF), ((16, 512), F32)],
        [gpa, ggate, wa, wg, nfull, gain, bo, nt_mine, small],
        [((TR, D), F32), ((8, D), F32)],
        light=True,
    )
    small_got = round_shift(small, "core", 1, 2)
    (early,) = call(sum_early, [((HW, 384), BF)], early)
    here, up, down, far_up, far_down = call(
        split_z,
        [((272, CA), BF)] * 3 + [((HALF, CA), BF), ((272 - HALF, CA), BF)],
        [late_own, got, small, small_got, early],
        [((272, CA), BF)],
        light=True,
    )
    far_up = round_shift(far_up, "z", 1)
    far_down = round_shift(far_down, "z", 3)
    up, down = call(relay_z, [((272, CA), BF)] * 2, [up, down, far_up, far_down], light=True)
    late = [here, round_shift(up, "z", 1), round_shift(down, "z", 3)]
    gn = lax.psum_scatter(gn, "x", scatter_dimension=0, tiled=True).reshape(272, D)
    *parts, early = call(
        split_y,
        [((192, 384), BF)] * 5,
        late,
        [((4, 192, 384), BF), ((192, CA), BF)],
        light=True,
    )
    parts = spread_out(parts, "y")
    parts = call(
        sum_y,
        [((80, 512), BF)] * 4,
        [*parts, early],
        [((192, 512), BF)],
        light=True,
    )
    parts = spread_out(parts, "x")
    *parts, gn = after_all([*parts, gn])
    final, g_gain, g_conv, g_ogain, g_heads = call(
        arrange_x,
        [((192, 640), BF), ((1, D), F32), ((8, DI + 256), F32), ((1, DI), F32), ((8, 128), F32)],
        [*parts, early],
        [((4, 16, 512), F32), ((4, 48, 16), BF)],
    )
    finals = around(final, "y")
    gn = after(gn, final)
    spill = lax.ppermute(
        gn[128:144], ("z", "x"), [(4 * s + 3, 4 * s - 1) for s in range(1, NZ)]
    )
    (block_out,) = call(finish_out, [((128, D), BF)], [tokens, gn])
    small = [
        g_gain[0], g_conv[:4], g_conv[4], g_heads[0, :48], g_heads[1, :48], g_heads[2, :48],
        g_ogain[0],
    ]
    spill, *small = after_all([spill, *small])
    (grad_tokens,) = call(
        finish_back,
        [((128, D), BF)],
        [tokens, cotangent, gn, spill, gain],
        [((128, D), F32)],
    )
    others = [round_shift(v, "core", 1, 2) for v in finals]
    g_main, g_dt, g_out = call(
        finish_weights,
        [((96, 6400), F32), ((48, 96), F32), ((192, D), F32)],
        [*finals, *others],
        [((4, 192, 640), BF), ((128, 128), F32)],
    )
    return (
        block_out, grad_tokens, small[0], g_main, g_dt.T, *small[1:], g_out,
    )


def solution(mesh):
    grid = Mesh(mesh.devices.reshape(4, 2, 4, 4), ("y", "core", "z", "x"))
    rows = P(("y", "core", "z", "x"), None)
    shard = P(("z", "x"), None)
    whole = P()
    return jax.shard_map(
        local,
        mesh=grid,
        in_specs=(
            rows, whole, shard, shard, whole, whole, whole, whole, whole, whole, shard, rows,
        ),
        out_specs=(
            rows, rows, whole, shard, shard, whole, whole, whole, whole, whole, whole, shard,
        ),
        check_vma=False,
    )
```

```python
import functools

import jax
import jax.numpy as jnp
from jax import lax
from jax.experimental import pallas as pl
from jax.experimental.pallas import tpu as pltpu
from jax.sharding import Mesh, PartitionSpec as P

EPS = 1e-05
BF = jnp.bfloat16
F32 = jnp.float32
HIGH = lax.Precision.HIGHEST
NX = 4
NZ = 4
D = 1536
HL = 12
PW = 64
HW = 768
NS = 128
L = 128
NC = 4
T = 512
LIMIT = 12
RIM = 16
TR = T + RIM
CC = 1024
HALF = 144
CA = 1152
DI = 3072


class Kernels:
    def __init__(self, idx):
        self.idx = idx

    def __call__(self, body, outs, ins, scratch=(), limit=LIMIT, light=False):
        specs = [pl.BlockSpec(memory_space=pltpu.SMEM)]
        specs += [pl.BlockSpec(memory_space=pltpu.VMEM)] * len(ins)
        got = pl.pallas_call(
            body,
            out_shape=[jax.ShapeDtypeStruct(shape, kind) for shape, kind in outs],
            in_specs=specs,
            out_specs=[pl.BlockSpec(memory_space=pltpu.VMEM)] * len(outs),
            scratch_shapes=[pltpu.VMEM(shape, kind) for shape, kind in scratch],
            compiler_params=pltpu.CompilerParams(vmem_limit_bytes=limit << 20),
            cost_estimate=pl.CostEstimate(
                flops=1 if light else 1 << 36,
                bytes_accessed=1 if light else 1 << 28,
                transcendentals=1 if light else 1 << 20,
            ),
            name=body.__name__,
        )(self.idx, *ins)
        self.idx, *got = lax.optimization_barrier((self.idx, *got))
        return got


def mm(a, b):
    return lax.dot_general(a, b, (((1,), (0,)), ((), ())), preferred_element_type=F32)


def mm_nt(a, b):
    return lax.dot_general(a, b, (((1,), (1,)), ((), ())), preferred_element_type=F32)


def mm_tn(a, b):
    return lax.dot_general(a, b, (((0,), (0,)), ((), ())), preferred_element_type=F32)


def mm_high(a, b):
    return lax.dot_general(
        a, b, (((1,), (0,)), ((), ())), precision=HIGH, preferred_element_type=F32
    )


def iota2(shape, dim):
    return lax.broadcasted_iota(jnp.int32, shape, dim)


def spread_matrix(kind):
    return (
        lax.shift_right_logical(iota2((128, HW), 1), 6) == iota2((128, HW), 0)
    ).astype(kind)


def spread(v, e):
    hi = v.astype(BF)
    rest = v - hi.astype(F32)
    mid = rest.astype(BF)
    lo = (rest - mid.astype(F32)).astype(BF)
    return mm(hi, e) + mm(mid, e) + mm(lo, e)


def head_sums(v, e):
    hi = v.astype(BF)
    lo = (v - hi.astype(F32)).astype(BF)
    return mm_nt(hi, e) + mm_nt(lo, e)


def sigmoid(v):
    return 1.0 / (1.0 + jnp.exp(-v))


def chunk(ref, c, lanes=slice(None), base=0):
    return ref[pl.ds(pl.multiple_of(base + c * L, 16), L), lanes]


def params(idx, taps, bias, gain, rates, par, hp):
    par[...] = jnp.zeros_like(par)
    hp[...] = jnp.zeros_like(hp)
    par[0:4, HW:CC] = taps[:, DI : DI + 256]
    par[4:5, HW:CC] = bias[:, DI : DI + 256]
    for xp in range(NX):

        @pl.when(idx[0] == xp)
        def _():
            for zp in range(NZ):
                at = 768 * zp + 192 * xp
                to = slice(192 * zp, 192 * zp + 192)
                par[0:4, to] = taps[:, at : at + 192]
                par[4:5, to] = bias[:, at : at + 192]
                par[5:6, to] = gain[:, at : at + 192]
                at = 12 * zp + 3 * xp
                hp[0:3, 3 * zp : 3 * zp + 3] = rates[:, at : at + 3]


def pack_main(idx, wm, wd, o0, o1, o2, o3, scr, steps):
    x, core = idx[0], idx[2]
    rows = pl.ds(pl.multiple_of(core * 48, 16), 48)
    steps[...] = jnp.zeros_like(steps)
    steps[0:48, 0:96] = wd[...].astype(F32)
    steps[...] = steps[...].T
    for xp in range(NX):
        scr[xp, :, CC:CA] = jnp.zeros((48, 128), BF)
        for zp in range(NZ):
            at = 768 * zp + 192 * xp
            to = slice(192 * zp, 192 * zp + 192)
            scr[xp, :, to] = wm[rows, DI + at : DI + at + 192]
            scr[xp, :, CA + 192 * zp : CA + 192 * zp + 192] = wm[rows, at : at + 192]
            scr[xp, :, CC + 3 * zp : CC + 3 * zp + 3] = steps[
                rows, 12 * zp + 3 * xp : 12 * zp + 3 * xp + 3
            ].astype(BF)
        scr[xp, :, HW:CC] = wm[rows, 2 * DI : 2 * DI + 256]
    for k, out in enumerate((o0, o1, o2, o3)):
        out[...] = scr[lax.rem(x + k, NX)]


def stack(idx, a, b, c, d, out, part):
    y = idx[3]
    for k, ref in enumerate((a, b, c, d)):
        out[48 * k : 48 * k + 48, :] = ref[...]
    part[...] = out[pl.ds(pl.multiple_of(48 * y, 16), 48), :]


def stack_far(idx, a, b, c, d, out):
    y = idx[3]
    for k, ref in enumerate((a, b, c, d)):
        at = pl.multiple_of(48 * lax.rem(y + 4 - k, 4), 16)
        out[pl.ds(at, 48), :] = ref[...]


def norm_rows(idx, both, gain, normed, tail, cot):
    for k in range(NX):
        v = both[256 * k : 256 * k + 128, :].astype(F32)
        root = lax.rsqrt(jnp.mean(v * v, axis=1, keepdims=True) + EPS)
        normed[128 * k : 128 * k + 128, :] = (v * root * gain[...]).astype(BF)
        cot[128 * k : 128 * k + 128, :] = both[256 * k + 128 : 256 * k + 256, :]
    tail[...] = normed[T - RIM : T, :]


def turn(idx, nfull, mine, other, scr):
    core = idx[2]
    blank = jnp.zeros((128 - RIM, 128), F32)
    for j in range(D // 128):
        lanes = slice(128 * j, 128 * j + 128)
        scr[lanes, 0:T] = nfull[0:T, lanes].astype(F32).T.astype(BF)
        edge = jnp.concatenate([nfull[T:TR, lanes].astype(F32), blank], axis=0)
        scr[lanes, T : T + 128] = edge.T.astype(BF)
    for block in range(16):
        for out, half in ((mine, core), (other, 1 - core)):
            at = pl.multiple_of(96 * block + 48 * half, 16)
            out[48 * block : 48 * block + 48, :] = scr[pl.ds(at, 48), 0:TR]


def place(idx, mine, other, lanes, out):
    x, z, core = idx[0], idx[1], idx[2]
    for step in range(NZ):
        for k in range(NX):
            block = 4 * lax.rem(z + NZ - step, NZ) + lax.rem(x + NX - k, NX)
            for refs, half in ((mine, core), (other, 1 - core)):
                at = pl.multiple_of(96 * block + 48 * half, 16)
                out[pl.ds(at, 48), :] = refs[step][48 * k : 48 * k + 48, lanes]


def project(
    idx, normed, rim, m0, m1, m2, m3, t0, t1, t2, t3, par, hp,
    nfull, wa, ci, act, dsl, sm, sc, fp, scr, state, total,
):
    place(idx, (m0, m1, m2, m3), (t0, t1, t2, t3), slice(0, CA), wa)
    nfull[0:T, :] = normed[...]
    nfull[T:TR, :] = rim[...]

    raw = mm(nfull[0:T, :], wa[:, CC:CA]) + hp[0:1, :]
    held = iota2((T, 128), 1) < HL
    dt = jnp.where(held, jnp.maximum(raw, 0.0) + jnp.log1p(jnp.exp(-jnp.abs(raw))), 0.0)
    sm[0] = dt
    sm[2] = sigmoid(raw)
    @pl.loop(0, 4)
    def _(j):
        lanes = pl.ds(pl.multiple_of(j * 256, 256), 256)
        low = mm(nfull[...], wa[:, lanes]).astype(BF)
        ci[:, lanes] = low
        scr[RIM:TR, :] = low[0:T].astype(F32)
        scr[0:RIM, :] = low[T:TR].astype(F32)
        pre = par[4:5, lanes] + par[0:1, lanes] * scr[13 : 13 + T, :]
        for k in range(1, 4):
            pre = pre + par[k : k + 1, lanes] * scr[13 + k : 13 + k + T, :]
        s = sigmoid(pre)
        act[:, lanes] = (pre * s).astype(BF)
        dsl[:, lanes] = (s * (1.0 + pre * (1.0 - s))).astype(BF)

    e = spread_matrix(BF)
    tri = (iota2((L, L), 0) >= iota2((L, L), 1)).astype(F32)
    state[...] = jnp.zeros_like(state)
    total[...] = jnp.zeros_like(total)

    @pl.loop(0, NC, unroll=True)
    def _(c):
        rows = pl.ds(pl.multiple_of(c * L, L), L)
        dt = sm[0, rows, :]
        s = mm_high(tri, -dt * jnp.exp(hp[1:2, :]))
        sm[1, rows, :] = s
        last = s[L - 1 : L, :]
        w = spread(jnp.exp(last - s) * dt, e)
        vw = (act[rows, 0:HW].astype(F32) * w).astype(BF)
        part = mm_tn(act[rows, HW : HW + NS], vw)
        sc[c] = part
        last_e = spread(jnp.broadcast_to(last, (8, 128)), e)
        state[...] = jnp.exp(last_e[0:1]) * state[...] + part
        total[...] += last_e

    pack_state(fp, state[...], total[...])


def pack_state(fp, state, total):
    hi = total.astype(BF)
    lo = (total - hi.astype(F32)).astype(BF)
    fp[0:NS, :] = state.astype(BF)
    fp[NS : NS + 16, :] = jnp.concatenate(
        [hi.astype(F32), lo.astype(F32)], axis=0
    ).astype(BF)


def incoming(p1, p2, p3):
    t1 = p1[NS : NS + 16, :].astype(F32)
    t2 = p2[NS : NS + 16, :].astype(F32)
    t1 = t1[0:1] + t1[8:9]
    t2 = t2[0:1] + t2[8:9]
    return (
        p1[0:NS, :].astype(F32)
        + jnp.exp(t1) * p2[0:NS, :].astype(F32)
        + jnp.exp(t1 + t2) * p3[0:NS, :].astype(F32)
    )


def gates(
    idx, nfull, m0, m1, m2, m3, t0, t1, t2, t3, held, near, far, near_t, far_t, cot,
    gate, gny, wg, wo,
):
    z, core = idx[1], idx[2]
    place(idx, (m0, m1, m2, m3), (t0, t1, t2, t3), slice(CA, CA + HW), wg)
    for ref, block in ((held, z), (near, z + 3 - 2 * core), (near_t, z + 1 + 2 * core)):
        wo[pl.ds(pl.multiple_of(192 * lax.rem(block, NZ), 64), 192), :] = ref[...]
    for ref, half in ((far, core), (far_t, 1 - core)):
        at = pl.multiple_of(192 * lax.rem(z + 2, NZ) + 96 * half, 16)
        wo[pl.ds(at, 96), :] = ref[...]

    @pl.loop(0, 3)
    def _(j):
        lanes = pl.ds(pl.multiple_of(j * 256, 256), 256)
        gate[:, lanes] = mm(nfull[0:T, :], wg[:, lanes])
        gny[:, lanes] = mm_nt(cot[...], wo[lanes, :])


def within(idx, act, sm, hp, yi):
    e = spread_matrix(BF)
    skip = spread(jnp.broadcast_to(hp[2:3, :], (8, 128)), e)[0:1]
    left = iota2((L, 128), 1) < PW
    causal = iota2((L, L), 0) >= iota2((L, L), 1)

    @pl.loop(0, NC, unroll=True)
    def _(c):
        rows = pl.ds(pl.multiple_of(c * L, L), L)
        s = sm[1, rows, :]
        s_t = s.T
        v = act[rows, 0:HW].astype(F32)
        u = v * spread(sm[0, rows, :], e)
        scores = mm_nt(act[rows, HW + NS : CC], act[rows, HW : HW + NS])
        for j in range(HL // 2):
            parts = []
            for h in (2 * j, 2 * j + 1):
                gap = s[:, h : h + 1] - s_t[h : h + 1, :]
                parts.append((scores * jnp.exp(jnp.where(causal, gap, -1e30))).astype(BF))
            pair = u[:, 128 * j : 128 * j + 128]
            both = jnp.concatenate(
                [jnp.where(left, pair, 0.0), jnp.where(left, 0.0, pair)], axis=0
            ).astype(BF)
            yi[rows, 128 * j : 128 * j + 128] = mm(jnp.concatenate(parts, axis=1), both)
        yi[rows, :] += skip * v


def mix(idx, yi, act, sm, sc, p1, p2, p3, gate, gny, par, mixed, hin, sums, state):
    e = spread_matrix(BF)
    ones = jnp.ones((8, HW), BF)

    def rowsum(v):
        hi = v.astype(BF)
        lo = (v - hi.astype(F32)).astype(BF)
        return mm_nt(ones, hi) + mm_nt(ones, lo)

    state[...] = incoming(p1, p2, p3)

    @pl.loop(0, NC, unroll=True)
    def _(c):
        rows = pl.ds(pl.multiple_of(c * L, L), L)
        s = sm[1, rows, :]
        low = state[...].astype(BF)
        hin[c] = low
        y = yi[rows, :] + spread(jnp.exp(s), e) * mm(act[rows, HW + NS : CC], low)
        mixed[rows, :] = y
        z = gate[rows, :]
        g = y * (z * sigmoid(z))
        sq = rowsum(g * g)
        sg = rowsum(g * (gny[rows, :] * par[5:6, 0:HW]))
        sums[:, rows] = jnp.where(iota2((8, L), 0) == 0, sq, sg)
        last = spread(jnp.broadcast_to(s[L - 1 : L, :], (8, 128)), e)[0:1]
        state[...] = jnp.exp(last) * state[...] + sc[c]


def gated(
    idx, mixed, gate, gny, act, sm, s0, s1, s2, s3, par,
    ny, gmix, ggate, rp, small, state, total,
):
    e = spread_matrix(BF)
    gain = par[5:6, 0:HW]
    pick0 = (iota2((8, 128), 0) == 0).astype(F32)
    pick1 = (iota2((8, 128), 0) == 1).astype(F32)
    state[...] = jnp.zeros_like(state)
    total[...] = jnp.zeros_like(total)
    small[...] = jnp.zeros_like(small)

    @pl.loop(0, NC, unroll=True)
    def _(i):
        rows = pl.ds(pl.multiple_of((NC - 1 - i) * L, L), L)
        here = s0[:, rows] + s1[:, rows] + s2[:, rows] + s3[:, rows]
        sq = lax.dot_general(
            here, pick0, (((0,), (0,)), ((), ())), precision=HIGH, preferred_element_type=F32
        )
        sg = lax.dot_general(
            here, pick1, (((0,), (0,)), ((), ())), precision=HIGH, preferred_element_type=F32
        )
        r1 = lax.rsqrt(sq * (1.0 / DI) + EPS)
        pull = r1 * r1 * (sg * (1.0 / DI))
        r1 = jnp.concatenate([r1] * 6, axis=1)
        pull = jnp.concatenate([pull] * 6, axis=1)
        y = mixed[rows, :]
        z = gate[rows, :]
        sz = sigmoid(z)
        sil = z * sz
        g = y * sil
        gn = gny[rows, :]
        ghat = g * r1
        ny[rows, :] = (ghat * gain).astype(BF)
        gg = r1 * (gn * gain - g * pull)
        gm = gg * sil
        gmix[rows, :] = gm.astype(BF)
        ggate[rows, :] = (gg * y * (sz * (1.0 + z * (1.0 - sz)))).astype(BF)
        small[0:1, :] += jnp.sum(gn * ghat, axis=0, keepdims=True)
        small[1:2, :] += jnp.sum(gm * act[rows, 0:HW].astype(F32), axis=0, keepdims=True)
        s = sm[1, rows, :]
        part = mm_tn(act[rows, HW + NS : CC], (gm * spread(jnp.exp(s), e)).astype(BF))
        last_e = spread(jnp.broadcast_to(s[L - 1 : L, :], (8, 128)), e)
        state[...] = jnp.exp(last_e[0:1]) * state[...] + part
        total[...] += last_e

    pack_state(rp, state[...], total[...])


def within_back(idx, act, gmix, sm, gu, gbc, dsi, rw):
    left = iota2((L, 128), 1) < PW
    lane = iota2((L, 128), 1)
    causal = iota2((L, L), 1) >= iota2((L, L), 0)
    rw[...] = jnp.zeros_like(rw)

    @pl.loop(0, NC)
    def _(c):
        rows = pl.ds(pl.multiple_of(c * L, L), L)
        s = sm[1, rows, :]
        s_t = s.T
        dt = sm[0, rows, :]
        b = act[rows, HW : HW + NS]
        r = act[rows, HW + NS : CC]
        scores = mm_nt(b, r)
        grad_scores = jnp.zeros((L, L), F32)
        cols = jnp.zeros((L, 128), F32)
        for j in range(HL // 2):
            v = act[rows, 128 * j : 128 * j + 128].astype(F32)
            g = gmix[rows, 128 * j : 128 * j + 128]
            gf = g.astype(F32)
            parts = []
            for i in range(2):
                h = 2 * j + i
                gap = s_t[h : h + 1, :] - s[:, h : h + 1]
                q = jnp.exp(jnp.where(causal, gap, -1e30))
                own = jnp.where(left, v, 0.0) if i == 0 else jnp.where(left, 0.0, v)
                vg = mm_nt(own.astype(BF), g) * (q * dt[:, h : h + 1])
                grad_scores = grad_scores + vg
                w = scores * vg
                rw[h : h + 1, :] = jnp.sum(w, axis=0, keepdims=True)
                cols = jnp.where(lane == h, jnp.sum(w, axis=1, keepdims=True), cols)
                parts.append((scores * q).astype(BF))
            both = jnp.concatenate(
                [jnp.where(left, gf, 0.0), jnp.where(left, 0.0, gf)], axis=0
            ).astype(BF)
            gu[rows, 128 * j : 128 * j + 128] = mm(jnp.concatenate(parts, axis=1), both)
        dsi[rows, :] = rw[...].T - cols
        low = grad_scores.astype(BF)
        gbc[rows, 0:NS] = mm(low, r)
        gbc[rows, NS : 2 * NS] = mm_tn(low, b)


def across_back(
    idx, act, gmix, sm, gu, gbc, dsi, hin, p1, p2, p3, dsl, ci, par, hp, gains, turned,
    gpa, late, out, small, gps, cis, state, sums,
):
    e = spread_matrix(BF)
    skip = spread(jnp.broadcast_to(hp[2:3, :], (8, 128)), e)[0:1]
    rate = jnp.exp(hp[1:2, :])
    upper = (iota2((L, L), 1) >= iota2((L, L), 0)).astype(F32)
    below = (iota2((L, L), 0) > iota2((L, L), 1)).astype(F32)
    held = iota2((L, 128), 1) < HL
    gps[0:RIM, :] = jnp.zeros((RIM, CC), F32)
    gps[RIM + T : RIM + T + 16, :] = jnp.zeros((16, CC), F32)
    gpa[T:TR, CC:CA] = jnp.zeros((RIM, 128), BF)
    state[...] = incoming(p1, p2, p3)
    sums[...] = jnp.zeros_like(sums)

    @pl.loop(0, NC, unroll=True)
    def _(i):
        c = NC - 1 - i
        rows = pl.ds(pl.multiple_of(c * L, L), L)
        b = act[rows, HW : HW + NS]
        r = act[rows, HW + NS : CC]
        old = state[...]
        low = old.astype(BF)
        s = sm[1, rows, :]
        dt = sm[0, rows, :]
        last = s[L - 1 : L, :]
        tail_e = spread(jnp.exp(last - s), e)
        dt_e = spread(dt, e)
        grow_e = spread(jnp.exp(s), e)
        last_e = jnp.exp(spread(jnp.broadcast_to(last, (8, 128)), e)[0:1])
        v = act[rows, 0:HW].astype(F32)
        g = gmix[rows, :].astype(F32)
        carried = tail_e * mm(b, low)
        grad_u = gu[rows, :] + carried
        u = v * dt_e
        grad_v = dt_e * grad_u + skip * g
        grad_b = gbc[rows, 0:NS] + mm_nt((u * tail_e).astype(BF), low)
        gs = (g * grow_e).astype(BF)
        h = hin[c]
        grad_c = gbc[rows, NS : 2 * NS] + mm_nt(gs, h)
        inter = head_sums(g * (grow_e * mm(r, h)), e)
        kept = head_sums(u * carried, e)
        grad_step = head_sums(v * grad_u, e)
        cross = jnp.sum(h.astype(F32) * old, axis=0, keepdims=True) * last_e
        cross = head_sums(jnp.broadcast_to(cross, (8, HW)), e)[0:1]
        grad_a = mm_high(upper, dsi[rows, :] + inter) + mm_high(below, kept) + cross
        grad_raw = (grad_step - rate * grad_a) * sm[2, rows, :]
        sums[0:1, :] += jnp.sum(grad_raw, axis=0, keepdims=True)
        sums[1:2, :] += jnp.sum(grad_a * dt, axis=0, keepdims=True)
        gpa[rows, CC:CA] = jnp.where(held, grad_raw, 0.0).astype(BF)
        d = dsl[rows, :].astype(F32)
        to = pl.ds(pl.multiple_of(RIM + c * L, 16), L)
        gps[to, 0:HW] = grad_v * d[:, 0:HW]
        gps[to, HW : HW + NS] = grad_b * d[:, HW : HW + NS]
        gps[to, HW + NS : CC] = grad_c * d[:, HW + NS : CC]
        state[...] = last_e * old + mm_tn(r, gs)

    @pl.loop(0, 4)
    def _(j):
        lanes = pl.ds(pl.multiple_of(j * 256, 256), 256)
        cis[RIM:TR, :] = ci[0:T, lanes].astype(F32)
        cis[0:RIM, :] = ci[T:TR, lanes].astype(F32)
        gp = gps[RIM : RIM + T, lanes]
        small[4:5, lanes] = jnp.sum(gp, axis=0, keepdims=True)
        res = par[3:4, lanes] * gps[0:TR, lanes]
        for k in range(4):
            small[k : k + 1, lanes] = jnp.sum(
                gp * cis[13 + k : 13 + k + T, :], axis=0, keepdims=True
            )
            if k < 3:
                res = res + par[k : k + 1, lanes] * gps[3 - k : 3 - k + TR, lanes]
        low = res.astype(BF)
        gpa[0:T, lanes] = low[RIM:TR]
        gpa[T:TR, lanes] = low[0:RIM]

    for j in range(0, CA, 384):
        late[:, j : j + 384] = mm(turned[...], gpa[:, j : j + 384]).astype(BF)

    out[0:3, :] = jnp.zeros((3, 512), F32)
    for k in range(5):
        for j in range(2):
            out[3 + 2 * k + j : 4 + 2 * k + j, :] = small[k : k + 1, 512 * j : 512 * j + 512]
    out[13:14, :] = gains[0:1, 0:512]
    out[14:15, 0:256] = gains[0:1, 512:768]
    out[14:15, 256:384] = head_sums(jnp.broadcast_to(gains[1:2, :], (8, HW)), e)[0:1]
    out[14:15, 384:512] = sums[0:1, :]
    out[15:16, 0:128] = -rate * sums[1:2, :]
    out[15:16, 128:512] = jnp.zeros((1, 384), F32)


def normed_back(
    idx, gpa, ggate, wa, wg, nfull, gain, ny, wo, own, part, gn, late, small, acc, gsum
):
    @pl.loop(0, 6)
    def _(j):
        lanes = pl.ds(pl.multiple_of(j * 256, 256), 256)
        acc[:, lanes] = mm_nt(gpa[...], wa[lanes, :])
        acc[0:T, lanes] += mm_nt(ggate[...], wg[lanes, :])
        gsum[:, lanes] = jnp.broadcast_to(
            jnp.sum(acc[:, lanes] * nfull[:, lanes].astype(F32), axis=0, keepdims=True)
            / gain[:, lanes],
            (8, 256),
        )
        block = mm(ny[...], wo[:, lanes]).astype(BF)
        for k in range(NX):
            gn[k, 144:272, lanes] = block[128 * k : 128 * k + 128]

    for j in range(0, CA, 384):
        late[:, j : j + 384] = mm(own[...], gpa[:, j : j + 384]).astype(BF)
    for k in range(NX):
        rows = slice(128 * k, 128 * k + 128)
        gn[k, 0:128, :] = acc[rows, :].astype(BF)
        gn[k, 128:144, :] = acc[T:TR, :].astype(BF)
    small[...] = part[...]
    for j in range(3):
        small[j : j + 1, :] = gsum[0:1, 512 * j : 512 * j + 512]


def finish_out(idx, tokens, summed, out):
    out[...] = (tokens[...].astype(F32) + summed[144:272].astype(F32)).astype(BF)


def finish_back(idx, tokens, cot, summed, spill, gain, out, acc):
    v = tokens[...].astype(F32)
    root = lax.rsqrt(jnp.mean(v * v, axis=1, keepdims=True) + EPS)
    acc[...] = summed[0:128].astype(F32)
    acc[128 - RIM : 128, :] += spill[...].astype(F32)
    q = acc[...] * gain[...]
    pull = jnp.mean(q * v, axis=1, keepdims=True)
    out[...] = (cot[...].astype(F32) + root * (q - v * (root * root) * pull)).astype(BF)


def grad_early(idx, ny, cot, ggate, tm, tt, mine, other, nyt, rows, part):
    core, y = idx[2], idx[3]
    for j in range(HW // 128):
        lanes = slice(128 * j, 128 * j + 128)
        nyt[lanes, :] = ny[:, lanes].astype(F32).T.astype(BF)
    for half, which in enumerate((core, 1 - core)):
        for z in range(NZ):
            at = pl.multiple_of(192 * z + 96 * which, 16)
            row = 384 * half + 96 * z
            rows[row : row + 96, :] = nyt[pl.ds(at, 96), :]
    for q in range(4):
        k = lax.rem(q + 4 - y, 4)
        part[...] = mm(rows[...], cot[:, 384 * q : 384 * q + 384]).astype(BF)
        for half, (turned, out) in enumerate(((tm, mine), (tt, other))):
            gate = mm(turned[:, 0:T], ggate[:, 192 * q : 192 * q + 192]).astype(BF)
            out[k, :, 0:192] = gate
            for z in range(NZ):
                row = 384 * half + 96 * z
                out[k, 192 * z : 192 * z + 96, 192:384] = part[row : row + 96, 0:192]
                out[k, 192 * z + 96 : 192 * z + 192, 192:384] = part[row : row + 96, 192:384]


def add_early(idx, a, b, o0, o1, o2, o3):
    for k, out in enumerate((o0, o1, o2, o3)):
        out[...] = a[k] + b[k]


def sum_early(idx, a, b, c, d, out):
    out[...] = (
        a[...].astype(F32) + b[...].astype(F32) + (c[...].astype(F32) + d[...].astype(F32))
    ).astype(BF)


def split_z(idx, late, got, s0, s1, early, o0, o1, o3, oa, ob, o2):
    z = idx[1]
    small = wide(s0[...] + s1[...])
    for k, out in enumerate((o0, o1, o2, o3)):
        at = pl.multiple_of(lax.rem(z + k, NZ) * 192, 64)
        rows = pl.ds(at, 192)
        out[0:192, :] = late[rows, :] + got[rows, :]
        out[192:208, 0:CC] = small
        out[192:208, CC:CA] = jnp.zeros((16, CA - CC), BF)
        for j in range(3):
            rows = pl.ds(pl.multiple_of(at + 64 * j, 64), 64)
            out[208:272, 384 * j : 384 * j + 384] = early[rows, :]
    oa[...] = o2[0:HALF, :]
    ob[...] = o2[HALF:272, :]


def relay_z(idx, o1, o3, a, b, up, down):
    up[0:HALF, :] = o1[0:HALF, :] + a[...]
    up[HALF:272, :] = o1[HALF:272, :]
    down[0:HALF, :] = o3[0:HALF, :]
    down[HALF:272, :] = o3[HALF:272, :] + b[...]


def wide(v):
    hi = v.astype(BF).astype(F32)
    return jnp.concatenate([hi, v - hi], axis=1).astype(BF)


def halves(v):
    hi = v.astype(BF).astype(F32)
    return jnp.concatenate([hi, v - hi], axis=0).astype(BF)


def joined(v):
    v = v.astype(F32)
    return v[0:16] + v[16:32]


def split_y(idx, l0, l1, l2, o0, o1, o2, o3, early, scr, late):
    y = idx[3]
    total = l0[...].astype(F32) + l1[...].astype(F32) + l2[...].astype(F32)
    late[...] = total[0:192].astype(BF)
    for j in range(3):
        early[64 * j : 64 * j + 64, :] = total[208:272, 384 * j : 384 * j + 384].astype(BF)
    small = halves(total[192:208, 0:512] + total[192:208, 512:1024])
    for q in range(4):
        scr[q, :, 0:192] = late[:, 192 * q : 192 * q + 192]
        scr[q, :, 192:256] = late[:, HW + 64 * q : HW + 64 * q + 64]
        for j in range(4):
            scr[q, 32 * j : 32 * j + 32, 256:384] = small[:, 128 * j : 128 * j + 128]
        scr[q, 128:192, 256:384] = jnp.zeros((64, 128), BF)
        for j in range(4):
            scr[q, 128:176, 256 + 16 * j : 272 + 16 * j] = late[48 * j : 48 * j + 48, CC : CC + 16]
    for k, out in enumerate((o0, o1, o2, o3)):
        out[...] = scr[lax.rem(y + k, 4)]


def sum_y(idx, a, b, c, d, early, o0, o1, o2, o3, scr):
    x = idx[0]
    total = a[...].astype(F32) + b[...].astype(F32) + (c[...].astype(F32) + d[...].astype(F32))
    total = total.astype(BF)
    scr[:, 0:256] = total[:, 0:256]
    scr[:, 256:448] = early[:, 0:192]
    scr[:, 448:512] = jnp.zeros((192, 64), BF)
    for j in range(4):
        scr[48 * j : 48 * j + 48, 448:464] = total[128:176, 256 + 16 * j : 272 + 16 * j]
    small = jnp.concatenate(
        [
            sum(joined(ref[32 * j : 32 * j + 32, 256:384]) for ref in (a, b, c, d))
            for j in range(4)
        ],
        axis=1,
    )
    small = halves(small)
    for k, out in enumerate((o0, o1, o2, o3)):
        at = pl.multiple_of(lax.rem(x + k, NX) * 48, 16)
        out[0:48, :] = scr[pl.ds(at, 48), :]
        out[48:80, :] = small


def arrange_x(idx, a, b, c, d, early, out, gain, conv, ogain, heads, scr, steps):
    x = idx[0]
    shared = jnp.zeros((48, 64), F32)
    for k, ref in enumerate((a, b, c, d)):
        source = lax.rem(x + NX - k, NX)
        rows = pl.ds(pl.multiple_of(source * 48, 16), 48)
        out[rows, 0:192] = ref[0:48, 0:192]
        out[rows, 256:448] = ref[0:48, 256:448]
        shared = shared + ref[0:48, 192:256].astype(F32)
        scr[source] = joined(ref[48:80, :])
        steps[source] = ref[0:48, 448:464]
    out[:, 192:256] = jnp.zeros((192, 64), BF)
    out[0:48, 192:256] = shared.astype(BF)
    for xp in range(NX):
        out[48:96, 192 + 16 * xp : 208 + 16 * xp] = steps[xp]
    out[:, 448:640] = early[:, 192:384]
    both = scr[0] + scr[1] + (scr[2] + scr[3])
    for j in range(3):
        gain[0:1, 512 * j : 512 * j + 512] = both[j : j + 1, :]
    for k in range(5):
        conv[k : k + 1, DI : DI + 256] = both[4 + 2 * k : 5 + 2 * k, 256:512]
    heads[...] = jnp.zeros_like(heads)
    for xp in range(NX):
        own = scr[xp]
        for q in range(4):
            lane = 768 * q + 192 * xp
            for k in range(5):
                for at, size in pieces(192 * q, 192):
                    conv[k : k + 1, lane + at - 192 * q : lane + at - 192 * q + size] = own[
                        3 + 2 * k + at // 512 : 4 + 2 * k + at // 512, at % 512 : at % 512 + size
                    ]
            for at, size in pieces(192 * q, 192):
                ogain[0:1, lane + at - 192 * q : lane + at - 192 * q + size] = own[
                    13 + at // 512 : 14 + at // 512, at % 512 : at % 512 + size
                ]
            to = slice(12 * q + 3 * xp, 12 * q + 3 * xp + 3)
            heads[0:1, to] = own[14:15, 384 + 3 * q : 387 + 3 * q]
            heads[1:2, to] = own[15:16, 3 * q : 3 * q + 3]
            heads[2:3, to] = own[14:15, 256 + 3 * q : 259 + 3 * q]


def pieces(at, size):
    end = at + size
    while at < end:
        step = min(end, (at // 512 + 1) * 512) - at
        yield at, step
        at += step


def finish_weights(idx, a, b, c, d, e, f, g, h, gmain, gdt, gout, scr, steps):
    y, core = idx[3], idx[2]
    steps[...] = jnp.zeros_like(steps)
    for half in range(2):
        place = lax.rem(core + half, 2)
        for k, ref in enumerate((a, b, c, d) if half == 0 else (e, f, g, h)):
            scr[lax.rem(y + 4 - k, 4)] = ref[...]
        rows = pl.ds(pl.multiple_of(48 * place, 16), 48)
        long = pl.ds(pl.multiple_of(96 * place, 16), 96)
        for q in range(4):
            gout[long, 384 * q : 384 * q + 192] = scr[q, 0:96, 448:640].astype(F32)
            gout[long, 384 * q + 192 : 384 * q + 384] = scr[q, 96:192, 448:640].astype(F32)
            gmain[rows, 6144 + 64 * q : 6144 + 64 * q + 64] = scr[q, 0:48, 192:256].astype(F32)
            for xp in range(NX):
                lane = 768 * q + 192 * xp
                part = scr[q, 48 * xp : 48 * xp + 48, :].astype(F32)
                gmain[rows, lane : lane + 192] = part[:, 256:448]
                gmain[rows, DI + lane : DI + lane + 192] = part[:, 0:192]
        for xp in range(NX):
            part = scr[0, 48:96, 192 + 16 * xp : 208 + 16 * xp].astype(F32)
            for q in range(4):
                steps[rows, 12 * q + 3 * xp : 12 * q + 3 * xp + 3] = part[:, 3 * q : 3 * q + 3]
    gdt[...] = steps[...].T[0:48, 0:96]


def round_shift(v, axis, k, n=4):
    return lax.ppermute(v, axis, [(s, (s + k) % n) for s in range(n)])


def onward(v, k):
    return lax.ppermute(v, "z", [(s, s + k) for s in range(NZ) if 0 <= s + k < NZ])


def around(v, axis, n=4):
    return [v] + [round_shift(v, axis, k, n) for k in range(1, n)]


def spread_out(parts, axis, n=4):
    return [parts[0]] + [round_shift(parts[k], axis, k, n) for k in range(1, n)]


def after(value, *others):
    return lax.optimization_barrier((value,) + others)[0]


def after_all(values, *others):
    return list(lax.optimization_barrier(tuple(values) + others)[: len(values)])


def local(
    tokens, norm_gain, w_main, w_dt, conv_weight, conv_bias, dt_bias, a_log, skip_gain,
    out_gain, w_out, cotangent,
):
    x, z, core, y = (lax.axis_index(name) for name in ("x", "z", "core", "y"))
    idx = jnp.stack([x, z, core, y]).astype(jnp.int32)

    gain = norm_gain[None]
    rates = jnp.stack([dt_bias, a_log, skip_gain])

    call = Kernels(idx)
    both = jnp.concatenate([tokens, cotangent], axis=0)
    both = lax.all_gather(both, "x", axis=0, tiled=True)
    first = call(
        pack_main, [((48, CA + HW), BF)] * 4,
        [w_main, w_dt.T],
        [((NX, 48, CA + HW), BF), ((128, 128), F32)],
    )
    first = after_all(first)
    held = after(w_out, first[0])
    near = lax.ppermute(
        held,
        ("core", "z"),
        [(s, (s + 1) % 4) for s in range(4)] + [(4 + s, 4 + (s + 3) % 4) for s in range(4)],
    )
    first = spread_out(first, "x")
    far = lax.dynamic_slice(after(held, first[1]), (core * 96, 0), (96, D))
    far = round_shift(far, "z", 2)
    par, hp = call(
        params,
        [((8, CC), F32), ((8, 128), F32)],
        [conv_weight, conv_bias[None], out_gain[None], rates],
    )
    *first, near = after_all([*first, near])
    rows, part = call(
        stack, [((192, CA + HW), BF), ((48, CA + HW), BF)], first, light=True
    )
    part = round_shift(part, "z", 2)
    behind = after(rows, part)
    up, down = round_shift(behind, "z", 1), round_shift(behind, "z", 3)
    part = around(part, "y")
    normed, tail, cot = call(
        norm_rows,
        [((T, D), BF), ((RIM, D), BF), ((T, D), BF)],
        [after(both, near, far), gain],
    )
    rim = onward(tail, 1)
    part = after_all(part, tail)
    (beyond,) = call(stack_far, [((192, CA + HW), BF)], part, light=True)
    w_mine = [rows, up, beyond, down]
    w_other = [round_shift(v, "core", 1, 2) for v in w_mine]
    near, far = after_all([near, far], tail)
    near_t, far_t = (round_shift(v, "core", 1, 2) for v in (near, far))
    nfull, wa, ci, act, dsl, sm, sc, fp = call(
        project,
        [
            ((TR, D), BF), ((D, CA), BF), ((TR, CC), BF), ((T, CC), BF), ((T, CC), BF),
            ((3, T, 128), F32), ((NC, NS, HW), F32), ((NS + 16, HW), BF),
        ],
        [normed, rim, *w_mine, *w_other, par, hp],
        [((TR, 256), F32), ((NS, HW), F32), ((8, HW), F32)],
            )
    states = [onward(fp, k) for k in (1, 2, 3)]
    (yi,) = call(within, [((T, HW), F32)], [act, sm, hp])
    gate, gny, wg, wo = call(
        gates,
        [((T, HW), F32), ((T, HW), F32), ((D, HW), BF), ((HW, D), BF)],
        [nfull, *w_mine, *w_other, held, near, far, near_t, far_t, cot],
    )
    mixed, hin, sums = call(
        mix,
        [((T, HW), F32), ((NC, NS, HW), BF), ((8, T), F32)],
        [yi, act, sm, sc, *states, gate, gny, par],
        [((NS, HW), F32)],
    )
    nt_mine, nt_other = call(
        turn, [((HW, TR), BF), ((HW, TR), BF)], [nfull], [((D, T + 128), BF)]
    )
    ny, gmix, ggate, rp, small_g = call(
        gated,
        [((T, HW), BF)] * 3 + [((NS + 16, HW), BF), ((8, HW), F32)],
        [mixed, gate, gny, act, sm, *around(sums, "x"), par],
        [((NS, HW), F32), ((8, HW), F32)],
    )
    pulls = [onward(rp, -k) for k in (1, 2, 3)]
    early, got = call(
        grad_early,
        [((4, HW, 384), BF)] * 2,
        [ny, cot, ggate, nt_mine, nt_other],
        [((HW, T), BF), ((HW, T), BF), ((HW, 384), BF)],
    )
    got = round_shift(got, "core", 1, 2)
    gu, gbc, dsi = call(
        within_back,
        [((T, HW), F32), ((T, 2 * NS), F32), ((T, 128), F32)],
        [act, gmix, sm],
        [((128, 128), F32)],
    )
    got, *pulls = after_all([got, *pulls], gu)
    early = call(add_early, [((HW, 384), BF)] * 4, [after(early, *pulls), got])
    early = spread_out(early, "y")
    gpa, late, small = call(
        across_back,
        [((TR, CA), BF), ((HW, CA), BF), ((16, 512), F32)],
        [act, gmix, sm, gu, gbc, dsi, hin, *pulls, dsl, ci, par, hp, small_g, nt_other],
        [
            ((8, CC), F32), ((T + 32, CC), F32), ((TR, 256), F32), ((NS, HW), F32),
            ((8, 128), F32),
        ],
    )
    got = round_shift(late, "core", 1, 2)
    gn, late_own, small = call(
        normed_back,
        [((NX, 272, D), BF), ((HW, CA), BF), ((16, 512), F32)],
        [gpa, ggate, wa, wg, nfull, gain, ny, wo, nt_mine, small],
        [((TR, D), F32), ((8, D), F32)],
        light=True,
    )
    small_got = round_shift(small, "core", 1, 2)
    (early,) = call(sum_early, [((HW, 384), BF)], early)
    here, up, down, far_up, far_down = call(
        split_z,
        [((272, CA), BF)] * 3 + [((HALF, CA), BF), ((272 - HALF, CA), BF)],
        [late_own, got, small, small_got, early],
        [((272, CA), BF)],
        light=True,
    )
    far_up = round_shift(far_up, "z", 1)
    far_down = round_shift(far_down, "z", 3)
    up, down = call(relay_z, [((272, CA), BF)] * 2, [up, down, far_up, far_down], light=True)
    late = [here, round_shift(up, "z", 1), round_shift(down, "z", 3)]
    gn = lax.psum_scatter(gn, "x", scatter_dimension=0, tiled=True).reshape(272, D)
    *parts, early = call(
        split_y,
        [((192, 384), BF)] * 5,
        late,
        [((4, 192, 384), BF), ((192, CA), BF)],
        light=True,
    )
    parts = spread_out(parts, "y")
    parts = call(
        sum_y,
        [((80, 512), BF)] * 4,
        [*parts, early],
        [((192, 512), BF)],
        light=True,
    )
    parts = spread_out(parts, "x")
    *parts, gn = after_all([*parts, gn])
    final, g_gain, g_conv, g_ogain, g_heads = call(
        arrange_x,
        [((192, 640), BF), ((1, D), F32), ((8, DI + 256), F32), ((1, DI), F32), ((8, 128), F32)],
        [*parts, early],
        [((4, 16, 512), F32), ((4, 48, 16), BF)],
    )
    finals = around(final, "y")
    gn = after(gn, final)
    spill = lax.ppermute(
        gn[128:144], ("z", "x"), [(4 * s + 3, 4 * s - 1) for s in range(1, NZ)]
    )
    (block_out,) = call(finish_out, [((128, D), BF)], [tokens, gn])
    small = [
        g_gain[0], g_conv[:4], g_conv[4], g_heads[0, :48], g_heads[1, :48], g_heads[2, :48],
        g_ogain[0],
    ]
    spill, *small = after_all([spill, *small])
    (grad_tokens,) = call(
        finish_back,
        [((128, D), BF)],
        [tokens, cotangent, gn, spill, gain],
        [((128, D), F32)],
    )
    others = [round_shift(v, "core", 1, 2) for v in finals]
    g_main, g_dt, g_out = call(
        finish_weights,
        [((96, 6400), F32), ((48, 96), F32), ((192, D), F32)],
        [*finals, *others],
        [((4, 192, 640), BF), ((128, 128), F32)],
    )
    return (
        block_out, grad_tokens, small[0], g_main, g_dt.T, *small[1:], g_out,
    )


def solution(mesh):
    grid = Mesh(mesh.devices.reshape(4, 2, 4, 4), ("y", "core", "z", "x"))
    rows = P(("y", "core", "z", "x"), None)
    shard = P(("z", "x"), None)
    whole = P()
    return jax.shard_map(
        local,
        mesh=grid,
        in_specs=(
            rows, whole, shard, shard, whole, whole, whole, whole, whole, whole, shard, rows,
        ),
        out_specs=(
            rows, rows, whole, shard, shard, whole, whole, whole, whole, whole, whole, shard,
        ),
        check_vma=False,
    )
```

```python
import functools

import jax
import jax.numpy as jnp
from jax import lax
from jax.experimental import pallas as pl
from jax.experimental.pallas import tpu as pltpu
from jax.sharding import Mesh, PartitionSpec as P

EPS = 1e-05
BF = jnp.bfloat16
F32 = jnp.float32
HIGH = lax.Precision.HIGHEST
NX = 4
NZ = 4
D = 1536
HL = 12
PW = 64
HW = 768
NS = 128
L = 128
NC = 4
T = 512
LIMIT = 12
RIM = 16
TR = T + RIM
CC = 1024
HALF = 144
CA = 1152
DI = 3072


class Kernels:
    def __init__(self, idx):
        self.idx = idx

    def __call__(self, body, outs, ins, scratch=(), limit=LIMIT, light=False):
        specs = [pl.BlockSpec(memory_space=pltpu.SMEM)]
        specs += [pl.BlockSpec(memory_space=pltpu.VMEM)] * len(ins)
        got = pl.pallas_call(
            body,
            out_shape=[jax.ShapeDtypeStruct(shape, kind) for shape, kind in outs],
            in_specs=specs,
            out_specs=[pl.BlockSpec(memory_space=pltpu.VMEM)] * len(outs),
            scratch_shapes=[pltpu.VMEM(shape, kind) for shape, kind in scratch],
            compiler_params=pltpu.CompilerParams(vmem_limit_bytes=limit << 20),
            cost_estimate=pl.CostEstimate(
                flops=1 if light else 1 << 36,
                bytes_accessed=1 if light else 1 << 28,
                transcendentals=1 if light else 1 << 20,
            ),
            name=body.__name__,
        )(self.idx, *ins)
        self.idx, *got = lax.optimization_barrier((self.idx, *got))
        return got


def mm(a, b):
    return lax.dot_general(a, b, (((1,), (0,)), ((), ())), preferred_element_type=F32)


def mm_nt(a, b):
    return lax.dot_general(a, b, (((1,), (1,)), ((), ())), preferred_element_type=F32)


def mm_tn(a, b):
    return lax.dot_general(a, b, (((0,), (0,)), ((), ())), preferred_element_type=F32)


def mm_high(a, b):
    return lax.dot_general(
        a, b, (((1,), (0,)), ((), ())), precision=HIGH, preferred_element_type=F32
    )


def iota2(shape, dim):
    return lax.broadcasted_iota(jnp.int32, shape, dim)


def spread_matrix(kind):
    return (
        lax.shift_right_logical(iota2((128, HW), 1), 6) == iota2((128, HW), 0)
    ).astype(kind)


def spread(v, e):
    hi = v.astype(BF)
    rest = v - hi.astype(F32)
    mid = rest.astype(BF)
    lo = (rest - mid.astype(F32)).astype(BF)
    return mm(hi, e) + mm(mid, e) + mm(lo, e)


def head_sums(v, e):
    hi = v.astype(BF)
    lo = (v - hi.astype(F32)).astype(BF)
    return mm_nt(hi, e) + mm_nt(lo, e)


def sigmoid(v):
    return 1.0 / (1.0 + jnp.exp(-v))


def chunk(ref, c, lanes=slice(None), base=0):
    return ref[pl.ds(pl.multiple_of(base + c * L, 16), L), lanes]


def params(idx, taps, bias, gain, rates, par, hp):
    par[...] = jnp.zeros_like(par)
    hp[...] = jnp.zeros_like(hp)
    par[0:4, HW:CC] = taps[:, DI : DI + 256]
    par[4:5, HW:CC] = bias[:, DI : DI + 256]
    for xp in range(NX):

        @pl.when(idx[0] == xp)
        def _():
            for zp in range(NZ):
                at = 768 * zp + 192 * xp
                to = slice(192 * zp, 192 * zp + 192)
                par[0:4, to] = taps[:, at : at + 192]
                par[4:5, to] = bias[:, at : at + 192]
                par[5:6, to] = gain[:, at : at + 192]
                at = 12 * zp + 3 * xp
                hp[0:3, 3 * zp : 3 * zp + 3] = rates[:, at : at + 3]


def pack_main(idx, wm, wd, o0, o1, o2, o3, scr, steps):
    x, core = idx[0], idx[2]
    rows = pl.ds(pl.multiple_of(core * 48, 16), 48)
    steps[...] = jnp.zeros_like(steps)
    steps[0:48, 0:96] = wd[...].astype(F32)
    steps[...] = steps[...].T
    for xp in range(NX):
        scr[xp, :, CC:CA] = jnp.zeros((48, 128), BF)
        for zp in range(NZ):
            at = 768 * zp + 192 * xp
            to = slice(192 * zp, 192 * zp + 192)
            scr[xp, :, to] = wm[rows, DI + at : DI + at + 192]
            scr[xp, :, CA + 192 * zp : CA + 192 * zp + 192] = wm[rows, at : at + 192]
            scr[xp, :, CC + 3 * zp : CC + 3 * zp + 3] = steps[
                rows, 12 * zp + 3 * xp : 12 * zp + 3 * xp + 3
            ].astype(BF)
        scr[xp, :, HW:CC] = wm[rows, 2 * DI : 2 * DI + 256]
    for k, out in enumerate((o0, o1, o2, o3)):
        out[...] = scr[lax.rem(x + k, NX)]


def stack(idx, a, b, c, d, out, part):
    y = idx[3]
    for k, ref in enumerate((a, b, c, d)):
        out[48 * k : 48 * k + 48, :] = ref[...]
    part[...] = out[pl.ds(pl.multiple_of(48 * y, 16), 48), :]


def stack_far(idx, a, b, c, d, out):
    y = idx[3]
    for k, ref in enumerate((a, b, c, d)):
        at = pl.multiple_of(48 * lax.rem(y + 4 - k, 4), 16)
        out[pl.ds(at, 48), :] = ref[...]


def norm_rows(idx, both, gain, normed, tail, cot):
    for k in range(NX):
        v = both[256 * k : 256 * k + 128, :].astype(F32)
        root = lax.rsqrt(jnp.mean(v * v, axis=1, keepdims=True) + EPS)
        normed[128 * k : 128 * k + 128, :] = (v * root * gain[...]).astype(BF)
        cot[128 * k : 128 * k + 128, :] = both[256 * k + 128 : 256 * k + 256, :]
    tail[...] = normed[T - RIM : T, :]


def turn(idx, nfull, mine, other, scr):
    core = idx[2]
    blank = jnp.zeros((128 - RIM, 128), F32)
    for j in range(D // 128):
        lanes = slice(128 * j, 128 * j + 128)
        scr[lanes, 0:T] = nfull[0:T, lanes].astype(F32).T.astype(BF)
        edge = jnp.concatenate([nfull[T:TR, lanes].astype(F32), blank], axis=0)
        scr[lanes, T : T + 128] = edge.T.astype(BF)
    for block in range(16):
        for out, half in ((mine, core), (other, 1 - core)):
            at = pl.multiple_of(96 * block + 48 * half, 16)
            out[48 * block : 48 * block + 48, :] = scr[pl.ds(at, 48), 0:TR]


def place(idx, mine, other, lanes, out):
    x, z, core = idx[0], idx[1], idx[2]
    for step in range(NZ):
        for k in range(NX):
            block = 4 * lax.rem(z + NZ - step, NZ) + lax.rem(x + NX - k, NX)
            for refs, half in ((mine, core), (other, 1 - core)):
                at = pl.multiple_of(96 * block + 48 * half, 16)
                out[pl.ds(at, 48), :] = refs[step][48 * k : 48 * k + 48, lanes]


def project(
    idx, normed, rim, m0, m1, m2, m3, t0, t1, t2, t3, par, hp,
    nfull, wa, ci, act, dsl, sm, sc, fp, scr, state, total,
):
    place(idx, (m0, m1, m2, m3), (t0, t1, t2, t3), slice(0, CA), wa)
    nfull[0:T, :] = normed[...]
    nfull[T:TR, :] = rim[...]

    raw = mm(nfull[0:T, :], wa[:, CC:CA]) + hp[0:1, :]
    held = iota2((T, 128), 1) < HL
    dt = jnp.where(held, jnp.maximum(raw, 0.0) + jnp.log1p(jnp.exp(-jnp.abs(raw))), 0.0)
    sm[0] = dt
    sm[2] = sigmoid(raw)
    @pl.loop(0, 4)
    def _(j):
        lanes = pl.ds(pl.multiple_of(j * 256, 256), 256)
        low = mm(nfull[...], wa[:, lanes]).astype(BF)
        ci[:, lanes] = low
        scr[RIM:TR, :] = low[0:T].astype(F32)
        scr[0:RIM, :] = low[T:TR].astype(F32)
        pre = par[4:5, lanes] + par[0:1, lanes] * scr[13 : 13 + T, :]
        for k in range(1, 4):
            pre = pre + par[k : k + 1, lanes] * scr[13 + k : 13 + k + T, :]
        s = sigmoid(pre)
        act[:, lanes] = (pre * s).astype(BF)
        dsl[:, lanes] = (s * (1.0 + pre * (1.0 - s))).astype(BF)

    e = spread_matrix(BF)
    tri = (iota2((L, L), 0) >= iota2((L, L), 1)).astype(F32)
    state[...] = jnp.zeros_like(state)
    total[...] = jnp.zeros_like(total)

    @pl.loop(0, NC, unroll=True)
    def _(c):
        rows = pl.ds(pl.multiple_of(c * L, L), L)
        dt = sm[0, rows, :]
        s = mm_high(tri, -dt * jnp.exp(hp[1:2, :]))
        sm[1, rows, :] = s
        last = s[L - 1 : L, :]
        w = spread(jnp.exp(last - s) * dt, e)
        vw = (act[rows, 0:HW].astype(F32) * w).astype(BF)
        part = mm_tn(act[rows, HW : HW + NS], vw)
        sc[c] = part
        last_e = spread(jnp.broadcast_to(last, (8, 128)), e)
        state[...] = jnp.exp(last_e[0:1]) * state[...] + part
        total[...] += last_e

    pack_state(fp, state[...], total[...])


def pack_state(fp, state, total):
    hi = total.astype(BF)
    lo = (total - hi.astype(F32)).astype(BF)
    fp[0:NS, :] = state.astype(BF)
    fp[NS : NS + 16, :] = jnp.concatenate(
        [hi.astype(F32), lo.astype(F32)], axis=0
    ).astype(BF)


def incoming(p1, p2, p3):
    t1 = p1[NS : NS + 16, :].astype(F32)
    t2 = p2[NS : NS + 16, :].astype(F32)
    t1 = t1[0:1] + t1[8:9]
    t2 = t2[0:1] + t2[8:9]
    return (
        p1[0:NS, :].astype(F32)
        + jnp.exp(t1) * p2[0:NS, :].astype(F32)
        + jnp.exp(t1 + t2) * p3[0:NS, :].astype(F32)
    )


def gates(
    idx, nfull, m0, m1, m2, m3, t0, t1, t2, t3, held, near, far, near_t, far_t, cot,
    gate, gny, wg, wo,
):
    z, core = idx[1], idx[2]
    place(idx, (m0, m1, m2, m3), (t0, t1, t2, t3), slice(CA, CA + HW), wg)
    for ref, block in ((held, z), (near, z + 3 - 2 * core), (near_t, z + 1 + 2 * core)):
        wo[pl.ds(pl.multiple_of(192 * lax.rem(block, NZ), 64), 192), :] = ref[...]
    for ref, half in ((far, core), (far_t, 1 - core)):
        at = pl.multiple_of(192 * lax.rem(z + 2, NZ) + 96 * half, 16)
        wo[pl.ds(at, 96), :] = ref[...]

    @pl.loop(0, 3)
    def _(j):
        lanes = pl.ds(pl.multiple_of(j * 256, 256), 256)
        gate[:, lanes] = mm(nfull[0:T, :], wg[:, lanes])
        gny[:, lanes] = mm_nt(cot[...], wo[lanes, :])


def within(idx, act, sm, hp, yi):
    e = spread_matrix(BF)
    skip = spread(jnp.broadcast_to(hp[2:3, :], (8, 128)), e)[0:1]
    left = iota2((L, 128), 1) < PW
    causal = iota2((L, L), 0) >= iota2((L, L), 1)

    @pl.loop(0, NC)
    def _(c):
        rows = pl.ds(pl.multiple_of(c * L, L), L)
        s = sm[1, rows, :]
        s_t = s.T
        v = act[rows, 0:HW].astype(F32)
        u = v * spread(sm[0, rows, :], e)
        scores = mm_nt(act[rows, HW + NS : CC], act[rows, HW : HW + NS])
        for j in range(HL // 2):
            parts = []
            for h in (2 * j, 2 * j + 1):
                gap = s[:, h : h + 1] - s_t[h : h + 1, :]
                parts.append((scores * jnp.exp(jnp.where(causal, gap, -1e30))).astype(BF))
            pair = u[:, 128 * j : 128 * j + 128]
            both = jnp.concatenate(
                [jnp.where(left, pair, 0.0), jnp.where(left, 0.0, pair)], axis=0
            ).astype(BF)
            yi[rows, 128 * j : 128 * j + 128] = mm(jnp.concatenate(parts, axis=1), both)
        yi[rows, :] += skip * v


def mix(idx, yi, act, sm, sc, p1, p2, p3, gate, gny, par, mixed, hin, sums, state):
    e = spread_matrix(BF)
    ones = jnp.ones((8, HW), BF)

    def rowsum(v):
        hi = v.astype(BF)
        lo = (v - hi.astype(F32)).astype(BF)
        return mm_nt(ones, hi) + mm_nt(ones, lo)

    state[...] = incoming(p1, p2, p3)

    @pl.loop(0, NC, unroll=True)
    def _(c):
        rows = pl.ds(pl.multiple_of(c * L, L), L)
        s = sm[1, rows, :]
        low = state[...].astype(BF)
        hin[c] = low
        y = yi[rows, :] + spread(jnp.exp(s), e) * mm(act[rows, HW + NS : CC], low)
        mixed[rows, :] = y
        z = gate[rows, :]
        g = y * (z * sigmoid(z))
        sq = rowsum(g * g)
        sg = rowsum(g * (gny[rows, :] * par[5:6, 0:HW]))
        sums[:, rows] = jnp.where(iota2((8, L), 0) == 0, sq, sg)
        last = spread(jnp.broadcast_to(s[L - 1 : L, :], (8, 128)), e)[0:1]
        state[...] = jnp.exp(last) * state[...] + sc[c]


def gated(
    idx, mixed, gate, gny, act, sm, s0, s1, s2, s3, par,
    ny, gmix, ggate, rp, small, state, total,
):
    e = spread_matrix(BF)
    gain = par[5:6, 0:HW]
    pick0 = (iota2((8, 128), 0) == 0).astype(F32)
    pick1 = (iota2((8, 128), 0) == 1).astype(F32)
    state[...] = jnp.zeros_like(state)
    total[...] = jnp.zeros_like(total)
    small[...] = jnp.zeros_like(small)

    @pl.loop(0, NC, unroll=True)
    def _(i):
        rows = pl.ds(pl.multiple_of((NC - 1 - i) * L, L), L)
        here = s0[:, rows] + s1[:, rows] + s2[:, rows] + s3[:, rows]
        sq = lax.dot_general(
            here, pick0, (((0,), (0,)), ((), ())), precision=HIGH, preferred_element_type=F32
        )
        sg = lax.dot_general(
            here, pick1, (((0,), (0,)), ((), ())), precision=HIGH, preferred_element_type=F32
        )
        r1 = lax.rsqrt(sq * (1.0 / DI) + EPS)
        pull = r1 * r1 * (sg * (1.0 / DI))
        r1 = jnp.concatenate([r1] * 6, axis=1)
        pull = jnp.concatenate([pull] * 6, axis=1)
        y = mixed[rows, :]
        z = gate[rows, :]
        sz = sigmoid(z)
        sil = z * sz
        g = y * sil
        gn = gny[rows, :]
        ghat = g * r1
        ny[rows, :] = (ghat * gain).astype(BF)
        gg = r1 * (gn * gain - g * pull)
        gm = gg * sil
        gmix[rows, :] = gm.astype(BF)
        ggate[rows, :] = (gg * y * (sz * (1.0 + z * (1.0 - sz)))).astype(BF)
        small[0:1, :] += jnp.sum(gn * ghat, axis=0, keepdims=True)
        small[1:2, :] += jnp.sum(gm * act[rows, 0:HW].astype(F32), axis=0, keepdims=True)
        s = sm[1, rows, :]
        part = mm_tn(act[rows, HW + NS : CC], (gm * spread(jnp.exp(s), e)).astype(BF))
        last_e = spread(jnp.broadcast_to(s[L - 1 : L, :], (8, 128)), e)
        state[...] = jnp.exp(last_e[0:1]) * state[...] + part
        total[...] += last_e

    pack_state(rp, state[...], total[...])


def within_back(idx, act, gmix, sm, gu, gbc, dsi, rw):
    left = iota2((L, 128), 1) < PW
    lane = iota2((L, 128), 1)
    causal = iota2((L, L), 1) >= iota2((L, L), 0)
    rw[...] = jnp.zeros_like(rw)

    @pl.loop(0, NC)
    def _(c):
        rows = pl.ds(pl.multiple_of(c * L, L), L)
        s = sm[1, rows, :]
        s_t = s.T
        dt = sm[0, rows, :]
        b = act[rows, HW : HW + NS]
        r = act[rows, HW + NS : CC]
        scores = mm_nt(b, r)
        grad_scores = jnp.zeros((L, L), F32)
        cols = jnp.zeros((L, 128), F32)
        for j in range(HL // 2):
            v = act[rows, 128 * j : 128 * j + 128].astype(F32)
            g = gmix[rows, 128 * j : 128 * j + 128]
            gf = g.astype(F32)
            parts = []
            for i in range(2):
                h = 2 * j + i
                gap = s_t[h : h + 1, :] - s[:, h : h + 1]
                q = jnp.exp(jnp.where(causal, gap, -1e30))
                own = jnp.where(left, v, 0.0) if i == 0 else jnp.where(left, 0.0, v)
                vg = mm_nt(own.astype(BF), g) * (q * dt[:, h : h + 1])
                grad_scores = grad_scores + vg
                w = scores * vg
                rw[h : h + 1, :] = jnp.sum(w, axis=0, keepdims=True)
                cols = jnp.where(lane == h, jnp.sum(w, axis=1, keepdims=True), cols)
                parts.append((scores * q).astype(BF))
            both = jnp.concatenate(
                [jnp.where(left, gf, 0.0), jnp.where(left, 0.0, gf)], axis=0
            ).astype(BF)
            gu[rows, 128 * j : 128 * j + 128] = mm(jnp.concatenate(parts, axis=1), both)
        dsi[rows, :] = rw[...].T - cols
        low = grad_scores.astype(BF)
        gbc[rows, 0:NS] = mm(low, r)
        gbc[rows, NS : 2 * NS] = mm_tn(low, b)


def across_back(
    idx, act, gmix, sm, gu, gbc, dsi, hin, p1, p2, p3, dsl, ci, par, hp, gains, turned,
    gpa, late, out, small, gps, cis, state, sums,
):
    e = spread_matrix(BF)
    skip = spread(jnp.broadcast_to(hp[2:3, :], (8, 128)), e)[0:1]
    rate = jnp.exp(hp[1:2, :])
    upper = (iota2((L, L), 1) >= iota2((L, L), 0)).astype(F32)
    below = (iota2((L, L), 0) > iota2((L, L), 1)).astype(F32)
    held = iota2((L, 128), 1) < HL
    gps[0:RIM, :] = jnp.zeros((RIM, CC), F32)
    gps[RIM + T : RIM + T + 16, :] = jnp.zeros((16, CC), F32)
    gpa[T:TR, CC:CA] = jnp.zeros((RIM, 128), BF)
    state[...] = incoming(p1, p2, p3)
    sums[...] = jnp.zeros_like(sums)

    @pl.loop(0, NC)
    def _(i):
        c = NC - 1 - i
        rows = pl.ds(pl.multiple_of(c * L, L), L)
        b = act[rows, HW : HW + NS]
        r = act[rows, HW + NS : CC]
        old = state[...]
        low = old.astype(BF)
        s = sm[1, rows, :]
        dt = sm[0, rows, :]
        last = s[L - 1 : L, :]
        tail_e = spread(jnp.exp(last - s), e)
        dt_e = spread(dt, e)
        grow_e = spread(jnp.exp(s), e)
        last_e = jnp.exp(spread(jnp.broadcast_to(last, (8, 128)), e)[0:1])
        v = act[rows, 0:HW].astype(F32)
        g = gmix[rows, :].astype(F32)
        carried = tail_e * mm(b, low)
        grad_u = gu[rows, :] + carried
        u = v * dt_e
        grad_v = dt_e * grad_u + skip * g
        grad_b = gbc[rows, 0:NS] + mm_nt((u * tail_e).astype(BF), low)
        gs = (g * grow_e).astype(BF)
        h = hin[c]
        grad_c = gbc[rows, NS : 2 * NS] + mm_nt(gs, h)
        inter = head_sums(g * (grow_e * mm(r, h)), e)
        kept = head_sums(u * carried, e)
        grad_step = head_sums(v * grad_u, e)
        cross = jnp.sum(h.astype(F32) * old, axis=0, keepdims=True) * last_e
        cross = head_sums(jnp.broadcast_to(cross, (8, HW)), e)[0:1]
        grad_a = mm_high(upper, dsi[rows, :] + inter) + mm_high(below, kept) + cross
        grad_raw = (grad_step - rate * grad_a) * sm[2, rows, :]
        sums[0:1, :] += jnp.sum(grad_raw, axis=0, keepdims=True)
        sums[1:2, :] += jnp.sum(grad_a * dt, axis=0, keepdims=True)
        gpa[rows, CC:CA] = jnp.where(held, grad_raw, 0.0).astype(BF)
        d = dsl[rows, :].astype(F32)
        to = pl.ds(pl.multiple_of(RIM + c * L, 16), L)
        gps[to, 0:HW] = grad_v * d[:, 0:HW]
        gps[to, HW : HW + NS] = grad_b * d[:, HW : HW + NS]
        gps[to, HW + NS : CC] = grad_c * d[:, HW + NS : CC]
        state[...] = last_e * old + mm_tn(r, gs)

    @pl.loop(0, 4)
    def _(j):
        lanes = pl.ds(pl.multiple_of(j * 256, 256), 256)
        cis[RIM:TR, :] = ci[0:T, lanes].astype(F32)
        cis[0:RIM, :] = ci[T:TR, lanes].astype(F32)
        gp = gps[RIM : RIM + T, lanes]
        small[4:5, lanes] = jnp.sum(gp, axis=0, keepdims=True)
        res = par[3:4, lanes] * gps[0:TR, lanes]
        for k in range(4):
            small[k : k + 1, lanes] = jnp.sum(
                gp * cis[13 + k : 13 + k + T, :], axis=0, keepdims=True
            )
            if k < 3:
                res = res + par[k : k + 1, lanes] * gps[3 - k : 3 - k + TR, lanes]
        low = res.astype(BF)
        gpa[0:T, lanes] = low[RIM:TR]
        gpa[T:TR, lanes] = low[0:RIM]

    for j in range(0, CA, 384):
        late[:, j : j + 384] = mm(turned[...], gpa[:, j : j + 384]).astype(BF)

    out[0:3, :] = jnp.zeros((3, 512), F32)
    for k in range(5):
        for j in range(2):
            out[3 + 2 * k + j : 4 + 2 * k + j, :] = small[k : k + 1, 512 * j : 512 * j + 512]
    out[13:14, :] = gains[0:1, 0:512]
    out[14:15, 0:256] = gains[0:1, 512:768]
    out[14:15, 256:384] = head_sums(jnp.broadcast_to(gains[1:2, :], (8, HW)), e)[0:1]
    out[14:15, 384:512] = sums[0:1, :]
    out[15:16, 0:128] = -rate * sums[1:2, :]
    out[15:16, 128:512] = jnp.zeros((1, 384), F32)


def normed_back(
    idx, gpa, ggate, wa, wg, nfull, gain, ny, wo, own, part, gn, late, small, acc, gsum
):
    @pl.loop(0, 6)
    def _(j):
        lanes = pl.ds(pl.multiple_of(j * 256, 256), 256)
        acc[:, lanes] = mm_nt(gpa[...], wa[lanes, :])
        acc[0:T, lanes] += mm_nt(ggate[...], wg[lanes, :])
        gsum[:, lanes] = jnp.broadcast_to(
            jnp.sum(acc[:, lanes] * nfull[:, lanes].astype(F32), axis=0, keepdims=True)
            / gain[:, lanes],
            (8, 256),
        )
        block = mm(ny[...], wo[:, lanes]).astype(BF)
        for k in range(NX):
            gn[k, 144:272, lanes] = block[128 * k : 128 * k + 128]

    for j in range(0, CA, 384):
        late[:, j : j + 384] = mm(own[...], gpa[:, j : j + 384]).astype(BF)
    for k in range(NX):
        rows = slice(128 * k, 128 * k + 128)
        gn[k, 0:128, :] = acc[rows, :].astype(BF)
        gn[k, 128:144, :] = acc[T:TR, :].astype(BF)
    small[...] = part[...]
    for j in range(3):
        small[j : j + 1, :] = gsum[0:1, 512 * j : 512 * j + 512]


def finish_out(idx, tokens, summed, out):
    out[...] = (tokens[...].astype(F32) + summed[144:272].astype(F32)).astype(BF)


def finish_back(idx, tokens, cot, summed, spill, gain, out, acc):
    v = tokens[...].astype(F32)
    root = lax.rsqrt(jnp.mean(v * v, axis=1, keepdims=True) + EPS)
    acc[...] = summed[0:128].astype(F32)
    acc[128 - RIM : 128, :] += spill[...].astype(F32)
    q = acc[...] * gain[...]
    pull = jnp.mean(q * v, axis=1, keepdims=True)
    out[...] = (cot[...].astype(F32) + root * (q - v * (root * root) * pull)).astype(BF)


def grad_early(idx, ny, cot, ggate, tm, tt, mine, other, nyt, rows, part):
    core, y = idx[2], idx[3]
    for j in range(HW // 128):
        lanes = slice(128 * j, 128 * j + 128)
        nyt[lanes, :] = ny[:, lanes].astype(F32).T.astype(BF)
    for half, which in enumerate((core, 1 - core)):
        for z in range(NZ):
            at = pl.multiple_of(192 * z + 96 * which, 16)
            row = 384 * half + 96 * z
            rows[row : row + 96, :] = nyt[pl.ds(at, 96), :]
    for q in range(4):
        k = lax.rem(q + 4 - y, 4)
        part[...] = mm(rows[...], cot[:, 384 * q : 384 * q + 384]).astype(BF)
        for half, (turned, out) in enumerate(((tm, mine), (tt, other))):
            gate = mm(turned[:, 0:T], ggate[:, 192 * q : 192 * q + 192]).astype(BF)
            out[k, :, 0:192] = gate
            for z in range(NZ):
                row = 384 * half + 96 * z
                out[k, 192 * z : 192 * z + 96, 192:384] = part[row : row + 96, 0:192]
                out[k, 192 * z + 96 : 192 * z + 192, 192:384] = part[row : row + 96, 192:384]


def add_early(idx, a, b, o0, o1, o2, o3):
    for k, out in enumerate((o0, o1, o2, o3)):
        out[...] = a[k] + b[k]


def sum_early(idx, a, b, c, d, out):
    out[...] = (
        a[...].astype(F32) + b[...].astype(F32) + (c[...].astype(F32) + d[...].astype(F32))
    ).astype(BF)


def split_z(idx, late, got, s0, s1, early, o0, o1, o3, oa, ob, o2):
    z = idx[1]
    small = wide(s0[...] + s1[...])
    for k, out in enumerate((o0, o1, o2, o3)):
        at = pl.multiple_of(lax.rem(z + k, NZ) * 192, 64)
        rows = pl.ds(at, 192)
        out[0:192, :] = late[rows, :] + got[rows, :]
        out[192:208, 0:CC] = small
        out[192:208, CC:CA] = jnp.zeros((16, CA - CC), BF)
        for j in range(3):
            rows = pl.ds(pl.multiple_of(at + 64 * j, 64), 64)
            out[208:272, 384 * j : 384 * j + 384] = early[rows, :]
    oa[...] = o2[0:HALF, :]
    ob[...] = o2[HALF:272, :]


def relay_z(idx, o1, o3, a, b, up, down):
    up[0:HALF, :] = o1[0:HALF, :] + a[...]
    up[HALF:272, :] = o1[HALF:272, :]
    down[0:HALF, :] = o3[0:HALF, :]
    down[HALF:272, :] = o3[HALF:272, :] + b[...]


def wide(v):
    hi = v.astype(BF).astype(F32)
    return jnp.concatenate([hi, v - hi], axis=1).astype(BF)


def halves(v):
    hi = v.astype(BF).astype(F32)
    return jnp.concatenate([hi, v - hi], axis=0).astype(BF)


def joined(v):
    v = v.astype(F32)
    return v[0:16] + v[16:32]


def split_y(idx, l0, l1, l2, o0, o1, o2, o3, early, scr, late):
    y = idx[3]
    total = l0[...].astype(F32) + l1[...].astype(F32) + l2[...].astype(F32)
    late[...] = total[0:192].astype(BF)
    for j in range(3):
        early[64 * j : 64 * j + 64, :] = total[208:272, 384 * j : 384 * j + 384].astype(BF)
    small = halves(total[192:208, 0:512] + total[192:208, 512:1024])
    for q in range(4):
        scr[q, :, 0:192] = late[:, 192 * q : 192 * q + 192]
        scr[q, :, 192:256] = late[:, HW + 64 * q : HW + 64 * q + 64]
        for j in range(4):
            scr[q, 32 * j : 32 * j + 32, 256:384] = small[:, 128 * j : 128 * j + 128]
        scr[q, 128:192, 256:384] = jnp.zeros((64, 128), BF)
        for j in range(4):
            scr[q, 128:176, 256 + 16 * j : 272 + 16 * j] = late[48 * j : 48 * j + 48, CC : CC + 16]
    for k, out in enumerate((o0, o1, o2, o3)):
        out[...] = scr[lax.rem(y + k, 4)]


def sum_y(idx, a, b, c, d, early, o0, o1, o2, o3, scr):
    x = idx[0]
    total = a[...].astype(F32) + b[...].astype(F32) + (c[...].astype(F32) + d[...].astype(F32))
    total = total.astype(BF)
    scr[:, 0:256] = total[:, 0:256]
    scr[:, 256:448] = early[:, 0:192]
    scr[:, 448:512] = jnp.zeros((192, 64), BF)
    for j in range(4):
        scr[48 * j : 48 * j + 48, 448:464] = total[128:176, 256 + 16 * j : 272 + 16 * j]
    small = jnp.concatenate(
        [
            sum(joined(ref[32 * j : 32 * j + 32, 256:384]) for ref in (a, b, c, d))
            for j in range(4)
        ],
        axis=1,
    )
    small = halves(small)
    for k, out in enumerate((o0, o1, o2, o3)):
        at = pl.multiple_of(lax.rem(x + k, NX) * 48, 16)
        out[0:48, :] = scr[pl.ds(at, 48), :]
        out[48:80, :] = small


def arrange_x(idx, a, b, c, d, early, out, gain, conv, ogain, heads, scr, steps):
    x = idx[0]
    shared = jnp.zeros((48, 64), F32)
    for k, ref in enumerate((a, b, c, d)):
        source = lax.rem(x + NX - k, NX)
        rows = pl.ds(pl.multiple_of(source * 48, 16), 48)
        out[rows, 0:192] = ref[0:48, 0:192]
        out[rows, 256:448] = ref[0:48, 256:448]
        shared = shared + ref[0:48, 192:256].astype(F32)
        scr[source] = joined(ref[48:80, :])
        steps[source] = ref[0:48, 448:464]
    out[:, 192:256] = jnp.zeros((192, 64), BF)
    out[0:48, 192:256] = shared.astype(BF)
    for xp in range(NX):
        out[48:96, 192 + 16 * xp : 208 + 16 * xp] = steps[xp]
    out[:, 448:640] = early[:, 192:384]
    both = scr[0] + scr[1] + (scr[2] + scr[3])
    for j in range(3):
        gain[0:1, 512 * j : 512 * j + 512] = both[j : j + 1, :]
    for k in range(5):
        conv[k : k + 1, DI : DI + 256] = both[4 + 2 * k : 5 + 2 * k, 256:512]
    heads[...] = jnp.zeros_like(heads)
    for xp in range(NX):
        own = scr[xp]
        for q in range(4):
            lane = 768 * q + 192 * xp
            for k in range(5):
                for at, size in pieces(192 * q, 192):
                    conv[k : k + 1, lane + at - 192 * q : lane + at - 192 * q + size] = own[
                        3 + 2 * k + at // 512 : 4 + 2 * k + at // 512, at % 512 : at % 512 + size
                    ]
            for at, size in pieces(192 * q, 192):
                ogain[0:1, lane + at - 192 * q : lane + at - 192 * q + size] = own[
                    13 + at // 512 : 14 + at // 512, at % 512 : at % 512 + size
                ]
            to = slice(12 * q + 3 * xp, 12 * q + 3 * xp + 3)
            heads[0:1, to] = own[14:15, 384 + 3 * q : 387 + 3 * q]
            heads[1:2, to] = own[15:16, 3 * q : 3 * q + 3]
            heads[2:3, to] = own[14:15, 256 + 3 * q : 259 + 3 * q]


def pieces(at, size):
    end = at + size
    while at < end:
        step = min(end, (at // 512 + 1) * 512) - at
        yield at, step
        at += step


def finish_weights(idx, a, b, c, d, e, f, g, h, gmain, gdt, gout, scr, steps):
    y, core = idx[3], idx[2]
    steps[...] = jnp.zeros_like(steps)
    for half in range(2):
        place = lax.rem(core + half, 2)
        for k, ref in enumerate((a, b, c, d) if half == 0 else (e, f, g, h)):
            scr[lax.rem(y + 4 - k, 4)] = ref[...]
        rows = pl.ds(pl.multiple_of(48 * place, 16), 48)
        long = pl.ds(pl.multiple_of(96 * place, 16), 96)
        for q in range(4):
            gout[long, 384 * q : 384 * q + 192] = scr[q, 0:96, 448:640].astype(F32)
            gout[long, 384 * q + 192 : 384 * q + 384] = scr[q, 96:192, 448:640].astype(F32)
            gmain[rows, 6144 + 64 * q : 6144 + 64 * q + 64] = scr[q, 0:48, 192:256].astype(F32)
            for xp in range(NX):
                lane = 768 * q + 192 * xp
                part = scr[q, 48 * xp : 48 * xp + 48, :].astype(F32)
                gmain[rows, lane : lane + 192] = part[:, 256:448]
                gmain[rows, DI + lane : DI + lane + 192] = part[:, 0:192]
        for xp in range(NX):
            part = scr[0, 48:96, 192 + 16 * xp : 208 + 16 * xp].astype(F32)
            for q in range(4):
                steps[rows, 12 * q + 3 * xp : 12 * q + 3 * xp + 3] = part[:, 3 * q : 3 * q + 3]
    gdt[...] = steps[...].T[0:48, 0:96]


def round_shift(v, axis, k, n=4):
    return lax.ppermute(v, axis, [(s, (s + k) % n) for s in range(n)])


def onward(v, k):
    return lax.ppermute(v, "z", [(s, s + k) for s in range(NZ) if 0 <= s + k < NZ])


def around(v, axis, n=4):
    return [v] + [round_shift(v, axis, k, n) for k in range(1, n)]


def spread_out(parts, axis, n=4):
    return [parts[0]] + [round_shift(parts[k], axis, k, n) for k in range(1, n)]


def after(value, *others):
    return lax.optimization_barrier((value,) + others)[0]


def after_all(values, *others):
    return list(lax.optimization_barrier(tuple(values) + others)[: len(values)])


def local(
    tokens, norm_gain, w_main, w_dt, conv_weight, conv_bias, dt_bias, a_log, skip_gain,
    out_gain, w_out, cotangent,
):
    x, z, core, y = (lax.axis_index(name) for name in ("x", "z", "core", "y"))
    idx = jnp.stack([x, z, core, y]).astype(jnp.int32)

    gain = norm_gain[None]
    rates = jnp.stack([dt_bias, a_log, skip_gain])

    call = Kernels(idx)
    both = jnp.concatenate([tokens, cotangent], axis=0)
    both = lax.all_gather(both, "x", axis=0, tiled=True)
    first = call(
        pack_main, [((48, CA + HW), BF)] * 4,
        [w_main, w_dt.T],
        [((NX, 48, CA + HW), BF), ((128, 128), F32)],
    )
    first = after_all(first)
    held = after(w_out, first[0])
    near = lax.ppermute(
        held,
        ("core", "z"),
        [(s, (s + 1) % 4) for s in range(4)] + [(4 + s, 4 + (s + 3) % 4) for s in range(4)],
    )
    first = spread_out(first, "x")
    far = lax.dynamic_slice(after(held, first[1]), (core * 96, 0), (96, D))
    far = round_shift(far, "z", 2)
    par, hp = call(
        params,
        [((8, CC), F32), ((8, 128), F32)],
        [conv_weight, conv_bias[None], out_gain[None], rates],
    )
    *first, near = after_all([*first, near])
    rows, part = call(
        stack, [((192, CA + HW), BF), ((48, CA + HW), BF)], first, light=True
    )
    part = round_shift(part, "z", 2)
    behind = after(rows, part)
    up, down = round_shift(behind, "z", 1), round_shift(behind, "z", 3)
    part = around(part, "y")
    normed, tail, cot = call(
        norm_rows,
        [((T, D), BF), ((RIM, D), BF), ((T, D), BF)],
        [after(both, near, far), gain],
    )
    rim = onward(tail, 1)
    part = after_all(part, tail)
    (beyond,) = call(stack_far, [((192, CA + HW), BF)], part, light=True)
    w_mine = [rows, up, beyond, down]
    w_other = [round_shift(v, "core", 1, 2) for v in w_mine]
    near, far = after_all([near, far], tail)
    near_t, far_t = (round_shift(v, "core", 1, 2) for v in (near, far))
    nfull, wa, ci, act, dsl, sm, sc, fp = call(
        project,
        [
            ((TR, D), BF), ((D, CA), BF), ((TR, CC), BF), ((T, CC), BF), ((T, CC), BF),
            ((3, T, 128), F32), ((NC, NS, HW), F32), ((NS + 16, HW), BF),
        ],
        [normed, rim, *w_mine, *w_other, par, hp],
        [((TR, 256), F32), ((NS, HW), F32), ((8, HW), F32)],
            )
    states = [onward(fp, k) for k in (1, 2, 3)]
    (yi,) = call(within, [((T, HW), F32)], [act, sm, hp])
    gate, gny, wg, wo = call(
        gates,
        [((T, HW), F32), ((T, HW), F32), ((D, HW), BF), ((HW, D), BF)],
        [nfull, *w_mine, *w_other, held, near, far, near_t, far_t, cot],
    )
    mixed, hin, sums = call(
        mix,
        [((T, HW), F32), ((NC, NS, HW), BF), ((8, T), F32)],
        [yi, act, sm, sc, *states, gate, gny, par],
        [((NS, HW), F32)],
    )
    nt_mine, nt_other = call(
        turn, [((HW, TR), BF), ((HW, TR), BF)], [nfull], [((D, T + 128), BF)]
    )
    ny, gmix, ggate, rp, small_g = call(
        gated,
        [((T, HW), BF)] * 3 + [((NS + 16, HW), BF), ((8, HW), F32)],
        [mixed, gate, gny, act, sm, *around(sums, "x"), par],
        [((NS, HW), F32), ((8, HW), F32)],
    )
    pulls = [onward(rp, -k) for k in (1, 2, 3)]
    early, got = call(
        grad_early,
        [((4, HW, 384), BF)] * 2,
        [ny, cot, ggate, nt_mine, nt_other],
        [((HW, T), BF), ((HW, T), BF), ((HW, 384), BF)],
    )
    got = round_shift(got, "core", 1, 2)
    gu, gbc, dsi = call(
        within_back,
        [((T, HW), F32), ((T, 2 * NS), F32), ((T, 128), F32)],
        [act, gmix, sm],
        [((128, 128), F32)],
    )
    got, *pulls = after_all([got, *pulls], gu)
    early = call(add_early, [((HW, 384), BF)] * 4, [after(early, *pulls), got])
    early = spread_out(early, "y")
    gpa, late, small = call(
        across_back,
        [((TR, CA), BF), ((HW, CA), BF), ((16, 512), F32)],
        [act, gmix, sm, gu, gbc, dsi, hin, *pulls, dsl, ci, par, hp, small_g, nt_other],
        [
            ((8, CC), F32), ((T + 32, CC), F32), ((TR, 256), F32), ((NS, HW), F32),
            ((8, 128), F32),
        ],
    )
    got = round_shift(late, "core", 1, 2)
    gn, late_own, small = call(
        normed_back,
        [((NX, 272, D), BF), ((HW, CA), BF), ((16, 512), F32)],
        [gpa, ggate, wa, wg, nfull, gain, ny, wo, nt_mine, small],
        [((TR, D), F32), ((8, D), F32)],
        light=True,
    )
    small_got = round_shift(small, "core", 1, 2)
    (early,) = call(sum_early, [((HW, 384), BF)], early)
    here, up, down, far_up, far_down = call(
        split_z,
        [((272, CA), BF)] * 3 + [((HALF, CA), BF), ((272 - HALF, CA), BF)],
        [late_own, got, small, small_got, early],
        [((272, CA), BF)],
        light=True,
    )
    far_up = round_shift(far_up, "z", 1)
    far_down = round_shift(far_down, "z", 3)
    up, down = call(relay_z, [((272, CA), BF)] * 2, [up, down, far_up, far_down], light=True)
    late = [here, round_shift(up, "z", 1), round_shift(down, "z", 3)]
    gn = lax.psum_scatter(gn, "x", scatter_dimension=0, tiled=True).reshape(272, D)
    *parts, early = call(
        split_y,
        [((192, 384), BF)] * 5,
        late,
        [((4, 192, 384), BF), ((192, CA), BF)],
        light=True,
    )
    parts = spread_out(parts, "y")
    parts = call(
        sum_y,
        [((80, 512), BF)] * 4,
        [*parts, early],
        [((192, 512), BF)],
        light=True,
    )
    parts = spread_out(parts, "x")
    *parts, gn = after_all([*parts, gn])
    final, g_gain, g_conv, g_ogain, g_heads = call(
        arrange_x,
        [((192, 640), BF), ((1, D), F32), ((8, DI + 256), F32), ((1, DI), F32), ((8, 128), F32)],
        [*parts, early],
        [((4, 16, 512), F32), ((4, 48, 16), BF)],
    )
    finals = around(final, "y")
    gn = after(gn, final)
    spill = lax.ppermute(
        gn[128:144], ("z", "x"), [(4 * s + 3, 4 * s - 1) for s in range(1, NZ)]
    )
    (block_out,) = call(finish_out, [((128, D), BF)], [tokens, gn])
    small = [
        g_gain[0], g_conv[:4], g_conv[4], g_heads[0, :48], g_heads[1, :48], g_heads[2, :48],
        g_ogain[0],
    ]
    spill, *small = after_all([spill, *small])
    (grad_tokens,) = call(
        finish_back,
        [((128, D), BF)],
        [tokens, cotangent, gn, spill, gain],
        [((128, D), F32)],
    )
    others = [round_shift(v, "core", 1, 2) for v in finals]
    g_main, g_dt, g_out = call(
        finish_weights,
        [((96, 6400), F32), ((48, 96), F32), ((192, D), F32)],
        [*finals, *others],
        [((4, 192, 640), BF), ((128, 128), F32)],
    )
    return (
        block_out, grad_tokens, small[0], g_main, g_dt.T, *small[1:], g_out,
    )


def solution(mesh):
    grid = Mesh(mesh.devices.reshape(4, 2, 4, 4), ("y", "core", "z", "x"))
    rows = P(("y", "core", "z", "x"), None)
    shard = P(("z", "x"), None)
    whole = P()
    return jax.shard_map(
        local,
        mesh=grid,
        in_specs=(
            rows, whole, shard, shard, whole, whole, whole, whole, whole, whole, shard, rows,
        ),
        out_specs=(
            rows, rows, whole, shard, shard, whole, whole, whole, whole, whole, whole, shard,
        ),
        check_vma=False,
    )
```
